512 devices in a mesh: cls: 64 (over x, z), ptl: 8 (over y, core).
Axes of the slice: x: 4, y: 4, z: 16, core: 2. Of those that a mesh axis runs over, the one named last changes fastest.
Arguments:
- images: float32 [128, 9216], P('ptl', 'cls'), may hold values from -13 to 13
- references: bfloat16 [256, 9216], P('cls'), may hold values from -6 to 6
- ctf_table: float32 [32, 32], replicated, may hold values from -1 to 1
- noise_inv: float32 [32, 32], replicated, may hold values from 0.003 to 0.30381945
- defocus_group: int32 [128], P('ptl'), may hold values from 0 to 31
- micrograph: int32 [128], P('ptl'), may hold values from 0 to 31, as said below
- batch_size: int32 [128], P('ptl'), may hold values from 0 to 16, as said below
Outputs:
- class_post: float32 [128, 256], P('ptl', 'cls')
- rot_post: float32 [128, 36], P('ptl')
The draws below stay inside these ranges and needn't reach their ends.
Inputs may be any that keep to these rules, and one draw needn't show every extreme that they name: The slots of index i of ptl name micrographs i * 4 to (i + 1) * 4 - 1, and the micrograph number never decreases from one slot to the next; live slots of one micrograph are consecutive. On each index of ptl the live slots (batch_size > 0) come first; a live slot holds the number of live slots of its micrograph. Some index of ptl has all 16 slots live; every index has at least one.
All inputs are finite; a program needn't handle non-finite values.
Results may differ from the reference program's by a relative error of at most 0.0003.
Values sent between devices are 32-bit elements; how exact they have to be, the bound alone decides.
A program may use at most 128 MiB of HBM per device.

```python
import math
import jax
import jax.numpy as jnp
from jax import lax

CYCLES = 32
ANG = 144
ROT = 36
SHIFTS = 128
BOX = 128
GROUPS = 32
MICS_DEV = 4
P_DEV = 16
CLASSES = 256
KR = 9216
PARTICLES = 128
MICS = 32


def slot_layout(key):
    devices = PARTICLES // P_DEV
    key_count, key_full, key_start = jax.random.split(key, 3)
    counts = jax.random.randint(key_count, (devices,), 1, P_DEV // 2 + 1)
    fullest = jax.random.randint(key_full, (), 0, devices)
    counts = jnp.where(jnp.arange(devices) == fullest, P_DEV, counts)
    slot = jnp.arange(P_DEV)[None, :]
    starts = (jax.random.randint(key_start, (devices, P_DEV), 0, 4) == 0).astype(jnp.int32)
    starts = jnp.where(slot == 0, 1, starts)
    segment = jnp.minimum(jnp.cumsum(starts, axis=1) - 1, MICS_DEV - 1)
    segment = jnp.where(slot == P_DEV - 1, MICS_DEV - 1, segment)
    segment = jnp.where((jnp.arange(devices) == fullest)[:, None], MICS_DEV - 1, segment)
    live = slot < counts[:, None]
    mic = jnp.arange(devices)[:, None] * MICS_DEV + segment
    same = (mic[:, :, None] == mic[:, None, :]) & live[:, None, :]
    sizes = jnp.where(live, jnp.sum(same.astype(jnp.int32), axis=2), 0)
    return (mic.reshape(-1).astype(jnp.int32), sizes.reshape(-1).astype(jnp.int32))


def scene(key, ctf_power):
    base = jax.random.fold_in(key, 101)
    streams = jax.random.split(base, 9)
    ref_shape = (CLASSES, 2, CYCLES, ANG)
    averages = jax.random.truncated_normal(streams[0], -6.0, 6.0, ref_shape)
    uneven = jax.random.uniform(streams[2], (GROUPS, CYCLES), minval=-1.0, maxval=1.0)
    ctf_values = jnp.sign(uneven) * jnp.abs(uneven) ** ctf_power
    slot_index = jnp.arange(PARTICLES)
    groups = jax.random.randint(streams[3], (PARTICLES,), 0, GROUPS)
    marked = jax.random.randint(streams[4], (), 0, PARTICLES)
    groups = jnp.where(slot_index == marked, GROUPS - 1, groups)
    groups = jnp.where(slot_index == (marked + PARTICLES // 2) % PARTICLES, 0, groups)
    chosen = jax.random.randint(streams[5], (PARTICLES,), 0, CLASSES)
    turns = jax.random.randint(streams[6], (PARTICLES,), 0, ROT)
    offsets = jax.random.randint(streams[7], (PARTICLES,), 0, SHIFTS)
    angle_index = jnp.arange(ANG)
    source = (angle_index[None, :] - turns[:, None] * (ANG // ROT)) % ANG
    picked = averages[chosen]
    turned = jnp.take_along_axis(picked, jnp.broadcast_to(source[:, None, None, :], (PARTICLES, 2, CYCLES, ANG)), axis=3)
    shift_x = (offsets % 16 - 8).astype(jnp.float32)
    shift_y = (offsets // 16 - SHIFTS // 32).astype(jnp.float32)
    radius = (jnp.arange(CYCLES, dtype=jnp.float32) + 1.0) / BOX
    theta = jnp.arange(ANG, dtype=jnp.float32) * (2.0 * math.pi / ANG)
    along = shift_x[:, None] * jnp.cos(theta)[None, :] + shift_y[:, None] * jnp.sin(theta)[None, :]
    phase = 2.0 * math.pi * radius[None, :, None] * along[:, None, :]
    ctf_slots = ctf_values[groups][:, :, None]
    real_part = ctf_slots * (turned[:, 0] * jnp.cos(phase) + turned[:, 1] * jnp.sin(phase))
    imag_part = ctf_slots * (turned[:, 1] * jnp.cos(phase) - turned[:, 0] * jnp.sin(phase))
    noise_shape = (PARTICLES, 2, CYCLES, ANG)
    noise = jax.random.truncated_normal(streams[8], -4.0, 4.0, noise_shape)
    signal = jnp.stack([real_part, imag_part], axis=1)
    pictures = (signal + noise).reshape(PARTICLES, KR)
    return (averages.reshape(CLASSES, KR), ctf_values, groups.astype(jnp.int32), pictures)


def draw_images(key, part):
    drawn = scene(key, 1.0)
    return drawn[3]


def draw_references(key, part):
    drawn = scene(key, 1.0)
    return drawn[0].astype(jnp.bfloat16)


def draw_ctf_table(key, part):
    drawn = scene(key, 1.0)
    return drawn[1]


def draw_defocus_group(key, part):
    drawn = scene(key, 1.0)
    return drawn[2]


def draw_micrograph(key, part):
    mic, sizes = slot_layout(key)
    return mic


def draw_batch_size(key, part):
    mic, sizes = slot_layout(key)
    return sizes


def setup_inputs(seed: int = 0) -> dict:
    splits = jax.random.split(jax.random.key(seed), 8)
    images = draw_images(jax.random.fold_in(splits[7], 71), 0)
    references = draw_references(jax.random.fold_in(splits[7], 71), 0)
    ctf_table = draw_ctf_table(jax.random.fold_in(splits[7], 71), 0)
    noise_inv = jnp.clip(jnp.exp(jax.random.uniform(splits[3], (MICS, CYCLES), jnp.float32, math.log(0.003), math.log(0.30381945))), 0.003, 0.30381945)
    defocus_group = draw_defocus_group(jax.random.fold_in(splits[7], 71), 0)
    micrograph = draw_micrograph(jax.random.fold_in(splits[7], 71), 0)
    batch_size = draw_batch_size(jax.random.fold_in(splits[7], 71), 0)
    return {"images": images, "references": references, "ctf_table": ctf_table, "noise_inv": noise_inv, "defocus_group": defocus_group, "micrograph": micrograph, "batch_size": batch_size}


def phase_table(cycles, angles, shifts, box):
    radius = (jnp.arange(cycles, dtype=jnp.float32) + 1.0) / box
    theta = jnp.arange(angles, dtype=jnp.float32) * (2.0 * math.pi / angles)
    index = jnp.arange(shifts, dtype=jnp.int32)
    shift_x = (index % 16 - 8).astype(jnp.float32)
    shift_y = (index // 16 - shifts // 32).astype(jnp.float32)
    along = jnp.cos(theta)[:, None] * shift_x[None, :] + jnp.sin(theta)[:, None] * shift_y[None, :]
    phase = (2.0 * math.pi) * radius[:, None, None] * along[None, :, :]
    table = jnp.concatenate([jnp.cos(phase), jnp.sin(phase)], axis=0)
    return table.reshape(2 * cycles * angles, shifts).astype(jnp.bfloat16)


def rotate_all(refs, turns, stride):
    return jnp.stack([jnp.roll(refs, stride * turn, axis=-1) for turn in range(turns)], axis=1)


def reference(images, references, ctf_table, noise_inv, defocus_group, micrograph, batch_size):
    ctf_rows = ctf_table[defocus_group]
    noise_rows = noise_inv[micrograph]
    counted = batch_size.astype(jnp.float32)
    shrink = counted / (counted + 1.0)
    weight = ctf_rows * noise_rows * shrink[:, None]
    refs = references.astype(jnp.float32).reshape(CLASSES, 2, CYCLES, ANG)
    power = jnp.sum(refs * refs, axis=(1, 3))
    quad = 0.5 * jnp.dot(ctf_rows * weight, power.T, precision=lax.Precision.HIGHEST)
    rotated = rotate_all(refs, ROT, ANG // ROT)
    table = phase_table(CYCLES, ANG, SHIFTS, BOX).astype(jnp.float32)
    parts = images.reshape(PARTICLES, 2, CYCLES, ANG)
    real_z = parts[:, 0] * weight[:, :, None]
    imag_z = -parts[:, 1] * weight[:, :, None]

    def one_particle(item):
        zre, zim, offset = item
        real_y = zre * rotated[:, :, 0] - zim * rotated[:, :, 1]
        imag_y = zre * rotated[:, :, 1] + zim * rotated[:, :, 0]
        product = jnp.stack([real_y, imag_y], axis=2).reshape(CLASSES * ROT, KR).astype(jnp.bfloat16)
        product = lax.optimization_barrier(product).astype(jnp.float32)
        corr = jnp.dot(product, table, precision=lax.Precision.HIGHEST)
        logits = corr.reshape(CLASSES, ROT, SHIFTS) - offset[:, None, None]
        return jax.nn.logsumexp(logits, axis=2)

    scores = lax.map(one_particle, (real_z, imag_z, quad))
    class_lse = jax.nn.logsumexp(scores, axis=2)
    peak = jnp.max(scores, axis=1)
    total = jnp.sum(jnp.exp(scores - peak[:, None, :]), axis=1)
    rot_lse = peak + jnp.log(total)
    norm = jax.nn.logsumexp(rot_lse, axis=1)
    live = (batch_size > 0)[:, None]
    class_post = jnp.where(live, class_lse - norm[:, None], 0.0)
    rot_post = jnp.where(live, rot_lse - norm[:, None], 0.0)
    return class_post, rot_post
```

```python
import math

import jax
import jax.numpy as jnp
import numpy as np
from jax import lax
from jax.experimental import pallas as pl
from jax.experimental.pallas import tpu as pltpu
from jax.sharding import PartitionSpec as P

CYCLES = 32
ANG = 144
ROT = 36
SHIFTS = 128
BOX = 128
STEP = ANG // ROT
NX, NZ = 4, 16
LOCAL = 4
MINE = 4
ALL_C = NX * LOCAL
ROWS = ROT * ALL_C
KT = 256
NB = 9
HALF = ROT // 2
CHUNKS = HALF // NB
HROWS = HALF * ALL_C
WIDE = (2 * HALF - NB) * ALL_C
NEAR = 4
MESH = pl.DeviceIdType.MESH
HIGH = lax.Precision.HIGHEST
NT = (((1,), (1,)), ((), ()))


def phase_tables():
    radius = (np.arange(CYCLES, dtype=np.float64) + 1.0) / BOX
    theta = np.arange(ANG, dtype=np.float64) * (2.0 * math.pi / ANG)
    index = np.arange(SHIFTS)
    shift_x = (index % 16 - 8).astype(np.float64)
    shift_y = (index // 16 - SHIFTS // 32).astype(np.float64)
    along = np.cos(theta)[:, None] * shift_x + np.sin(theta)[:, None] * shift_y
    phase = 2.0 * math.pi * radius[:, None, None] * along[None]

    def order(table):
        table = table.reshape(2, NZ, ROT, STEP, SHIFTS).transpose(2, 4, 1, 0, 3)
        return table.reshape(ROT, SHIFTS, 128)[:HALF].astype(jnp.bfloat16)

    return order(np.cos(phase)), order(np.sin(phase))


def iota(shape, axis):
    return lax.broadcasted_iota(jnp.int32, shape, axis)


def send(src, dst, send_sem, recv_sem, device):
    copy = pltpu.make_async_remote_copy(
        src_ref=src,
        dst_ref=dst,
        send_sem=send_sem,
        recv_sem=recv_sem,
        device_id={"cls": device},
        device_id_type=MESH,
    )
    copy.start()
    return copy


def spread_z(buffer, sends, recvs, x, z):
    copies = {}
    for reach in range(NEAR, 0, -1):
        for step in (reach, -reach):
            device = x * NZ + (z + step) % NZ
            slot = buffer.at[z]
            copies[step] = send(slot, slot, sends.at[step % NZ], recvs.at[step % NZ], device)
    return copies


def relay_z(buffer, sends, recvs, x, z, copies):
    for side, last in ((1, NEAR), (-1, NEAR - 1)):
        copies[side * NEAR].wait_recv()
        slot = buffer.at[(z - side * NEAR) % NZ]
        for reach in range(last, 0, -1):
            step = side * (NEAR + reach)
            device = x * NZ + (z + side * reach) % NZ
            copies[step] = send(slot, slot, sends.at[step % NZ], recvs.at[step % NZ], device)


def finish_z(copies):
    for step, copy in copies.items():
        if abs(step) != NEAR:
            copy.wait_recv()
    for copy in copies.values():
        copy.wait_send()


def kernel(
    cos_hbm, sin_hbm, images_hbm, references_hbm, ctf_hbm, noise_hbm, group_hbm, mic_hbm, count_hbm,
    class_post, rot_post,
    cos, sin, images, references, ctf, noise, group, mic, count,
    rows_c, rows_n, rows_s, padded, split_a, split_b, xs, xr, tail, rall, gathered, cross,
    turned, ends, wide, zt, mixed, shifted_a, shifted_b, acc_a, acc_b, score, half, flip, tiles, post, outs,
    local, xsend, xrecv, rsend, rrecv, zsend, zrecv, tsend, trecv, osend, orecv,
):
    me = lax.axis_index("cls")
    x, z = me // NZ, me % NZ
    along_x = [((x + step) % NX) * NZ + z for step in range(1, NX)]

    pairs = [
        (images_hbm, images), (ctf_hbm, ctf), (noise_hbm, noise), (group_hbm, group), (mic_hbm, mic),
        (count_hbm, count), (references_hbm, references), (cos_hbm, cos), (sin_hbm, sin),
    ]
    loads = [pltpu.make_async_copy(a, b, local.at[n]) for n, (a, b) in enumerate(pairs)]
    for load in loads:
        load.start()
    barrier = pltpu.get_barrier_semaphore()
    near = [x * NZ + (z + step) % NZ for step in range(-NEAR, NEAR + 1) if step]
    for device in along_x + near:
        pl.semaphore_signal(barrier, inc=1, device_id={"cls": device}, device_id_type=MESH)

    for load in loads[:6]:
        load.wait()
    for p in range(16):
        rows_c[p : p + 1, :] = ctf[pl.ds(group[p], 1), :]
        rows_n[p : p + 1, :] = noise[pl.ds(mic[p], 1), :]
        rows_s[p : p + 1, :] = jnp.full((1, CYCLES), count[p], jnp.int32).astype(jnp.float32)
    counted = rows_s[...]
    ctf_rows = rows_c[...]
    weight = ctf_rows * rows_n[...] * (counted / (counted + 1.0))
    cross[...] = 0.5 * ctf_rows * weight
    own = (x % 2) * NZ + z
    column = jnp.sum(jnp.where(iota((16, CYCLES), 1) == own, weight, 0.0), axis=1, keepdims=True)
    column = column * jnp.where(x >= 2, -1.0, 1.0)
    padded[...] = jnp.zeros_like(padded)
    padded[:, 0:ANG] = images[...] * column
    full = padded[...]
    row, lane = iota((16, 256), 0) & 3, iota((16, 256), 1) & 3
    rolled = {t: (pltpu.roll(full, t % 256, 1) if t else full) for t in range(-3, 4)}
    for d in range(STEP):
        value = jnp.zeros_like(full)
        for p in range(MINE):
            value = jnp.where((row == p) & (lane == p), rolled[p - d], value)
        for t in range(NX):
            line = jnp.sum(value[4 * t : 4 * t + 4], axis=0, keepdims=True)
            xs[t, d : d + 1, :] = line[:, 0:128]
            xs[t, 4 + d : 5 + d, :] = line[:, 128:256]

    pl.semaphore_wait(barrier, NX - 1 + 2 * NEAR)
    x_copies = []
    for n, device in enumerate(along_x):
        x_copies.append(send(xs.at[(x + n + 1) % NX], xr.at[x], xsend.at[n], xrecv.at[n], device))
    xr[x] = xs[x]

    loads[6].wait()
    for k in range(2 * CYCLES):
        base, off = (ANG * k) // 128 * 128, (ANG * k) % 128
        block = references[:, base : base + 256].astype(jnp.float32)
        if off:
            block = pltpu.roll(block, 256 - off, 1)
        split_a[pl.ds(k, LOCAL, stride=2 * CYCLES), :] = block[:, 0:128]
        split_b[pl.ds(k, LOCAL, stride=2 * CYCLES), :] = block[:, 128:256]
    rho = iota((KT, 1), 0)
    kappa = ((rho >> 7) << 5) + (((rho >> 2) & 1) << 4) + ((rho >> 3) & 15)
    repeat = (iota((KT, 2 * CYCLES), 1) == kappa).astype(jnp.float32).astype(jnp.bfloat16)
    angle = iota((1, 256), 1)
    keep = ((rho & 3) == (angle & 3)) & (angle < ANG)
    rho = iota((ROT * LOCAL, 1), 0)
    block_of = jnp.where(rho < LOCAL, 0, ROT - (rho >> 2))
    hit = (angle >> 2) == block_of
    total = jnp.zeros((ROT * LOCAL, KT), jnp.float32)
    for c in range(LOCAL):
        lines = slice(2 * CYCLES * c, 2 * CYCLES * (c + 1))
        one = jnp.concatenate([split_a[lines, :], split_b[lines, :]], axis=1).astype(jnp.bfloat16)
        spread = jnp.dot(repeat, one, preferred_element_type=jnp.float32)
        spread = jnp.where(keep, spread, 0.0).astype(jnp.bfloat16)
        pick = (hit & ((rho & 3) == c)).astype(jnp.float32).astype(jnp.bfloat16)
        total += lax.dot_general(pick, spread, NT, preferred_element_type=jnp.float32)
    rall[x] = total
    left, right = (x + NX - 1) % NX, (x + 1) % NX
    part_a, part_b = pl.ds(0, ROT * LOCAL // 2), pl.ds(ROT * LOCAL // 2, ROT * LOCAL // 2)
    from_left = send(rall.at[x], rall.at[x], rsend.at[0], rrecv.at[0], right * NZ + z)
    from_right = send(rall.at[x], rall.at[x], rsend.at[1], rrecv.at[1], left * NZ + z)

    for copy in x_copies:
        copy.wait()
    for part in range(2):
        for low in range(2):
            block = xr[2 * part + low]
            gathered[z, part, 4 * low : 4 * low + 4, :] = block[0:4]
            tail[part, 4 * low : 4 * low + 4, :] = block[4:8]
    gathered[z, 2] = tail[0] + pltpu.roll(tail[1], 16, 1)
    z_copies = spread_z(gathered, zsend, zrecv, x, z)
    relay_z(gathered, zsend, zrecv, x, z, z_copies)
    from_left.wait_recv()
    slot = rall.at[left, part_a]
    onward_a = send(slot, slot, rsend.at[2], rrecv.at[2], right * NZ + z)
    from_right.wait_recv()
    slot = rall.at[right, part_b]
    onward_b = send(slot, slot, rsend.at[3], rrecv.at[3], left * NZ + z)
    rho = iota((ROWS, 1), 0)
    kappa = ((rho >> 2) & 3) * (ROT * LOCAL) + (rho >> 4) * LOCAL + (rho & 3)
    place = (iota((ROWS, ROWS), 1) == kappa).astype(jnp.float32).astype(jnp.bfloat16)
    onward_a.wait_recv()
    onward_b.wait_recv()

    stacked = rall[...].reshape(ROWS, KT).astype(jnp.bfloat16)
    turned[...] = jnp.dot(place, stacked, preferred_element_type=jnp.float32)

    near_half, far_half = turned[0:HROWS, :], turned[HROWS:ROWS, :]
    plus = (near_half + far_half).astype(jnp.bfloat16)
    minus = (near_half - far_half).astype(jnp.bfloat16)
    ends[0, 0:HROWS, :] = plus
    ends[0, HROWS:ROWS, :] = plus
    ends[1, 0:HROWS, :] = -minus
    ends[1, HROWS:ROWS, :] = minus
    for sign in range(2):
        for q in range(NB):
            first = ALL_C * (NB - q)
            wide[sign, :, q * KT : (q + 1) * KT] = ends[sign, first : first + WIDE, :]

    power = jnp.zeros((ALL_C, KT), jnp.float32)
    for i in range(ROT):
        line = turned[16 * i : 16 * i + 16, :]
        power += line * line
    half[...] = jnp.zeros_like(half)
    half[0:MINE, :] = cross[pl.ds(x * MINE, MINE), :]
    lam = iota((1, KT), 1)
    spread = (iota((CYCLES, KT), 0) == (((lam >> 2) & 1) << 4) + ((lam >> 3) & 15)).astype(jnp.float32)
    half_wide = jnp.dot(half[...], spread, precision=HIGH, preferred_element_type=jnp.float32)
    quad = lax.dot_general(power, half_wide, NT, precision=HIGH, preferred_element_type=jnp.float32)
    loads[7].wait()
    loads[8].wait()

    finish_z(z_copies)
    for copy in (from_left, from_right, onward_a, onward_b):
        copy.wait_send()
    zt[0, 0:128] = gathered[:, 0].reshape(128, 128).T
    zt[1, 0:128] = gathered[:, 1].reshape(128, 128).T
    rest = gathered[:, 2].reshape(128, 128).T
    zt[0, 128:ANG] = rest[0:16]
    zt[1, 128:ANG] = rest[16:32]
    for part in range(2):
        one, two = zt[part, 0 : ANG // 2, :], zt[part, ANG // 2 : ANG, :]
        mixed[part, 0] = 0.5 * (one + two)
        mixed[part, 1] = 0.5 * (one - two)

    def build(chunk, pair, target):
        for q in range(NB):
            b = chunk * NB + q
            c, s = cos[b].astype(jnp.float32), sin[b].astype(jnp.float32)
            left, right = slice(q * KT, q * KT + 128), slice(q * KT + 128, q * KT + 256)
            for h in range(2):
                line = slice(4 * b + 2 * pair + h, 4 * b + 2 * pair + h + 1)
                rp, rm, ip, im = mixed[0, 0, line], mixed[0, 1, line], mixed[1, 0, line], mixed[1, 1, line]
                rows = slice(128 * h, 128 * h + 128)
                target[0, rows, left] = (c * rp + s * im).astype(jnp.bfloat16)
                target[0, rows, right] = (s * rm - c * ip).astype(jnp.bfloat16)
                target[1, rows, left] = (c * rm + s * ip).astype(jnp.bfloat16)
                target[1, rows, right] = (s * rp - c * im).astype(jnp.bfloat16)

    def multiply(chunk, source, acc):
        start = ALL_C * NB * (CHUNKS - 1 - chunk)
        for sign in range(2):
            left = wide[sign, start : start + HROWS, :]
            part = lax.dot_general(left, source[sign], NT, preferred_element_type=jnp.float32)
            if chunk:
                acc[sign] += part
            else:
                acc[sign] = part

    def reduce(pair, acc):
        size = 48
        lane = iota((size, 128), 1)
        for first in range(0, HROWS, size):
            tops = [jnp.zeros((size, 128), jnp.float32)] * 2
            totals = [jnp.ones((size, 128), jnp.float32)] * 2
            for h in range(2):
                even = acc[0, first : first + size, 128 * h : 128 * h + 128]
                odd = acc[1, first : first + size, 128 * h : 128 * h + 128]
                for half, value in enumerate((even + odd, even - odd)):
                    high = jnp.max(value, axis=1, keepdims=True)
                    low = jnp.sum(jnp.exp(value - high), axis=1, keepdims=True)
                    tops[half] = jnp.where(lane == 2 * pair + h, high, tops[half])
                    totals[half] = jnp.where(lane == 2 * pair + h, low, totals[half])
            for half in range(2):
                rows = slice(half * HROWS + first, half * HROWS + first + size)
                value = tops[half] + jnp.log(totals[half])
                score[rows, :] = value if pair == 0 else value + score[rows, :]

    build(0, 0, shifted_a)
    build(1, 0, shifted_b)
    multiply(0, shifted_a, acc_a)
    build(0, 1, shifted_a)
    multiply(1, shifted_b, acc_a)
    build(1, 1, shifted_b)
    multiply(0, shifted_a, acc_b)
    reduce(0, acc_a)
    multiply(1, shifted_b, acc_b)
    reduce(1, acc_b)

    values = score[...].reshape(ROT, ALL_C, 128) - quad[None]
    high = jnp.max(values, axis=0)
    by_class = high + jnp.log(jnp.sum(jnp.exp(values - high[None]), axis=0))
    high = jnp.max(values, axis=1)
    by_rot = high + jnp.log(jnp.sum(jnp.exp(values - high[:, None]), axis=1))
    flip[...] = jnp.zeros_like(flip)
    flip[0:ROT, :] = by_rot
    flip[64 : 64 + ALL_C, :] = by_class
    tile = flip[...].T[0:MINE, :]

    tiles[z] = tile
    t_copies = []
    for reach in range(NZ // 2, 0, -1):
        for step in (reach, -reach) if reach < NZ // 2 else (reach,):
            device = x * NZ + (z + step) % NZ
            n = step % NZ
            t_copies.append(send(tiles.at[z], tiles.at[z], tsend.at[n], trecv.at[n], device))
    for copy in t_copies:
        copy.wait()
    values = tiles[...]
    high = jnp.max(values, axis=0)
    rot_lse = high + jnp.log(jnp.sum(jnp.exp(values - high[None]), axis=0))
    lane = iota((MINE, 128), 1)
    masked = jnp.where(lane < ROT, rot_lse, -jnp.inf)
    high = jnp.max(masked, axis=1, keepdims=True)
    norm = high + jnp.log(jnp.sum(jnp.exp(masked - high), axis=1, keepdims=True))
    post[...] = jnp.where(lane < ROT, rot_lse, tile) - norm
    outs[x] = post[...]
    o_copies = []
    for n, device in enumerate(along_x):
        o_copies.append(send(post, outs.at[x], osend.at[n], orecv.at[n], device))
    for copy in o_copies:
        copy.wait()
    line = iota((MINE, 128), 0)
    for t in range(NX):
        live = jnp.zeros((MINE, 128), jnp.int32)
        for p in range(MINE):
            live = jnp.where(line == p, count[MINE * t + p], live)
        value = jnp.where(live > 0, outs[t], 0.0)
        rot_post[MINE * t : MINE * t + MINE, :] = value[:, 0:ROT]
        class_post[MINE * t : MINE * t + MINE, :] = pltpu.roll(value, 64 - LOCAL * x, 1)[:, 0:LOCAL]


def body(cos, sin, images, references, ctf_table, noise_inv, defocus_group, micrograph, batch_size):
    vmem, hbm = pl.BlockSpec(memory_space=pltpu.VMEM), pl.BlockSpec(memory_space=pltpu.HBM)
    f32, bf16, i32, dma = jnp.float32, jnp.bfloat16, jnp.int32, pltpu.SemaphoreType.DMA
    operands = (cos, sin, images, references, ctf_table, noise_inv, defocus_group, micrograph, batch_size)
    operands = [pltpu.with_memory_space_constraint(a, pltpu.HBM) for a in operands]
    class_post, rot_post = pl.pallas_call(
        kernel,
        out_shape=(
            jax.ShapeDtypeStruct((16, LOCAL), f32),
            jax.ShapeDtypeStruct((16, ROT), f32),
        ),
        in_specs=[hbm] * 9,
        out_specs=(vmem, vmem),
        scratch_shapes=[
            pltpu.VMEM(cos.shape, bf16),
            pltpu.VMEM(sin.shape, bf16),
            pltpu.VMEM(images.shape, f32),
            pltpu.VMEM(references.shape, bf16),
            pltpu.VMEM(ctf_table.shape, f32),
            pltpu.VMEM(noise_inv.shape, f32),
            pltpu.SMEM((16,), i32),
            pltpu.SMEM((16,), i32),
            pltpu.SMEM((16,), i32),
            pltpu.VMEM((16, CYCLES), f32),
            pltpu.VMEM((16, CYCLES), f32),
            pltpu.VMEM((16, CYCLES), f32),
            pltpu.VMEM((16, 256), f32),
            pltpu.VMEM((2 * CYCLES * LOCAL, 128), f32),
            pltpu.VMEM((2 * CYCLES * LOCAL, 128), f32),
            pltpu.VMEM((NX, 8, 128), f32),
            pltpu.VMEM((NX, 8, 128), f32),
            pltpu.VMEM((2, 8, 128), f32),
            pltpu.VMEM((NX, ROT * LOCAL, KT), f32),
            pltpu.VMEM((NZ, 3, 8, 128), f32),
            pltpu.VMEM((16, CYCLES), f32),
            pltpu.VMEM((ROWS, KT), f32),
            pltpu.VMEM((2, ROWS, KT), bf16),
            pltpu.VMEM((2, WIDE, NB * KT), bf16),
            pltpu.VMEM((2, ANG, 128), f32),
            pltpu.VMEM((2, 2, ANG // 2, 128), f32),
            pltpu.VMEM((2, 2 * SHIFTS, NB * KT), bf16),
            pltpu.VMEM((2, 2 * SHIFTS, NB * KT), bf16),
            pltpu.VMEM((2, HROWS, 2 * SHIFTS), f32),
            pltpu.VMEM((2, HROWS, 2 * SHIFTS), f32),
            pltpu.VMEM((ROWS, 128), f32),
            pltpu.VMEM((128, CYCLES), f32),
            pltpu.VMEM((128, 128), f32),
            pltpu.VMEM((NZ, MINE, 128), f32),
            pltpu.VMEM((MINE, 128), f32),
            pltpu.VMEM((NX, MINE, 128), f32),
            dma((9,)),
            dma((NX - 1,)),
            dma((NX - 1,)),
            dma((4,)),
            dma((4,)),
            dma((NZ,)),
            dma((NZ,)),
            dma((NZ,)),
            dma((NZ,)),
            dma((NX - 1,)),
            dma((NX - 1,)),
        ],
        compiler_params=pltpu.CompilerParams(collective_id=0, has_side_effects=True, vmem_limit_bytes=40 << 20),
        name="expectation",
    )(*operands)
    return class_post, rot_post


def solution(mesh):
    cos, sin = phase_tables()
    in_specs = (P("ptl", "cls"), P("cls", None), P(), P(), P("ptl"), P("ptl"), P("ptl"))
    out_specs = (P("ptl", "cls"), P("ptl", None))
    mapped = jax.shard_map(
        body, mesh=mesh, in_specs=(P(), P()) + in_specs, out_specs=out_specs, check_vma=False
    )

    def run(*args):
        return mapped(jnp.asarray(cos), jnp.asarray(sin), *args)

    return run
```

```python
import math

import jax
import jax.numpy as jnp
import numpy as np
from jax import lax
from jax.experimental import pallas as pl
from jax.experimental.pallas import tpu as pltpu
from jax.sharding import PartitionSpec as P

CYCLES = 32
ANG = 144
ROT = 36
SHIFTS = 128
BOX = 128
STEP = ANG // ROT
NX, NZ = 4, 16
LOCAL = 4
MINE = 4
ALL_C = NX * LOCAL
ROWS = ROT * ALL_C
KT = 256
NB = 9
HALF = ROT // 2
CHUNKS = HALF // NB
HROWS = HALF * ALL_C
WIDE = (2 * HALF - NB) * ALL_C
NEAR = 4
MESH = pl.DeviceIdType.MESH
HIGH = lax.Precision.HIGHEST
NT = (((1,), (1,)), ((), ()))


def phase_tables():
    radius = (np.arange(CYCLES, dtype=np.float64) + 1.0) / BOX
    theta = np.arange(ANG, dtype=np.float64) * (2.0 * math.pi / ANG)
    index = np.arange(SHIFTS)
    shift_x = (index % 16 - 8).astype(np.float64)
    shift_y = (index // 16 - SHIFTS // 32).astype(np.float64)
    along = np.cos(theta)[:, None] * shift_x + np.sin(theta)[:, None] * shift_y
    phase = 2.0 * math.pi * radius[:, None, None] * along[None]

    def order(table):
        table = table.reshape(2, NZ, ROT, STEP, SHIFTS).transpose(2, 4, 1, 0, 3)
        return table.reshape(ROT, SHIFTS, 128)[:HALF].astype(jnp.bfloat16)

    return order(np.cos(phase)), order(np.sin(phase))


def iota(shape, axis):
    return lax.broadcasted_iota(jnp.int32, shape, axis)


def send(src, dst, send_sem, recv_sem, device):
    copy = pltpu.make_async_remote_copy(
        src_ref=src,
        dst_ref=dst,
        send_sem=send_sem,
        recv_sem=recv_sem,
        device_id={"cls": device},
        device_id_type=MESH,
    )
    copy.start()
    return copy


def spread_z(buffer, sends, recvs, x, z):
    copies = {}
    for reach in range(NEAR, 0, -1):
        for step in (reach, -reach):
            device = x * NZ + ((z + step) & (NZ - 1))
            slot = buffer.at[z]
            copies[step] = send(slot, slot, sends.at[step % NZ], recvs.at[step % NZ], device)
    return copies


def relay_z(buffer, sends, recvs, x, z, copies):
    for side, last in ((1, NEAR), (-1, NEAR - 1)):
        copies[side * NEAR].wait_recv()
        slot = buffer.at[(z - side * NEAR) & (NZ - 1)]
        for reach in range(last, 0, -1):
            step = side * (NEAR + reach)
            device = x * NZ + ((z + side * reach) & (NZ - 1))
            copies[step] = send(slot, slot, sends.at[step % NZ], recvs.at[step % NZ], device)


def arrive_z(copies):
    for step, copy in copies.items():
        if abs(step) != NEAR:
            copy.wait_recv()


def kernel(
    cos_hbm, sin_hbm, images_hbm, references_hbm, ctf_hbm, noise_hbm, group_hbm, mic_hbm, count_hbm,
    class_post, rot_post,
    cos, sin, images, references, ctf, noise, group, mic, count,
    rows_c, rows_n, rows_s, padded, split_a, split_b, xs, xr, tail, rall, gathered, cross,
    turned, ends, wide, zt, mixed, shifted_a, shifted_b, acc_a, acc_b, score, half, flip, tiles, post, outs,
    local, xsend, xrecv, rsend, rrecv, zsend, zrecv, tsend, trecv, osend, orecv,
):
    me = lax.axis_index("cls")
    x, z = me >> 4, me & (NZ - 1)
    along_x = [((x + step) & (NX - 1)) * NZ + z for step in range(1, NX)]

    barrier = pltpu.get_barrier_semaphore()
    near = [x * NZ + ((z + step) & (NZ - 1)) for step in range(-NEAR, NEAR + 1) if step]
    for device in along_x + near:
        pl.semaphore_signal(barrier, inc=1, device_id={"cls": device}, device_id_type=MESH)
    pairs = [
        (images_hbm, images), (ctf_hbm, ctf), (noise_hbm, noise), (group_hbm, group), (mic_hbm, mic),
        (count_hbm, count), (references_hbm, references), (cos_hbm, cos), (sin_hbm, sin),
    ]
    loads = [pltpu.make_async_copy(a, b, local.at[n]) for n, (a, b) in enumerate(pairs)]
    for load in loads:
        load.start()

    for load in loads[:6]:
        load.wait()
    for p in range(16):
        rows_c[p : p + 1, :] = ctf[pl.ds(group[p], 1), :]
        rows_n[p : p + 1, :] = noise[pl.ds(mic[p], 1), :]
        rows_s[p : p + 1, :] = jnp.full((1, CYCLES), count[p], jnp.int32).astype(jnp.float32)
    counted = rows_s[...]
    ctf_rows = rows_c[...]
    weight = ctf_rows * rows_n[...] * (counted / (counted + 1.0))
    cross[...] = 0.5 * ctf_rows * weight
    own = (x & 1) * NZ + z
    column = jnp.sum(jnp.where(iota((16, CYCLES), 1) == own, weight, 0.0), axis=1, keepdims=True)
    column = column * jnp.where(x >= 2, -1.0, 1.0)
    padded[...] = jnp.zeros_like(padded)
    padded[:, 0:ANG] = images[...] * column
    full = padded[...]
    row, lane = iota((16, 256), 0) & 3, iota((16, 256), 1) & 3
    rolled = {t: (pltpu.roll(full, t % 256, 1) if t else full) for t in range(-3, 4)}
    for d in range(STEP):
        value = jnp.zeros_like(full)
        for p in range(MINE):
            value = jnp.where((row == p) & (lane == p), rolled[p - d], value)
        for t in range(NX):
            line = jnp.sum(value[4 * t : 4 * t + 4], axis=0, keepdims=True)
            xs[t, d : d + 1, :] = line[:, 0:128]
            xs[t, 4 + d : 5 + d, :] = line[:, 128:256]

    loads[6].wait()
    for k in range(2 * CYCLES):
        base, off = (ANG * k) // 128 * 128, (ANG * k) % 128
        block = references[:, base : base + 256].astype(jnp.float32)
        if off:
            block = pltpu.roll(block, 256 - off, 1)
        split_a[pl.ds(k, LOCAL, stride=2 * CYCLES), :] = block[:, 0:128]
        split_b[pl.ds(k, LOCAL, stride=2 * CYCLES), :] = block[:, 128:256]
    rho = iota((KT, 1), 0)
    kappa = ((rho >> 7) << 5) + (((rho >> 2) & 1) << 4) + ((rho >> 3) & 15)
    repeat = (iota((KT, 2 * CYCLES), 1) == kappa).astype(jnp.float32).astype(jnp.bfloat16)
    angle = iota((1, 256), 1)
    keep = ((rho & 3) == (angle & 3)) & (angle < ANG)
    rho = iota((ROT * LOCAL, 1), 0)
    block_of = jnp.where(rho < LOCAL, 0, ROT - (rho >> 2))
    hit = (angle >> 2) == block_of
    total = jnp.zeros((ROT * LOCAL, KT), jnp.float32)
    for c in range(LOCAL):
        lines = slice(2 * CYCLES * c, 2 * CYCLES * (c + 1))
        one = jnp.concatenate([split_a[lines, :], split_b[lines, :]], axis=1).astype(jnp.bfloat16)
        spread = jnp.dot(repeat, one, preferred_element_type=jnp.float32)
        spread = jnp.where(keep, spread, 0.0).astype(jnp.bfloat16)
        pick = (hit & ((rho & 3) == c)).astype(jnp.float32).astype(jnp.bfloat16)
        total += lax.dot_general(pick, spread, NT, preferred_element_type=jnp.float32)
    rall[x] = total

    pl.semaphore_wait(barrier, NX - 1 + 2 * NEAR)
    x_copies = []
    for n, device in enumerate(along_x):
        x_copies.append(send(xs.at[(x + n + 1) & (NX - 1)], xr.at[x], xsend.at[n], xrecv.at[n], device))
    xr[x] = xs[x]
    left, right = (x + NX - 1) & (NX - 1), (x + 1) & (NX - 1)
    part_a, part_b = pl.ds(0, ROT * LOCAL // 2), pl.ds(ROT * LOCAL // 2, ROT * LOCAL // 2)
    from_left = send(rall.at[x], rall.at[x], rsend.at[0], rrecv.at[0], right * NZ + z)
    from_right = send(rall.at[x], rall.at[x], rsend.at[1], rrecv.at[1], left * NZ + z)

    for copy in x_copies:
        copy.wait_recv()
    for part in range(2):
        for low in range(2):
            block = xr[2 * part + low]
            gathered[z, part, 4 * low : 4 * low + 4, :] = block[0:4]
            tail[part, 4 * low : 4 * low + 4, :] = block[4:8]
    gathered[z, 2] = tail[0] + pltpu.roll(tail[1], 16, 1)
    z_copies = spread_z(gathered, zsend, zrecv, x, z)
    relay_z(gathered, zsend, zrecv, x, z, z_copies)
    from_left.wait_recv()
    slot = rall.at[left, part_a]
    onward_a = send(slot, slot, rsend.at[2], rrecv.at[2], right * NZ + z)
    from_right.wait_recv()
    slot = rall.at[right, part_b]
    onward_b = send(slot, slot, rsend.at[3], rrecv.at[3], left * NZ + z)
    rho = iota((ROWS, 1), 0)
    kappa = ((rho >> 2) & 3) * (ROT * LOCAL) + (rho >> 4) * LOCAL + (rho & 3)
    place = (iota((ROWS, ROWS), 1) == kappa).astype(jnp.float32).astype(jnp.bfloat16)
    onward_a.wait_recv()
    onward_b.wait_recv()

    stacked = rall[...].reshape(ROWS, KT).astype(jnp.bfloat16)
    turned[...] = jnp.dot(place, stacked, preferred_element_type=jnp.float32)

    near_half, far_half = turned[0:HROWS, :], turned[HROWS:ROWS, :]
    plus = (near_half + far_half).astype(jnp.bfloat16)
    minus = (near_half - far_half).astype(jnp.bfloat16)
    ends[0, 0:HROWS, :] = plus
    ends[0, HROWS:ROWS, :] = plus
    ends[1, 0:HROWS, :] = -minus
    ends[1, HROWS:ROWS, :] = minus
    for sign in range(2):
        for q in range(NB):
            first = ALL_C * (NB - q)
            wide[sign, :, q * KT : (q + 1) * KT] = ends[sign, first : first + WIDE, :]

    power = jnp.zeros((ALL_C, KT), jnp.float32)
    for i in range(ROT):
        line = turned[16 * i : 16 * i + 16, :]
        power += line * line
    half[...] = jnp.zeros_like(half)
    half[0:MINE, :] = cross[pl.ds(x * MINE, MINE), :]
    lam = iota((1, KT), 1)
    spread = (iota((CYCLES, KT), 0) == (((lam >> 2) & 1) << 4) + ((lam >> 3) & 15)).astype(jnp.float32)
    half_wide = jnp.dot(half[...], spread, precision=HIGH, preferred_element_type=jnp.float32)
    quad = lax.dot_general(power, half_wide, NT, precision=HIGH, preferred_element_type=jnp.float32)
    loads[7].wait()
    loads[8].wait()

    arrive_z(z_copies)
    zt[0, 0:128] = gathered[:, 0].reshape(128, 128).T
    zt[1, 0:128] = gathered[:, 1].reshape(128, 128).T
    rest = gathered[:, 2].reshape(128, 128).T
    zt[0, 128:ANG] = rest[0:16]
    zt[1, 128:ANG] = rest[16:32]
    for part in range(2):
        one, two = zt[part, 0 : ANG // 2, :], zt[part, ANG // 2 : ANG, :]
        mixed[part, 0] = 0.5 * (one + two)
        mixed[part, 1] = 0.5 * (one - two)

    def build(chunk, pair, target):
        for q in range(NB):
            b = chunk * NB + q
            c, s = cos[b].astype(jnp.float32), sin[b].astype(jnp.float32)
            left, right = slice(q * KT, q * KT + 128), slice(q * KT + 128, q * KT + 256)
            for h in range(2):
                line = slice(4 * b + 2 * pair + h, 4 * b + 2 * pair + h + 1)
                rp, rm, ip, im = mixed[0, 0, line], mixed[0, 1, line], mixed[1, 0, line], mixed[1, 1, line]
                rows = slice(128 * h, 128 * h + 128)
                target[0, rows, left] = (c * rp + s * im).astype(jnp.bfloat16)
                target[0, rows, right] = (s * rm - c * ip).astype(jnp.bfloat16)
                target[1, rows, left] = (c * rm + s * ip).astype(jnp.bfloat16)
                target[1, rows, right] = (s * rp - c * im).astype(jnp.bfloat16)

    def multiply(chunk, source, acc):
        start = ALL_C * NB * (CHUNKS - 1 - chunk)
        for sign in range(2):
            left = wide[sign, start : start + HROWS, :]
            part = lax.dot_general(left, source[sign], NT, preferred_element_type=jnp.float32)
            if chunk:
                acc[sign] += part
            else:
                acc[sign] = part

    def reduce(pair, acc):
        size = 48
        lane = iota((size, 128), 1)
        for first in range(0, HROWS, size):
            tops = [jnp.zeros((size, 128), jnp.float32)] * 2
            totals = [jnp.ones((size, 128), jnp.float32)] * 2
            for h in range(2):
                even = acc[0, first : first + size, 128 * h : 128 * h + 128]
                odd = acc[1, first : first + size, 128 * h : 128 * h + 128]
                for half, value in enumerate((even + odd, even - odd)):
                    high = jnp.max(value, axis=1, keepdims=True)
                    low = jnp.sum(jnp.exp(value - high), axis=1, keepdims=True)
                    tops[half] = jnp.where(lane == 2 * pair + h, high, tops[half])
                    totals[half] = jnp.where(lane == 2 * pair + h, low, totals[half])
            for half in range(2):
                rows = slice(half * HROWS + first, half * HROWS + first + size)
                value = tops[half] + jnp.log(totals[half])
                score[rows, :] = value if pair == 0 else value + score[rows, :]

    build(0, 0, shifted_a)
    build(1, 0, shifted_b)
    multiply(0, shifted_a, acc_a)
    build(0, 1, shifted_a)
    multiply(1, shifted_b, acc_a)
    build(1, 1, shifted_b)
    multiply(0, shifted_a, acc_b)
    reduce(0, acc_a)
    multiply(1, shifted_b, acc_b)
    reduce(1, acc_b)

    values = score[...].reshape(ROT, ALL_C, 128) - quad[None]
    high = jnp.max(values, axis=0)
    by_class = high + jnp.log(jnp.sum(jnp.exp(values - high[None]), axis=0))
    high = jnp.max(values, axis=1)
    by_rot = high + jnp.log(jnp.sum(jnp.exp(values - high[:, None]), axis=1))
    flip[...] = jnp.zeros_like(flip)
    flip[0:ROT, :] = by_rot
    flip[64 : 64 + ALL_C, :] = by_class
    tile = flip[...].T[0:MINE, :]

    tiles[z] = tile
    t_copies = []
    for reach in range(NZ // 2, 0, -1):
        for step in (reach, -reach) if reach < NZ // 2 else (reach,):
            device = x * NZ + ((z + step) & (NZ - 1))
            n = step % NZ
            t_copies.append(send(tiles.at[z], tiles.at[z], tsend.at[n], trecv.at[n], device))
    for copy in t_copies:
        copy.wait_recv()
    values = tiles[...]
    high = jnp.max(values, axis=0)
    rot_lse = high + jnp.log(jnp.sum(jnp.exp(values - high[None]), axis=0))
    lane = iota((MINE, 128), 1)
    masked = jnp.where(lane < ROT, rot_lse, -jnp.inf)
    high = jnp.max(masked, axis=1, keepdims=True)
    norm = high + jnp.log(jnp.sum(jnp.exp(masked - high), axis=1, keepdims=True))
    post[...] = jnp.where(lane < ROT, rot_lse, tile) - norm
    outs[x] = post[...]
    o_copies = []
    for n, device in enumerate(along_x):
        o_copies.append(send(post, outs.at[x], osend.at[n], orecv.at[n], device))
    for copy in o_copies:
        copy.wait_recv()
    line = iota((MINE, 128), 0)
    for t in range(NX):
        live = jnp.zeros((MINE, 128), jnp.int32)
        for p in range(MINE):
            live = jnp.where(line == p, count[MINE * t + p], live)
        value = jnp.where(live > 0, outs[t], 0.0)
        rot_post[MINE * t : MINE * t + MINE, :] = value[:, 0:ROT]
        class_post[MINE * t : MINE * t + MINE, :] = pltpu.roll(value, 64 - LOCAL * x, 1)[:, 0:LOCAL]
    sent = x_copies + [from_left, from_right, onward_a, onward_b] + list(z_copies.values()) + t_copies + o_copies
    for copy in sent:
        copy.wait_send()


def body(cos, sin, images, references, ctf_table, noise_inv, defocus_group, micrograph, batch_size):
    vmem, hbm = pl.BlockSpec(memory_space=pltpu.VMEM), pl.BlockSpec(memory_space=pltpu.HBM)
    f32, bf16, i32, dma = jnp.float32, jnp.bfloat16, jnp.int32, pltpu.SemaphoreType.DMA
    operands = (cos, sin, images, references, ctf_table, noise_inv, defocus_group, micrograph, batch_size)
    operands = [pltpu.with_memory_space_constraint(a, pltpu.HBM) for a in operands]
    class_post, rot_post = pl.pallas_call(
        kernel,
        out_shape=(
            jax.ShapeDtypeStruct((16, LOCAL), f32),
            jax.ShapeDtypeStruct((16, ROT), f32),
        ),
        in_specs=[hbm] * 9,
        out_specs=(vmem, vmem),
        scratch_shapes=[
            pltpu.VMEM(cos.shape, bf16),
            pltpu.VMEM(sin.shape, bf16),
            pltpu.VMEM(images.shape, f32),
            pltpu.VMEM(references.shape, bf16),
            pltpu.VMEM(ctf_table.shape, f32),
            pltpu.VMEM(noise_inv.shape, f32),
            pltpu.SMEM((16,), i32),
            pltpu.SMEM((16,), i32),
            pltpu.SMEM((16,), i32),
            pltpu.VMEM((16, CYCLES), f32),
            pltpu.VMEM((16, CYCLES), f32),
            pltpu.VMEM((16, CYCLES), f32),
            pltpu.VMEM((16, 256), f32),
            pltpu.VMEM((2 * CYCLES * LOCAL, 128), f32),
            pltpu.VMEM((2 * CYCLES * LOCAL, 128), f32),
            pltpu.VMEM((NX, 8, 128), f32),
            pltpu.VMEM((NX, 8, 128), f32),
            pltpu.VMEM((2, 8, 128), f32),
            pltpu.VMEM((NX, ROT * LOCAL, KT), f32),
            pltpu.VMEM((NZ, 3, 8, 128), f32),
            pltpu.VMEM((16, CYCLES), f32),
            pltpu.VMEM((ROWS, KT), f32),
            pltpu.VMEM((2, ROWS, KT), bf16),
            pltpu.VMEM((2, WIDE, NB * KT), bf16),
            pltpu.VMEM((2, ANG, 128), f32),
            pltpu.VMEM((2, 2, ANG // 2, 128), f32),
            pltpu.VMEM((2, 2 * SHIFTS, NB * KT), bf16),
            pltpu.VMEM((2, 2 * SHIFTS, NB * KT), bf16),
            pltpu.VMEM((2, HROWS, 2 * SHIFTS), f32),
            pltpu.VMEM((2, HROWS, 2 * SHIFTS), f32),
            pltpu.VMEM((ROWS, 128), f32),
            pltpu.VMEM((128, CYCLES), f32),
            pltpu.VMEM((128, 128), f32),
            pltpu.VMEM((NZ, MINE, 128), f32),
            pltpu.VMEM((MINE, 128), f32),
            pltpu.VMEM((NX, MINE, 128), f32),
            dma((9,)),
            dma((NX - 1,)),
            dma((NX - 1,)),
            dma((4,)),
            dma((4,)),
            dma((NZ,)),
            dma((NZ,)),
            dma((NZ,)),
            dma((NZ,)),
            dma((NX - 1,)),
            dma((NX - 1,)),
        ],
        compiler_params=pltpu.CompilerParams(collective_id=0, has_side_effects=True, vmem_limit_bytes=40 << 20),
        name="expectation",
    )(*operands)
    return class_post, rot_post


def solution(mesh):
    cos, sin = phase_tables()
    in_specs = (P("ptl", "cls"), P("cls", None), P(), P(), P("ptl"), P("ptl"), P("ptl"))
    out_specs = (P("ptl", "cls"), P("ptl", None))
    mapped = jax.shard_map(
        body, mesh=mesh, in_specs=(P(), P()) + in_specs, out_specs=out_specs, check_vma=False
    )

    def run(*args):
        return mapped(jnp.asarray(cos), jnp.asarray(sin), *args)

    return run
```

```python
import math

import jax
import jax.numpy as jnp
import numpy as np
from jax import lax
from jax.experimental import pallas as pl
from jax.experimental.pallas import tpu as pltpu
from jax.sharding import PartitionSpec as P

CYCLES = 32
ANG = 144
ROT = 36
SHIFTS = 128
BOX = 128
STEP = ANG // ROT
NX, NZ = 4, 16
LOCAL = 4
MINE = 4
ALL_C = NX * LOCAL
ROWS = ROT * ALL_C
KT = 256
NB = 9
HALF = ROT // 2
HREF = ROT * LOCAL // 2
CHUNKS = HALF // NB
HROWS = HALF * ALL_C
WIDE = (2 * HALF - NB) * ALL_C
NEAR = 4
MESH = pl.DeviceIdType.MESH
HIGH = lax.Precision.HIGHEST
NT = (((1,), (1,)), ((), ()))


def phase_tables():
    radius = (np.arange(CYCLES, dtype=np.float64) + 1.0) / BOX
    theta = np.arange(ANG, dtype=np.float64) * (2.0 * math.pi / ANG)
    index = np.arange(SHIFTS)
    shift_x = (index % 16 - 8).astype(np.float64)
    shift_y = (index // 16 - SHIFTS // 32).astype(np.float64)
    along = np.cos(theta)[:, None] * shift_x + np.sin(theta)[:, None] * shift_y
    phase = 2.0 * math.pi * radius[:, None, None] * along[None]

    def order(table):
        table = table.reshape(2, NZ, ROT, STEP, SHIFTS).transpose(2, 4, 0, 1, 3)
        return table.reshape(ROT, SHIFTS, 128)[:HALF].astype(jnp.bfloat16)

    return order(np.cos(phase)), order(np.sin(phase))


def iota(shape, axis):
    return lax.broadcasted_iota(jnp.int32, shape, axis)


def send(src, dst, send_sem, recv_sem, device, **other):
    copy = pltpu.make_async_remote_copy(
        src_ref=src,
        dst_ref=dst,
        send_sem=send_sem,
        recv_sem=recv_sem,
        device_id={"cls": device, **other},
        device_id_type=MESH,
    )
    copy.start()
    return copy


def spread_z(buffer, sends, recvs, x, z):
    copies = {}
    for reach in range(NEAR, 0, -1):
        for step in (reach, -reach):
            device = x * NZ + ((z + step) & (NZ - 1))
            slot = buffer.at[z]
            copies[step] = send(slot, slot, sends.at[step % NZ], recvs.at[step % NZ], device)
    return copies


def relay_z(buffer, sends, recvs, x, z, copies):
    for side, last in ((1, NEAR), (-1, NEAR - 1)):
        copies[side * NEAR].wait_recv()
        slot = buffer.at[(z - side * NEAR) & (NZ - 1)]
        for reach in range(last, 0, -1):
            step = side * (NEAR + reach)
            device = x * NZ + ((z + side * reach) & (NZ - 1))
            copies[step] = send(slot, slot, sends.at[step % NZ], recvs.at[step % NZ], device)


def arrive_z(copies):
    for step, copy in copies.items():
        if abs(step) != NEAR:
            copy.wait_recv()


def kernel(
    cos_hbm, sin_hbm, images_hbm, references_hbm, ctf_hbm, noise_hbm, group_hbm, mic_hbm, count_hbm,
    class_post, rot_post,
    cos, sin, images, references, ctf, noise, group, mic, count,
    rows_c, rows_n, rows_s, padded, split_a, split_b, xs, xr, main, tail, rall, gathered, cross,
    turned, ends, wide, zt, mixed, shifted_a, shifted_b, acc_a, acc_b, score, half, flip, tiles, post, outs,
    local, xsend, xrecv, rsend, rrecv, zsend, zrecv, tsend, trecv, osend, orecv,
):
    me = lax.axis_index("cls")
    x, z = me >> 4, me & (NZ - 1)
    ptl = lax.axis_index("ptl")
    core = ptl & 1
    sibling = ptl + 1 - 2 * core
    along_x = [((x + step) & (NX - 1)) * NZ + z for step in range(1, NX)]

    barrier = pltpu.get_barrier_semaphore()
    near = [x * NZ + ((z + step) & (NZ - 1)) for step in range(-NEAR, NEAR + 1) if step]
    for device in along_x + near:
        pl.semaphore_signal(barrier, inc=1, device_id={"cls": device}, device_id_type=MESH)
    pl.semaphore_signal(barrier, inc=1, device_id={"ptl": sibling}, device_id_type=MESH)
    pairs = [
        (images_hbm, images), (ctf_hbm, ctf), (noise_hbm, noise), (group_hbm, group), (mic_hbm, mic),
        (count_hbm, count), (references_hbm, references), (cos_hbm, cos), (sin_hbm, sin),
    ]
    loads = [pltpu.make_async_copy(a, b, local.at[n]) for n, (a, b) in enumerate(pairs)]
    for load in loads:
        load.start()

    for load in loads[:6]:
        load.wait()
    for p in range(16):
        rows_c[p : p + 1, :] = ctf[pl.ds(group[p], 1), :]
        rows_n[p : p + 1, :] = noise[pl.ds(mic[p], 1), :]
        rows_s[p : p + 1, :] = jnp.full((1, CYCLES), count[p], jnp.int32).astype(jnp.float32)
    counted = rows_s[...]
    ctf_rows = rows_c[...]
    weight = ctf_rows * rows_n[...] * (counted / (counted + 1.0))
    cross[...] = 0.5 * ctf_rows * weight
    own = (x & 1) * NZ + z
    column = jnp.sum(jnp.where(iota((16, CYCLES), 1) == own, weight, 0.0), axis=1, keepdims=True)
    column = column * jnp.where(x >= 2, -1.0, 1.0)
    padded[...] = jnp.zeros_like(padded)
    tail[...] = jnp.zeros_like(tail)
    padded[:, 0:ANG] = images[...] * column
    full = padded[...]
    row, lane = iota((16, 256), 0) & 3, iota((16, 256), 1) & 3
    rolled = {t: (pltpu.roll(full, t % 256, 1) if t else full) for t in range(-3, 4)}
    for d in range(STEP):
        value = jnp.zeros_like(full)
        for p in range(MINE):
            value = jnp.where((row == p) & (lane == p), rolled[p - d], value)
        for t in range(NX):
            line = jnp.sum(value[4 * t : 4 * t + 4], axis=0, keepdims=True)
            xs[t, d : d + 1, :] = line[:, 0:128]
            xs[t, 4 + d : 5 + d, :] = line[:, 128:256]

    loads[6].wait()
    for k in range(2 * CYCLES):
        base, off = (ANG * k) // 128 * 128, (ANG * k) % 128
        block = references[:, base : base + 256].astype(jnp.float32)
        if off:
            block = pltpu.roll(block, 256 - off, 1)
        split_a[pl.ds(k, LOCAL, stride=2 * CYCLES), :] = block[:, 0:128]
        split_b[pl.ds(k, LOCAL, stride=2 * CYCLES), :] = block[:, 128:256]
    rho = iota((KT, 1), 0)
    repeat = (iota((KT, 2 * CYCLES), 1) == (rho >> 2)).astype(jnp.float32).astype(jnp.bfloat16)
    angle = iota((1, 256), 1)
    keep = ((rho & 3) == (angle & 3)) & (angle < ANG)
    rho = iota((ROT * LOCAL, 1), 0)
    block_of = jnp.where(rho < LOCAL, 0, ROT - (rho >> 2))
    hit = (angle >> 2) == block_of
    total = jnp.zeros((ROT * LOCAL, KT), jnp.float32)
    for c in range(LOCAL):
        lines = slice(2 * CYCLES * c, 2 * CYCLES * (c + 1))
        one = jnp.concatenate([split_a[lines, :], split_b[lines, :]], axis=1).astype(jnp.bfloat16)
        spread = jnp.dot(repeat, one, preferred_element_type=jnp.float32)
        spread = jnp.where(keep, spread, 0.0).astype(jnp.bfloat16)
        pick = (hit & ((rho & 3) == c)).astype(jnp.float32).astype(jnp.bfloat16)
        total += lax.dot_general(pick, spread, NT, preferred_element_type=jnp.float32)
    rall[x, 0] = total[0:HREF]
    rall[x, 1] = total[HREF:]

    pl.semaphore_wait(barrier, NX + 2 * NEAR)
    x_copies = []
    for n, device in enumerate(along_x):
        x_copies.append(send(xs.at[(x + n + 1) & (NX - 1)], xr.at[x], xsend.at[n], xrecv.at[n], device))
    xr[x] = xs[x]
    left, right = (x + NX - 1) & (NX - 1), (x + 1) & (NX - 1)
    opposite = (x + 2) & (NX - 1)
    part_a, part_b = pl.ds(0, 40), pl.ds(40, HREF - 40)
    slot = rall.at[x, core]
    from_left = send(slot, slot, rsend.at[0], rrecv.at[0], right * NZ + z)
    from_right = send(slot, slot, rsend.at[1], rrecv.at[1], left * NZ + z)

    for copy in x_copies:
        copy.wait_recv()
    last = jnp.zeros((STEP, 128), jnp.float32)
    for t in range(NX):
        block = xr[t]
        gathered[z, 2 * t] = block[0:2]
        gathered[z, 2 * t + 1] = block[2:4]
        rest = block[4:8]
        last = last + (pltpu.roll(rest, 16 * t, 1) if t else rest)
    moved = pltpu.roll(last, 64, 1)
    gathered[z, 8, 0:1, :] = last[0:1] + moved[1:2]
    gathered[z, 8, 1:2, :] = last[2:3] + moved[3:4]
    z_copies = spread_z(gathered, zsend, zrecv, x, z)

    from_left.wait_recv()
    slot = rall.at[left, core]
    part = rall.at[left, core, part_a]
    onward_a = send(part, part, rsend.at[2], rrecv.at[2], right * NZ + z)
    over_left = send(slot, slot, rsend.at[4], rrecv.at[4], me, ptl=sibling)
    from_right.wait_recv()
    slot = rall.at[right, core]
    part = rall.at[right, core, part_b]
    onward_b = send(part, part, rsend.at[3], rrecv.at[3], left * NZ + z)
    over_right = send(slot, slot, rsend.at[5], rrecv.at[5], me, ptl=sibling)
    relay_z(gathered, zsend, zrecv, x, z, z_copies)
    rho = iota((ROWS, 1), 0)
    kappa = ((rho >> 2) & 3) * (ROT * LOCAL) + (rho >> 4) * LOCAL + (rho & 3)
    place = (iota((ROWS, ROWS), 1) == kappa).astype(jnp.float32).astype(jnp.bfloat16)
    onward_a.wait_recv()
    onward_b.wait_recv()
    slot = rall.at[opposite, core]
    over_opposite = send(slot, slot, rsend.at[6], rrecv.at[6], me, ptl=sibling)
    for copy in (over_left, over_right, over_opposite):
        copy.wait_recv()

    stacked = rall[...].reshape(ROWS, KT).astype(jnp.bfloat16)
    turned[...] = jnp.dot(place, stacked, preferred_element_type=jnp.float32)

    near_half, far_half = turned[0:HROWS, :], turned[HROWS:ROWS, :]
    plus = (near_half + far_half).astype(jnp.bfloat16)
    minus = (near_half - far_half).astype(jnp.bfloat16)
    ends[0, 0:HROWS, :] = plus
    ends[0, HROWS:ROWS, :] = plus
    ends[1, 0:HROWS, :] = -minus
    ends[1, HROWS:ROWS, :] = minus
    for sign in range(2):
        for q in range(NB):
            first = ALL_C * (NB - q)
            wide[sign, :, q * KT : (q + 1) * KT] = ends[sign, first : first + WIDE, :]

    power = jnp.zeros((ALL_C, KT), jnp.float32)
    for i in range(ROT):
        line = turned[16 * i : 16 * i + 16, :]
        power += line * line
    half[...] = jnp.zeros_like(half)
    half[0:MINE, :] = cross[pl.ds(x * MINE, MINE), :]
    lam = iota((1, KT), 1)
    spread = (iota((CYCLES, KT), 0) == ((lam >> 2) & 31)).astype(jnp.float32)
    half_wide = jnp.dot(half[...], spread, precision=HIGH, preferred_element_type=jnp.float32)
    quad = lax.dot_general(power, half_wide, NT, precision=HIGH, preferred_element_type=jnp.float32)
    loads[7].wait()
    loads[8].wait()

    arrive_z(z_copies)
    for origin in range(NZ):
        for t in range(NX):
            row = 64 * (t % 2) + 4 * origin
            main[t // 2, row : row + 2, :] = gathered[origin, 2 * t]
            main[t // 2, row + 2 : row + 4, :] = gathered[origin, 2 * t + 1]
        last = gathered[origin, 8]
        moved = pltpu.roll(last, 64, 1)
        row = 4 * origin
        tail[row : row + 1, :] = last[0:1]
        tail[row + 1 : row + 2, :] = moved[0:1]
        tail[row + 2 : row + 3, :] = last[1:2]
        tail[row + 3 : row + 4, :] = moved[1:2]
    rest = tail[...].T
    lane = iota((16, 128), 1)
    for part in range(2):
        zt[part, 0:128] = main[part].T
        low, high = rest[32 * part : 32 * part + 16], rest[32 * part + 16 : 32 * part + 32]
        zt[part, 128:ANG] = jnp.where(lane < 64, low, pltpu.roll(high, 64, 1))
    for part in range(2):
        one, two = zt[part, 0 : ANG // 2, :], zt[part, ANG // 2 : ANG, :]
        mixed[part, 0] = 0.5 * (one + two)
        mixed[part, 1] = 0.5 * (one - two)

    def build(chunk, pair, target):
        for q in range(NB):
            b = chunk * NB + q
            c, s = cos[b].astype(jnp.float32), sin[b].astype(jnp.float32)
            left, right = slice(q * KT, q * KT + 128), slice(q * KT + 128, q * KT + 256)
            for h in range(2):
                line = slice(4 * b + 2 * pair + h, 4 * b + 2 * pair + h + 1)
                rp, rm, ip, im = mixed[0, 0, line], mixed[0, 1, line], mixed[1, 0, line], mixed[1, 1, line]
                rows = slice(128 * h, 128 * h + 128)
                target[0, rows, left] = (c * rp + s * im).astype(jnp.bfloat16)
                target[0, rows, right] = (s * rm - c * ip).astype(jnp.bfloat16)
                target[1, rows, left] = (c * rm + s * ip).astype(jnp.bfloat16)
                target[1, rows, right] = (s * rp - c * im).astype(jnp.bfloat16)

    def multiply(chunk, source, acc):
        start = ALL_C * NB * (CHUNKS - 1 - chunk)
        for sign in range(2):
            left = wide[sign, start : start + HROWS, :]
            part = lax.dot_general(left, source[sign], NT, preferred_element_type=jnp.float32)
            if chunk:
                acc[sign] += part
            else:
                acc[sign] = part

    def reduce(pair, acc):
        size = 48
        lane = iota((size, 128), 1)
        for first in range(0, HROWS, size):
            tops = [jnp.zeros((size, 128), jnp.float32)] * 2
            totals = [jnp.ones((size, 128), jnp.float32)] * 2
            for h in range(2):
                even = acc[0, first : first + size, 128 * h : 128 * h + 128]
                odd = acc[1, first : first + size, 128 * h : 128 * h + 128]
                for half, value in enumerate((even + odd, even - odd)):
                    high = jnp.max(value, axis=1, keepdims=True)
                    low = jnp.sum(jnp.exp(value - high), axis=1, keepdims=True)
                    tops[half] = jnp.where(lane == 2 * pair + h, high, tops[half])
                    totals[half] = jnp.where(lane == 2 * pair + h, low, totals[half])
            for half in range(2):
                rows = slice(half * HROWS + first, half * HROWS + first + size)
                value = tops[half] + jnp.log(totals[half])
                score[rows, :] = value if pair == 0 else value + score[rows, :]

    build(0, 0, shifted_a)
    build(1, 0, shifted_b)
    multiply(0, shifted_a, acc_a)
    build(0, 1, shifted_a)
    multiply(1, shifted_b, acc_a)
    build(1, 1, shifted_b)
    multiply(0, shifted_a, acc_b)
    reduce(0, acc_a)
    multiply(1, shifted_b, acc_b)
    reduce(1, acc_b)

    values = score[...].reshape(ROT, ALL_C, 128) - quad[None]
    high = jnp.max(values, axis=0)
    by_class = high + jnp.log(jnp.sum(jnp.exp(values - high[None]), axis=0))
    high = jnp.max(values, axis=1)
    by_rot = high + jnp.log(jnp.sum(jnp.exp(values - high[:, None]), axis=1))
    flip[...] = jnp.zeros_like(flip)
    flip[0:ROT, :] = by_rot
    flip[64 : 64 + ALL_C, :] = by_class
    tile = flip[...].T[0:MINE, :]

    tiles[z] = tile
    t_copies = []
    for reach in range(NZ // 2, 0, -1):
        for step in (reach, -reach) if reach < NZ // 2 else (reach,):
            device = x * NZ + ((z + step) & (NZ - 1))
            n = step % NZ
            t_copies.append(send(tiles.at[z], tiles.at[z], tsend.at[n], trecv.at[n], device))
    for copy in t_copies:
        copy.wait_recv()
    values = tiles[...]
    high = jnp.max(values, axis=0)
    rot_lse = high + jnp.log(jnp.sum(jnp.exp(values - high[None]), axis=0))
    lane = iota((MINE, 128), 1)
    masked = jnp.where(lane < ROT, rot_lse, -jnp.inf)
    high = jnp.max(masked, axis=1, keepdims=True)
    norm = high + jnp.log(jnp.sum(jnp.exp(masked - high), axis=1, keepdims=True))
    post[...] = jnp.where(lane < ROT, rot_lse, tile) - norm
    outs[x] = post[...]
    o_copies = []
    for n, device in enumerate(along_x):
        o_copies.append(send(post, outs.at[x], osend.at[n], orecv.at[n], device))
    for copy in o_copies:
        copy.wait_recv()
    line = iota((MINE, 128), 0)
    for t in range(NX):
        live = jnp.zeros((MINE, 128), jnp.int32)
        for p in range(MINE):
            live = jnp.where(line == p, count[MINE * t + p], live)
        value = jnp.where(live > 0, outs[t], 0.0)
        rot_post[MINE * t : MINE * t + MINE, :] = value[:, 0:ROT]
        class_post[MINE * t : MINE * t + MINE, :] = pltpu.roll(value, 64 - LOCAL * x, 1)[:, 0:LOCAL]
    sent = x_copies + [from_left, from_right, onward_a, onward_b, over_left, over_right, over_opposite] + list(z_copies.values()) + t_copies + o_copies
    for copy in sent:
        copy.wait_send()


def body(cos, sin, images, references, ctf_table, noise_inv, defocus_group, micrograph, batch_size):
    vmem, hbm = pl.BlockSpec(memory_space=pltpu.VMEM), pl.BlockSpec(memory_space=pltpu.HBM)
    f32, bf16, i32, dma = jnp.float32, jnp.bfloat16, jnp.int32, pltpu.SemaphoreType.DMA
    operands = (cos, sin, images, references, ctf_table, noise_inv, defocus_group, micrograph, batch_size)
    operands = [pltpu.with_memory_space_constraint(a, pltpu.HBM) for a in operands]
    class_post, rot_post = pl.pallas_call(
        kernel,
        out_shape=(
            jax.ShapeDtypeStruct((16, LOCAL), f32),
            jax.ShapeDtypeStruct((16, ROT), f32),
        ),
        in_specs=[hbm] * 9,
        out_specs=(vmem, vmem),
        scratch_shapes=[
            pltpu.VMEM(cos.shape, bf16),
            pltpu.VMEM(sin.shape, bf16),
            pltpu.VMEM(images.shape, f32),
            pltpu.VMEM(references.shape, bf16),
            pltpu.VMEM(ctf_table.shape, f32),
            pltpu.VMEM(noise_inv.shape, f32),
            pltpu.SMEM((16,), i32),
            pltpu.SMEM((16,), i32),
            pltpu.SMEM((16,), i32),
            pltpu.VMEM((16, CYCLES), f32),
            pltpu.VMEM((16, CYCLES), f32),
            pltpu.VMEM((16, CYCLES), f32),
            pltpu.VMEM((16, 256), f32),
            pltpu.VMEM((2 * CYCLES * LOCAL, 128), f32),
            pltpu.VMEM((2 * CYCLES * LOCAL, 128), f32),
            pltpu.VMEM((NX, 8, 128), f32),
            pltpu.VMEM((NX, 8, 128), f32),
            pltpu.VMEM((2, 128, 128), f32),
            pltpu.VMEM((128, 128), f32),
            pltpu.VMEM((NX, 2, HREF, KT), f32),
            pltpu.VMEM((NZ, 9, 2, 128), f32),
            pltpu.VMEM((16, CYCLES), f32),
            pltpu.VMEM((ROWS, KT), f32),
            pltpu.VMEM((2, ROWS, KT), bf16),
            pltpu.VMEM((2, WIDE, NB * KT), bf16),
            pltpu.VMEM((2, ANG, 128), f32),
            pltpu.VMEM((2, 2, ANG // 2, 128), f32),
            pltpu.VMEM((2, 2 * SHIFTS, NB * KT), bf16),
            pltpu.VMEM((2, 2 * SHIFTS, NB * KT), bf16),
            pltpu.VMEM((2, HROWS, 2 * SHIFTS), f32),
            pltpu.VMEM((2, HROWS, 2 * SHIFTS), f32),
            pltpu.VMEM((ROWS, 128), f32),
            pltpu.VMEM((128, CYCLES), f32),
            pltpu.VMEM((128, 128), f32),
            pltpu.VMEM((NZ, MINE, 128), f32),
            pltpu.VMEM((MINE, 128), f32),
            pltpu.VMEM((NX, MINE, 128), f32),
            dma((9,)),
            dma((NX - 1,)),
            dma((NX - 1,)),
            dma((7,)),
            dma((7,)),
            dma((NZ,)),
            dma((NZ,)),
            dma((NZ,)),
            dma((NZ,)),
            dma((NX - 1,)),
            dma((NX - 1,)),
        ],
        compiler_params=pltpu.CompilerParams(collective_id=0, has_side_effects=True, vmem_limit_bytes=40 << 20),
        name="expectation",
    )(*operands)
    return class_post, rot_post


def solution(mesh):
    cos, sin = phase_tables()
    in_specs = (P("ptl", "cls"), P("cls", None), P(), P(), P("ptl"), P("ptl"), P("ptl"))
    out_specs = (P("ptl", "cls"), P("ptl", None))
    mapped = jax.shard_map(
        body, mesh=mesh, in_specs=(P(), P()) + in_specs, out_specs=out_specs, check_vma=False
    )

    def run(*args):
        return mapped(jnp.asarray(cos), jnp.asarray(sin), *args)

    return run
```

```python
import math

import jax
import jax.numpy as jnp
import numpy as np
from jax import lax
from jax.experimental import pallas as pl
from jax.experimental.pallas import tpu as pltpu
from jax.sharding import PartitionSpec as P

CYCLES = 32
ANG = 144
ROT = 36
SHIFTS = 128
BOX = 128
STEP = ANG // ROT
NX, NZ = 4, 16
LOCAL = 4
MINE = 4
ALL_C = NX * LOCAL
ROWS = ROT * ALL_C
KT = 256
NB = 9
HALF = ROT // 2
HREF = ROT * LOCAL // 2
CHUNKS = HALF // NB
HROWS = HALF * ALL_C
WIDE = (2 * HALF - NB) * ALL_C
NEAR = 4
MESH = pl.DeviceIdType.MESH
HIGH = lax.Precision.HIGHEST
NT = (((1,), (1,)), ((), ()))


def phase_tables():
    radius = (np.arange(CYCLES, dtype=np.float64) + 1.0) / BOX
    theta = np.arange(ANG, dtype=np.float64) * (2.0 * math.pi / ANG)
    index = np.arange(SHIFTS)
    shift_x = (index % 16 - 8).astype(np.float64)
    shift_y = (index // 16 - SHIFTS // 32).astype(np.float64)
    along = np.cos(theta)[:, None] * shift_x + np.sin(theta)[:, None] * shift_y
    phase = 2.0 * math.pi * radius[:, None, None] * along[None]

    def order(table):
        table = table.reshape(2, NZ, ROT, STEP, SHIFTS).transpose(2, 4, 0, 1, 3)
        return table.reshape(ROT, SHIFTS, 128)[:HALF].astype(jnp.bfloat16)

    return order(np.cos(phase)), order(np.sin(phase))


def iota(shape, axis):
    return lax.broadcasted_iota(jnp.int32, shape, axis)


def send(src, dst, send_sem, recv_sem, device, **other):
    copy = pltpu.make_async_remote_copy(
        src_ref=src,
        dst_ref=dst,
        send_sem=send_sem,
        recv_sem=recv_sem,
        device_id={"cls": device, **other},
        device_id_type=MESH,
    )
    copy.start()
    return copy


def spread_z(buffer, sends, recvs, x, z):
    copies = {}
    for reach in range(NEAR, 0, -1):
        for step in (reach, -reach):
            device = x * NZ + ((z + step) & (NZ - 1))
            slot = buffer.at[z]
            copies[step] = send(slot, slot, sends.at[step % NZ], recvs.at[step % NZ], device)
    return copies


def relay_z(buffer, sends, recvs, x, z, copies):
    for side, last in ((1, NEAR), (-1, NEAR - 1)):
        copies[side * NEAR].wait_recv()
        slot = buffer.at[(z - side * NEAR) & (NZ - 1)]
        for reach in range(last, 0, -1):
            step = side * (NEAR + reach)
            device = x * NZ + ((z + side * reach) & (NZ - 1))
            copies[step] = send(slot, slot, sends.at[step % NZ], recvs.at[step % NZ], device)


def arrive_z(copies):
    for step, copy in copies.items():
        if abs(step) != NEAR:
            copy.wait_recv()


def kernel(
    cos_hbm, sin_hbm, images_hbm, references_hbm, ctf_hbm, noise_hbm, group_hbm, mic_hbm, count_hbm,
    class_post, rot_post,
    cos, sin, images, references, ctf, noise, group, mic, count,
    rows_c, rows_n, rows_s, padded, split_a, split_b, xs, xr, main, tail, rall, gathered, cross,
    turned, ends, wide, zt, mixed, shifted_a, shifted_b, acc_a, score, half, flip, tiles, post, outs,
    local, xsend, xrecv, rsend, rrecv, zsend, zrecv, tsend, trecv, osend, orecv,
):
    me = lax.axis_index("cls")
    x, z = me >> 4, me & (NZ - 1)
    ptl = lax.axis_index("ptl")
    core = ptl & 1
    sibling = ptl + 1 - 2 * core
    along_x = [((x + step) & (NX - 1)) * NZ + z for step in range(1, NX)]

    barrier = pltpu.get_barrier_semaphore()
    near = [x * NZ + ((z + step) & (NZ - 1)) for step in range(-NEAR, NEAR + 1) if step]
    for device in along_x + near:
        pl.semaphore_signal(barrier, inc=1, device_id={"cls": device}, device_id_type=MESH)
    pl.semaphore_signal(barrier, inc=1, device_id={"ptl": sibling}, device_id_type=MESH)
    pairs = [
        (images_hbm, images), (ctf_hbm, ctf), (noise_hbm, noise), (group_hbm, group), (mic_hbm, mic),
        (count_hbm, count), (references_hbm, references), (cos_hbm, cos), (sin_hbm, sin),
    ]
    loads = [pltpu.make_async_copy(a, b, local.at[n]) for n, (a, b) in enumerate(pairs)]
    for load in loads:
        load.start()

    for load in loads[:6]:
        load.wait()
    for p in range(16):
        rows_c[p : p + 1, :] = ctf[pl.ds(group[p], 1), :]
        rows_n[p : p + 1, :] = noise[pl.ds(mic[p], 1), :]
        rows_s[p : p + 1, :] = jnp.full((1, CYCLES), count[p], jnp.int32).astype(jnp.float32)
    counted = rows_s[...]
    ctf_rows = rows_c[...]
    weight = ctf_rows * rows_n[...] * (counted / (counted + 1.0))
    cross[...] = 0.5 * ctf_rows * weight
    own = (x & 1) * NZ + z
    column = jnp.sum(jnp.where(iota((16, CYCLES), 1) == own, weight, 0.0), axis=1, keepdims=True)
    column = column * jnp.where(x >= 2, -1.0, 1.0)
    padded[...] = jnp.zeros_like(padded)
    tail[...] = jnp.zeros_like(tail)
    score[...] = jnp.zeros_like(score)
    padded[:, 0:ANG] = images[...] * column
    full = padded[...]
    row, lane = iota((16, 256), 0) & 3, iota((16, 256), 1) & 3
    rolled = {t: (pltpu.roll(full, t % 256, 1) if t else full) for t in range(-3, 4)}
    for d in range(STEP):
        value = jnp.zeros_like(full)
        for p in range(MINE):
            value = jnp.where((row == p) & (lane == p), rolled[p - d], value)
        for t in range(NX):
            line = jnp.sum(value[4 * t : 4 * t + 4], axis=0, keepdims=True)
            xs[t, d : d + 1, :] = line[:, 0:128]
            xs[t, 4 + d : 5 + d, :] = line[:, 128:256]

    loads[6].wait()
    def divide(m, carry):
        for n in range(8):
            base = pl.multiple_of(8 * ANG * m + ANG * n // 128 * 128, 128)
            block = references[:, pl.ds(base, 256)].astype(jnp.float32)
            if n:
                block = pltpu.roll(block, 256 - 16 * n, 1)
            split_a[pl.ds(8 * m + n, LOCAL, stride=2 * CYCLES), :] = block[:, 0:128]
            split_b[pl.ds(8 * m + n, LOCAL, stride=2 * CYCLES), :] = block[:, 128:256]
        return carry

    lax.fori_loop(0, 2 * CYCLES // 8, divide, 0)
    rho = iota((KT, 1), 0)
    repeat = (iota((KT, 2 * CYCLES), 1) == (rho >> 2)).astype(jnp.float32).astype(jnp.bfloat16)
    angle = iota((1, 256), 1)
    keep = ((rho & 3) == (angle & 3)) & (angle < ANG)
    rho = iota((ROT * LOCAL, 1), 0)
    block_of = jnp.where(rho < LOCAL, 0, ROT - (rho >> 2))
    hit = (angle >> 2) == block_of
    total = jnp.zeros((ROT * LOCAL, KT), jnp.float32)
    for c in range(LOCAL):
        lines = slice(2 * CYCLES * c, 2 * CYCLES * (c + 1))
        one = jnp.concatenate([split_a[lines, :], split_b[lines, :]], axis=1).astype(jnp.bfloat16)
        spread = jnp.dot(repeat, one, preferred_element_type=jnp.float32)
        spread = jnp.where(keep, spread, 0.0).astype(jnp.bfloat16)
        pick = (hit & ((rho & 3) == c)).astype(jnp.float32).astype(jnp.bfloat16)
        total += lax.dot_general(pick, spread, NT, preferred_element_type=jnp.float32)
    rall[x, 0] = total[0:HREF]
    rall[x, 1] = total[HREF:]

    pl.semaphore_wait(barrier, NX + 2 * NEAR)
    x_copies = []
    for n, device in enumerate(along_x):
        x_copies.append(send(xs.at[(x + n + 1) & (NX - 1)], xr.at[x], xsend.at[n], xrecv.at[n], device))
    xr[x] = xs[x]
    left, right = (x + NX - 1) & (NX - 1), (x + 1) & (NX - 1)
    opposite = (x + 2) & (NX - 1)
    part_a, part_b = pl.ds(0, 40), pl.ds(40, HREF - 40)
    slot = rall.at[x, core]
    from_left = send(slot, slot, rsend.at[0], rrecv.at[0], right * NZ + z)
    from_right = send(slot, slot, rsend.at[1], rrecv.at[1], left * NZ + z)

    for copy in x_copies:
        copy.wait_recv()
    last = jnp.zeros((STEP, 128), jnp.float32)
    for t in range(NX):
        block = xr[t]
        gathered[z, 2 * t] = block[0:2]
        gathered[z, 2 * t + 1] = block[2:4]
        rest = block[4:8]
        last = last + (pltpu.roll(rest, 16 * t, 1) if t else rest)
    moved = pltpu.roll(last, 64, 1)
    gathered[z, 8, 0:1, :] = last[0:1] + moved[1:2]
    gathered[z, 8, 1:2, :] = last[2:3] + moved[3:4]
    z_copies = spread_z(gathered, zsend, zrecv, x, z)

    from_left.wait_recv()
    slot = rall.at[left, core]
    part = rall.at[left, core, part_a]
    onward_a = send(part, part, rsend.at[2], rrecv.at[2], right * NZ + z)
    over_left = send(slot, slot, rsend.at[4], rrecv.at[4], me, ptl=sibling)
    from_right.wait_recv()
    slot = rall.at[right, core]
    part = rall.at[right, core, part_b]
    onward_b = send(part, part, rsend.at[3], rrecv.at[3], left * NZ + z)
    over_right = send(slot, slot, rsend.at[5], rrecv.at[5], me, ptl=sibling)
    relay_z(gathered, zsend, zrecv, x, z, z_copies)
    rho = iota((ROWS, 1), 0)
    kappa = ((rho >> 2) & 3) * (ROT * LOCAL) + (rho >> 4) * LOCAL + (rho & 3)
    place = (iota((ROWS, ROWS), 1) == kappa).astype(jnp.float32).astype(jnp.bfloat16)
    onward_a.wait_recv()
    onward_b.wait_recv()
    slot = rall.at[opposite, core]
    over_opposite = send(slot, slot, rsend.at[6], rrecv.at[6], me, ptl=sibling)
    for copy in (over_left, over_right, over_opposite):
        copy.wait_recv()

    stacked = rall[...].reshape(ROWS, KT).astype(jnp.bfloat16)
    turned[...] = jnp.dot(place, stacked, preferred_element_type=jnp.float32)

    near_half, far_half = turned[0:HROWS, :], turned[HROWS:ROWS, :]
    plus = (near_half + far_half).astype(jnp.bfloat16)
    minus = (near_half - far_half).astype(jnp.bfloat16)
    ends[0, 0:HROWS, :] = plus
    ends[0, HROWS:ROWS, :] = plus
    ends[1, 0:HROWS, :] = -minus
    ends[1, HROWS:ROWS, :] = minus
    for sign in range(2):
        for q in range(NB):
            first = ALL_C * (NB - q)
            wide[sign, :, q * KT : (q + 1) * KT] = ends[sign, first : first + WIDE, :]

    power = jnp.zeros((ALL_C, KT), jnp.float32)
    for i in range(ROT):
        line = turned[16 * i : 16 * i + 16, :]
        power += line * line
    half[...] = jnp.zeros_like(half)
    half[0:MINE, :] = cross[pl.ds(x * MINE, MINE), :]
    lam = iota((1, KT), 1)
    spread = (iota((CYCLES, KT), 0) == ((lam >> 2) & 31)).astype(jnp.float32)
    half_wide = jnp.dot(half[...], spread, precision=HIGH, preferred_element_type=jnp.float32)
    quad = lax.dot_general(power, half_wide, NT, precision=HIGH, preferred_element_type=jnp.float32)
    loads[7].wait()
    loads[8].wait()

    arrive_z(z_copies)
    for origin in range(NZ):
        for t in range(NX):
            row = 64 * (t % 2) + 4 * origin
            main[t // 2, row : row + 2, :] = gathered[origin, 2 * t]
            main[t // 2, row + 2 : row + 4, :] = gathered[origin, 2 * t + 1]
        last = gathered[origin, 8]
        moved = pltpu.roll(last, 64, 1)
        row = 4 * origin
        tail[row : row + 1, :] = last[0:1]
        tail[row + 1 : row + 2, :] = moved[0:1]
        tail[row + 2 : row + 3, :] = last[1:2]
        tail[row + 3 : row + 4, :] = moved[1:2]
    rest = tail[...].T
    lane = iota((16, 128), 1)
    for part in range(2):
        zt[part, 0:128] = main[part].T
        low, high = rest[32 * part : 32 * part + 16], rest[32 * part + 16 : 32 * part + 32]
        zt[part, 128:ANG] = jnp.where(lane < 64, low, pltpu.roll(high, 64, 1))
    for part in range(2):
        one, two = zt[part, 0 : ANG // 2, :], zt[part, ANG // 2 : ANG, :]
        mixed[part, 0] = 0.5 * (one + two)
        mixed[part, 1] = 0.5 * (one - two)

    def build(chunk, pair, target):
        for q in range(NB):
            b = chunk * NB + q
            c, s = cos[b].astype(jnp.float32), sin[b].astype(jnp.float32)
            left, right = slice(q * KT, q * KT + 128), slice(q * KT + 128, q * KT + 256)
            for h in range(2):
                line = pl.ds(4 * b + 2 * pair + h, 1)
                rp, rm, ip, im = mixed[0, 0, line], mixed[0, 1, line], mixed[1, 0, line], mixed[1, 1, line]
                rows = slice(128 * h, 128 * h + 128)
                target[0, rows, left] = (c * rp + s * im).astype(jnp.bfloat16)
                target[0, rows, right] = (s * rm - c * ip).astype(jnp.bfloat16)
                target[1, rows, left] = (c * rm + s * ip).astype(jnp.bfloat16)
                target[1, rows, right] = (s * rp - c * im).astype(jnp.bfloat16)

    def multiply(chunk, source, acc):
        start = ALL_C * NB * (CHUNKS - 1 - chunk)
        for sign in range(2):
            left = wide[sign, start : start + HROWS, :]
            part = lax.dot_general(left, source[sign], NT, preferred_element_type=jnp.float32)
            if chunk:
                acc[sign] += part
            else:
                acc[sign] = part

    def reduce(pair, acc):
        size = 48
        lane = iota((size, 128), 1)

        def part(m, carry):
            first = pl.multiple_of(m * size, 16)
            tops = [jnp.zeros((size, 128), jnp.float32)] * 2
            totals = [jnp.ones((size, 128), jnp.float32)] * 2
            for h in range(2):
                even = acc[0, pl.ds(first, size), 128 * h : 128 * h + 128]
                odd = acc[1, pl.ds(first, size), 128 * h : 128 * h + 128]
                for half, value in enumerate((even + odd, even - odd)):
                    high = jnp.max(value, axis=1, keepdims=True)
                    low = jnp.sum(jnp.exp(value - high), axis=1, keepdims=True)
                    tops[half] = jnp.where(lane == 2 * pair + h, high, tops[half])
                    totals[half] = jnp.where(lane == 2 * pair + h, low, totals[half])
            for half in range(2):
                rows = pl.ds(pl.multiple_of(half * HROWS + first, 16), size)
                score[rows, :] += tops[half] + jnp.log(totals[half])
            return carry

        lax.fori_loop(0, HROWS // size, part, 0, unroll=2)

    def step(pair, carry):
        build(1, pair, shifted_b)
        multiply(0, shifted_a, acc_a)
        build(0, jnp.minimum(pair + 1, 1), shifted_a)
        multiply(1, shifted_b, acc_a)
        reduce(pair, acc_a)
        return carry

    build(0, 0, shifted_a)
    lax.fori_loop(0, 2, step, 0)

    values = score[...].reshape(ROT, ALL_C, 128) - quad[None]
    high = jnp.max(values, axis=0)
    by_class = high + jnp.log(jnp.sum(jnp.exp(values - high[None]), axis=0))
    high = jnp.max(values, axis=1)
    by_rot = high + jnp.log(jnp.sum(jnp.exp(values - high[:, None]), axis=1))
    flip[...] = jnp.zeros_like(flip)
    flip[0:ROT, :] = by_rot
    flip[64 : 64 + ALL_C, :] = by_class
    tile = flip[...].T[0:MINE, :]

    tiles[z] = tile
    t_copies = []
    for reach in range(NZ // 2, 0, -1):
        for step in (reach, -reach) if reach < NZ // 2 else (reach,):
            device = x * NZ + ((z + step) & (NZ - 1))
            n = step % NZ
            t_copies.append(send(tiles.at[z], tiles.at[z], tsend.at[n], trecv.at[n], device))
    for copy in t_copies:
        copy.wait_recv()
    values = tiles[...]
    high = jnp.max(values, axis=0)
    rot_lse = high + jnp.log(jnp.sum(jnp.exp(values - high[None]), axis=0))
    lane = iota((MINE, 128), 1)
    masked = jnp.where(lane < ROT, rot_lse, -jnp.inf)
    high = jnp.max(masked, axis=1, keepdims=True)
    norm = high + jnp.log(jnp.sum(jnp.exp(masked - high), axis=1, keepdims=True))
    post[...] = jnp.where(lane < ROT, rot_lse, tile) - norm
    outs[x] = post[...]
    o_copies = []
    for n, device in enumerate(along_x):
        o_copies.append(send(post, outs.at[x], osend.at[n], orecv.at[n], device))
    for copy in o_copies:
        copy.wait_recv()
    line = iota((MINE, 128), 0)
    for t in range(NX):
        live = jnp.zeros((MINE, 128), jnp.int32)
        for p in range(MINE):
            live = jnp.where(line == p, count[MINE * t + p], live)
        value = jnp.where(live > 0, outs[t], 0.0)
        rot_post[MINE * t : MINE * t + MINE, :] = value[:, 0:ROT]
        class_post[MINE * t : MINE * t + MINE, :] = pltpu.roll(value, 64 - LOCAL * x, 1)[:, 0:LOCAL]
    sent = x_copies + [from_left, from_right, onward_a, onward_b, over_left, over_right, over_opposite] + list(z_copies.values()) + t_copies + o_copies
    for copy in sent:
        copy.wait_send()


def body(cos, sin, images, references, ctf_table, noise_inv, defocus_group, micrograph, batch_size):
    vmem, hbm = pl.BlockSpec(memory_space=pltpu.VMEM), pl.BlockSpec(memory_space=pltpu.HBM)
    f32, bf16, i32, dma = jnp.float32, jnp.bfloat16, jnp.int32, pltpu.SemaphoreType.DMA
    operands = (cos, sin, images, references, ctf_table, noise_inv, defocus_group, micrograph, batch_size)
    operands = [pltpu.with_memory_space_constraint(a, pltpu.HBM) for a in operands]
    class_post, rot_post = pl.pallas_call(
        kernel,
        out_shape=(
            jax.ShapeDtypeStruct((16, LOCAL), f32),
            jax.ShapeDtypeStruct((16, ROT), f32),
        ),
        in_specs=[hbm] * 9,
        out_specs=(vmem, vmem),
        scratch_shapes=[
            pltpu.VMEM(cos.shape, bf16),
            pltpu.VMEM(sin.shape, bf16),
            pltpu.VMEM(images.shape, f32),
            pltpu.VMEM(references.shape, bf16),
            pltpu.VMEM(ctf_table.shape, f32),
            pltpu.VMEM(noise_inv.shape, f32),
            pltpu.SMEM((16,), i32),
            pltpu.SMEM((16,), i32),
            pltpu.SMEM((16,), i32),
            pltpu.VMEM((16, CYCLES), f32),
            pltpu.VMEM((16, CYCLES), f32),
            pltpu.VMEM((16, CYCLES), f32),
            pltpu.VMEM((16, 256), f32),
            pltpu.VMEM((2 * CYCLES * LOCAL, 128), f32),
            pltpu.VMEM((2 * CYCLES * LOCAL, 128), f32),
            pltpu.VMEM((NX, 8, 128), f32),
            pltpu.VMEM((NX, 8, 128), f32),
            pltpu.VMEM((2, 128, 128), f32),
            pltpu.VMEM((128, 128), f32),
            pltpu.VMEM((NX, 2, HREF, KT), f32),
            pltpu.VMEM((NZ, 9, 2, 128), f32),
            pltpu.VMEM((16, CYCLES), f32),
            pltpu.VMEM((ROWS, KT), f32),
            pltpu.VMEM((2, ROWS, KT), bf16),
            pltpu.VMEM((2, WIDE, NB * KT), bf16),
            pltpu.VMEM((2, ANG, 128), f32),
            pltpu.VMEM((2, 2, ANG // 2, 128), f32),
            pltpu.VMEM((2, 2 * SHIFTS, NB * KT), bf16),
            pltpu.VMEM((2, 2 * SHIFTS, NB * KT), bf16),
            pltpu.VMEM((2, HROWS, 2 * SHIFTS), f32),
            pltpu.VMEM((ROWS, 128), f32),
            pltpu.VMEM((128, CYCLES), f32),
            pltpu.VMEM((128, 128), f32),
            pltpu.VMEM((NZ, MINE, 128), f32),
            pltpu.VMEM((MINE, 128), f32),
            pltpu.VMEM((NX, MINE, 128), f32),
            dma((9,)),
            dma((NX - 1,)),
            dma((NX - 1,)),
            dma((7,)),
            dma((7,)),
            dma((NZ,)),
            dma((NZ,)),
            dma((NZ,)),
            dma((NZ,)),
            dma((NX - 1,)),
            dma((NX - 1,)),
        ],
        compiler_params=pltpu.CompilerParams(collective_id=0, has_side_effects=True, vmem_limit_bytes=40 << 20),
        name="expectation",
    )(*operands)
    return class_post, rot_post


def solution(mesh):
    cos, sin = phase_tables()
    in_specs = (P("ptl", "cls"), P("cls", None), P(), P(), P("ptl"), P("ptl"), P("ptl"))
    out_specs = (P("ptl", "cls"), P("ptl", None))
    mapped = jax.shard_map(
        body, mesh=mesh, in_specs=(P(), P()) + in_specs, out_specs=out_specs, check_vma=False
    )

    def run(*args):
        return mapped(jnp.asarray(cos), jnp.asarray(sin), *args)

    return run
```

```python
import math

import jax
import jax.numpy as jnp
import numpy as np
from jax import lax
from jax.experimental import pallas as pl
from jax.experimental.pallas import tpu as pltpu
from jax.sharding import PartitionSpec as P

CYCLES = 32
ANG = 144
ROT = 36
SHIFTS = 128
BOX = 128
STEP = ANG // ROT
NX, NZ = 4, 16
LOCAL = 4
MINE = 4
ALL_C = NX * LOCAL
ROWS = ROT * ALL_C
KT = 256
NB = 9
HALF = ROT // 2
HREF = ROT * LOCAL // 2
CHUNKS = HALF // NB
HROWS = HALF * ALL_C
WIDE = (2 * HALF - NB) * ALL_C
NEAR = 4
MESH = pl.DeviceIdType.MESH
HIGH = lax.Precision.HIGHEST
NT = (((1,), (1,)), ((), ()))


def phase_tables():
    radius = (np.arange(CYCLES, dtype=np.float64) + 1.0) / BOX
    theta = np.arange(ANG, dtype=np.float64) * (2.0 * math.pi / ANG)
    index = np.arange(SHIFTS)
    shift_x = (index % 16 - 8).astype(np.float64)
    shift_y = (index // 16 - SHIFTS // 32).astype(np.float64)
    along = np.cos(theta)[:, None] * shift_x + np.sin(theta)[:, None] * shift_y
    phase = 2.0 * math.pi * radius[:, None, None] * along[None]

    def order(table):
        table = table.reshape(2, NZ, ROT, STEP, SHIFTS).transpose(2, 4, 0, 1, 3)
        return table.reshape(ROT, SHIFTS, 128)[:HALF].astype(jnp.bfloat16)

    return order(np.cos(phase)), order(np.sin(phase))


def iota(shape, axis):
    return lax.broadcasted_iota(jnp.int32, shape, axis)


def send(src, dst, send_sem, recv_sem, device, **other):
    copy = pltpu.make_async_remote_copy(
        src_ref=src,
        dst_ref=dst,
        send_sem=send_sem,
        recv_sem=recv_sem,
        device_id={"cls": device, **other},
        device_id_type=MESH,
    )
    copy.start()
    return copy


def spread_z(buffer, sends, recvs, x, z):
    copies = {}
    for reach in range(NEAR, 0, -1):
        for step in (reach, -reach):
            device = x * NZ + ((z + step) & (NZ - 1))
            slot = buffer.at[z]
            copies[step] = send(slot, slot, sends.at[step % NZ], recvs.at[step % NZ], device)
    return copies


def relay_z(buffer, sends, recvs, x, z, copies):
    for side, last in ((1, NEAR), (-1, NEAR - 1)):
        copies[side * NEAR].wait_recv()
        slot = buffer.at[(z - side * NEAR) & (NZ - 1)]
        for reach in range(last, 0, -1):
            step = side * (NEAR + reach)
            device = x * NZ + ((z + side * reach) & (NZ - 1))
            copies[step] = send(slot, slot, sends.at[step % NZ], recvs.at[step % NZ], device)


def arrive_z(copies):
    for step, copy in copies.items():
        if abs(step) != NEAR:
            copy.wait_recv()


def kernel(
    cos_hbm, sin_hbm, images_hbm, references_hbm, ctf_hbm, noise_hbm, group_hbm, mic_hbm, count_hbm,
    class_post, rot_post,
    cos, sin, images, references, ctf, noise, group, mic, count,
    rows_c, rows_n, rows_s, padded, split_a, split_b, xs, xr, main, tail, rall, gathered, cross,
    turned, ends, wide, zt, mixed, shifted_a, shifted_b, acc_a, score, half, flip, tiles, post, outs,
    local, xsend, xrecv, rsend, rrecv, zsend, zrecv, tsend, trecv, osend, orecv,
):
    me = lax.axis_index("cls")
    x, z = me >> 4, me & (NZ - 1)
    ptl = lax.axis_index("ptl")
    core = ptl & 1
    sibling = ptl + 1 - 2 * core
    along_x = [((x + step) & (NX - 1)) * NZ + z for step in range(1, NX)]

    barrier = pltpu.get_barrier_semaphore()
    near = [x * NZ + ((z + step) & (NZ - 1)) for step in range(-NEAR, NEAR + 1) if step]
    for device in along_x + near:
        pl.semaphore_signal(barrier, inc=1, device_id={"cls": device}, device_id_type=MESH)
    pl.semaphore_signal(barrier, inc=1, device_id={"ptl": sibling}, device_id_type=MESH)
    pairs = [
        (images_hbm, images), (ctf_hbm, ctf), (noise_hbm, noise), (group_hbm, group), (mic_hbm, mic),
        (count_hbm, count), (references_hbm, references), (cos_hbm, cos), (sin_hbm, sin),
    ]
    loads = [pltpu.make_async_copy(a, b, local.at[n]) for n, (a, b) in enumerate(pairs)]
    for load in loads:
        load.start()

    for load in loads[:6]:
        load.wait()
    for p in range(16):
        rows_c[p : p + 1, :] = ctf[pl.ds(group[p], 1), :]
        rows_n[p : p + 1, :] = noise[pl.ds(mic[p], 1), :]
        rows_s[p : p + 1, :] = jnp.full((1, CYCLES), count[p], jnp.int32).astype(jnp.float32)
    counted = rows_s[...]
    ctf_rows = rows_c[...]
    weight = ctf_rows * rows_n[...] * (counted / (counted + 1.0))
    cross[...] = 0.5 * ctf_rows * weight
    own = (x & 1) * NZ + z
    column = jnp.sum(jnp.where(iota((16, CYCLES), 1) == own, weight, 0.0), axis=1, keepdims=True)
    column = column * jnp.where(x >= 2, -1.0, 1.0)
    padded[...] = jnp.zeros_like(padded)
    tail[...] = jnp.zeros_like(tail)
    score[...] = jnp.zeros_like(score)
    padded[:, 0:ANG] = images[...] * column
    full = padded[...]
    row, lane = iota((16, 256), 0) & 3, iota((16, 256), 1) & 3
    rolled = {t: (pltpu.roll(full, t % 256, 1) if t else full) for t in range(-3, 4)}
    for d in range(STEP):
        value = jnp.zeros_like(full)
        for p in range(MINE):
            value = jnp.where((row == p) & (lane == p), rolled[p - d], value)
        for t in range(NX):
            line = jnp.sum(value[4 * t : 4 * t + 4], axis=0, keepdims=True)
            xs[t, d : d + 1, :] = line[:, 0:128]
            xs[t, 4 + d : 5 + d, :] = line[:, 128:256]

    loads[6].wait()
    def divide(m, carry):
        for n in range(8):
            base = pl.multiple_of(8 * ANG * m + ANG * n // 128 * 128, 128)
            block = references[:, pl.ds(base, 256)].astype(jnp.float32)
            if n:
                block = pltpu.roll(block, 256 - 16 * n, 1)
            split_a[pl.ds(8 * m + n, LOCAL, stride=2 * CYCLES), :] = block[:, 0:128]
            split_b[pl.ds(8 * m + n, LOCAL, stride=2 * CYCLES), :] = block[:, 128:256]
        return carry

    lax.fori_loop(0, 2 * CYCLES // 8, divide, 0)
    rho = iota((KT, 1), 0)
    repeat = (iota((KT, 2 * CYCLES), 1) == (rho >> 2)).astype(jnp.float32).astype(jnp.bfloat16)
    angle = iota((1, 256), 1)
    keep = ((rho & 3) == (angle & 3)) & (angle < ANG)
    rho = iota((ROT * LOCAL, 1), 0)
    block_of = jnp.where(rho < LOCAL, 0, ROT - (rho >> 2))
    hit = (angle >> 2) == block_of
    total = jnp.zeros((ROT * LOCAL, KT), jnp.float32)
    for c in range(LOCAL):
        lines = slice(2 * CYCLES * c, 2 * CYCLES * (c + 1))
        one = jnp.concatenate([split_a[lines, :], split_b[lines, :]], axis=1).astype(jnp.bfloat16)
        spread = jnp.dot(repeat, one, preferred_element_type=jnp.float32)
        spread = jnp.where(keep, spread, 0.0).astype(jnp.bfloat16)
        pick = (hit & ((rho & 3) == c)).astype(jnp.float32).astype(jnp.bfloat16)
        total += lax.dot_general(pick, spread, NT, preferred_element_type=jnp.float32)
    rall[x, 0] = total[0:HREF]
    rall[x, 1] = total[HREF:]

    pl.semaphore_wait(barrier, NX + 2 * NEAR)
    x_copies = []
    for n, device in enumerate(along_x):
        x_copies.append(send(xs.at[(x + n + 1) & (NX - 1)], xr.at[x], xsend.at[n], xrecv.at[n], device))
    xr[x] = xs[x]
    left, right = (x + NX - 1) & (NX - 1), (x + 1) & (NX - 1)
    opposite = (x + 2) & (NX - 1)
    part_a, part_b = pl.ds(0, 40), pl.ds(40, HREF - 40)

    for copy in x_copies:
        copy.wait_recv()
    last = jnp.zeros((STEP, 128), jnp.float32)
    for t in range(NX):
        block = xr[t]
        gathered[z, 2 * t] = block[0:2]
        gathered[z, 2 * t + 1] = block[2:4]
        rest = block[4:8]
        last = last + (pltpu.roll(rest, 16 * t, 1) if t else rest)
    moved = pltpu.roll(last, 64, 1)
    gathered[z, 8, 0:1, :] = last[0:1] + moved[1:2]
    gathered[z, 8, 1:2, :] = last[2:3] + moved[3:4]
    z_copies = spread_z(gathered, zsend, zrecv, x, z)
    slot = rall.at[x, core]
    from_left = send(slot, slot, rsend.at[0], rrecv.at[0], right * NZ + z)
    from_right = send(slot, slot, rsend.at[1], rrecv.at[1], left * NZ + z)

    relay_z(gathered, zsend, zrecv, x, z, z_copies)
    from_left.wait_recv()
    slot = rall.at[left, core]
    part = rall.at[left, core, part_a]
    onward_a = send(part, part, rsend.at[2], rrecv.at[2], right * NZ + z)
    over_left = send(slot, slot, rsend.at[4], rrecv.at[4], me, ptl=sibling)
    from_right.wait_recv()
    slot = rall.at[right, core]
    part = rall.at[right, core, part_b]
    onward_b = send(part, part, rsend.at[3], rrecv.at[3], left * NZ + z)
    over_right = send(slot, slot, rsend.at[5], rrecv.at[5], me, ptl=sibling)
    rho = iota((ROWS, 1), 0)
    kappa = ((rho >> 2) & 3) * (ROT * LOCAL) + (rho >> 4) * LOCAL + (rho & 3)
    place = (iota((ROWS, ROWS), 1) == kappa).astype(jnp.float32).astype(jnp.bfloat16)
    onward_a.wait_recv()
    onward_b.wait_recv()
    slot = rall.at[opposite, core]
    over_opposite = send(slot, slot, rsend.at[6], rrecv.at[6], me, ptl=sibling)
    for copy in (over_left, over_right, over_opposite):
        copy.wait_recv()

    stacked = rall[...].reshape(ROWS, KT).astype(jnp.bfloat16)
    turned[...] = jnp.dot(place, stacked, preferred_element_type=jnp.float32)

    near_half, far_half = turned[0:HROWS, :], turned[HROWS:ROWS, :]
    plus = (near_half + far_half).astype(jnp.bfloat16)
    minus = (near_half - far_half).astype(jnp.bfloat16)
    ends[0, 0:HROWS, :] = plus
    ends[0, HROWS:ROWS, :] = plus
    ends[1, 0:HROWS, :] = -minus
    ends[1, HROWS:ROWS, :] = minus
    for sign in range(2):
        for q in range(NB):
            first = ALL_C * (NB - q)
            wide[sign, :, q * KT : (q + 1) * KT] = ends[sign, first : first + WIDE, :]

    power = jnp.zeros((ALL_C, KT), jnp.float32)
    for i in range(ROT):
        line = turned[16 * i : 16 * i + 16, :]
        power += line * line
    half[...] = jnp.zeros_like(half)
    half[0:MINE, :] = cross[pl.ds(x * MINE, MINE), :]
    lam = iota((1, KT), 1)
    spread = (iota((CYCLES, KT), 0) == ((lam >> 2) & 31)).astype(jnp.float32)
    half_wide = jnp.dot(half[...], spread, precision=HIGH, preferred_element_type=jnp.float32)
    quad = lax.dot_general(power, half_wide, NT, precision=HIGH, preferred_element_type=jnp.float32)
    loads[7].wait()
    loads[8].wait()

    arrive_z(z_copies)
    for origin in range(NZ):
        for t in range(NX):
            row = 64 * (t % 2) + 4 * origin
            main[t // 2, row : row + 2, :] = gathered[origin, 2 * t]
            main[t // 2, row + 2 : row + 4, :] = gathered[origin, 2 * t + 1]
        last = gathered[origin, 8]
        moved = pltpu.roll(last, 64, 1)
        row = 4 * origin
        tail[row : row + 1, :] = last[0:1]
        tail[row + 1 : row + 2, :] = moved[0:1]
        tail[row + 2 : row + 3, :] = last[1:2]
        tail[row + 3 : row + 4, :] = moved[1:2]
    rest = tail[...].T
    lane = iota((16, 128), 1)
    for part in range(2):
        zt[part, 0:128] = main[part].T
        low, high = rest[32 * part : 32 * part + 16], rest[32 * part + 16 : 32 * part + 32]
        zt[part, 128:ANG] = jnp.where(lane < 64, low, pltpu.roll(high, 64, 1))
    for part in range(2):
        one, two = zt[part, 0 : ANG // 2, :], zt[part, ANG // 2 : ANG, :]
        mixed[part, 0] = 0.5 * (one + two)
        mixed[part, 1] = 0.5 * (one - two)

    def build(chunk, pair, target):
        for q in range(NB):
            b = chunk * NB + q
            c, s = cos[b].astype(jnp.float32), sin[b].astype(jnp.float32)
            left, right = slice(q * KT, q * KT + 128), slice(q * KT + 128, q * KT + 256)
            for h in range(2):
                line = pl.ds(4 * b + 2 * pair + h, 1)
                rp, rm, ip, im = mixed[0, 0, line], mixed[0, 1, line], mixed[1, 0, line], mixed[1, 1, line]
                rows = slice(128 * h, 128 * h + 128)
                target[0, rows, left] = (c * rp + s * im).astype(jnp.bfloat16)
                target[0, rows, right] = (s * rm - c * ip).astype(jnp.bfloat16)
                target[1, rows, left] = (c * rm + s * ip).astype(jnp.bfloat16)
                target[1, rows, right] = (s * rp - c * im).astype(jnp.bfloat16)

    def multiply(chunk, source, acc):
        start = ALL_C * NB * (CHUNKS - 1 - chunk)
        for sign in range(2):
            left = wide[sign, start : start + HROWS, :]
            part = lax.dot_general(left, source[sign], NT, preferred_element_type=jnp.float32)
            if chunk:
                acc[sign] += part
            else:
                acc[sign] = part

    def reduce(pair, acc):
        size = 48
        lane = iota((size, 128), 1)

        def part(m, carry):
            first = pl.multiple_of(m * size, 16)
            tops = [jnp.zeros((size, 128), jnp.float32)] * 2
            totals = [jnp.ones((size, 128), jnp.float32)] * 2
            for h in range(2):
                even = acc[0, pl.ds(first, size), 128 * h : 128 * h + 128]
                odd = acc[1, pl.ds(first, size), 128 * h : 128 * h + 128]
                for half, value in enumerate((even + odd, even - odd)):
                    high = jnp.max(value, axis=1, keepdims=True)
                    low = jnp.sum(jnp.exp(value - high), axis=1, keepdims=True)
                    tops[half] = jnp.where(lane == 2 * pair + h, high, tops[half])
                    totals[half] = jnp.where(lane == 2 * pair + h, low, totals[half])
            for half in range(2):
                rows = pl.ds(pl.multiple_of(half * HROWS + first, 16), size)
                score[rows, :] += tops[half] + jnp.log(totals[half])
            return carry

        lax.fori_loop(0, HROWS // size, part, 0, unroll=2)

    def step(pair, carry):
        build(1, pair, shifted_b)
        multiply(0, shifted_a, acc_a)
        build(0, jnp.minimum(pair + 1, 1), shifted_a)
        multiply(1, shifted_b, acc_a)
        reduce(pair, acc_a)
        return carry

    build(0, 0, shifted_a)
    lax.fori_loop(0, 2, step, 0)

    values = score[...].reshape(ROT, ALL_C, 128) - quad[None]
    high = jnp.max(values, axis=0)
    by_class = high + jnp.log(jnp.sum(jnp.exp(values - high[None]), axis=0))
    high = jnp.max(values, axis=1)
    by_rot = high + jnp.log(jnp.sum(jnp.exp(values - high[:, None]), axis=1))
    flip[...] = jnp.zeros_like(flip)
    flip[0:ROT, :] = by_rot
    flip[64 : 64 + ALL_C, :] = by_class
    tile = flip[...].T[0:MINE, :]

    tiles[z] = tile
    t_copies = []
    for reach in range(NZ // 2, 0, -1):
        for step in (reach, -reach) if reach < NZ // 2 else (reach,):
            device = x * NZ + ((z + step) & (NZ - 1))
            n = step % NZ
            t_copies.append(send(tiles.at[z], tiles.at[z], tsend.at[n], trecv.at[n], device))
    for copy in t_copies:
        copy.wait_recv()
    values = tiles[...]
    high = jnp.max(values, axis=0)
    rot_lse = high + jnp.log(jnp.sum(jnp.exp(values - high[None]), axis=0))
    lane = iota((MINE, 128), 1)
    masked = jnp.where(lane < ROT, rot_lse, -jnp.inf)
    high = jnp.max(masked, axis=1, keepdims=True)
    norm = high + jnp.log(jnp.sum(jnp.exp(masked - high), axis=1, keepdims=True))
    post[...] = jnp.where(lane < ROT, rot_lse, tile) - norm
    outs[x] = post[...]
    o_copies = []
    for n, device in enumerate(along_x):
        o_copies.append(send(post, outs.at[x], osend.at[n], orecv.at[n], device))
    for copy in o_copies:
        copy.wait_recv()
    line = iota((MINE, 128), 0)
    for t in range(NX):
        live = jnp.zeros((MINE, 128), jnp.int32)
        for p in range(MINE):
            live = jnp.where(line == p, count[MINE * t + p], live)
        value = jnp.where(live > 0, outs[t], 0.0)
        rot_post[MINE * t : MINE * t + MINE, :] = value[:, 0:ROT]
        class_post[MINE * t : MINE * t + MINE, :] = pltpu.roll(value, 64 - LOCAL * x, 1)[:, 0:LOCAL]
    sent = x_copies + [from_left, from_right, onward_a, onward_b, over_left, over_right, over_opposite] + list(z_copies.values()) + t_copies + o_copies
    for copy in sent:
        copy.wait_send()


def body(cos, sin, images, references, ctf_table, noise_inv, defocus_group, micrograph, batch_size):
    vmem, hbm = pl.BlockSpec(memory_space=pltpu.VMEM), pl.BlockSpec(memory_space=pltpu.HBM)
    f32, bf16, i32, dma = jnp.float32, jnp.bfloat16, jnp.int32, pltpu.SemaphoreType.DMA
    operands = (cos, sin, images, references, ctf_table, noise_inv, defocus_group, micrograph, batch_size)
    operands = [pltpu.with_memory_space_constraint(a, pltpu.HBM) for a in operands]
    class_post, rot_post = pl.pallas_call(
        kernel,
        out_shape=(
            jax.ShapeDtypeStruct((16, LOCAL), f32),
            jax.ShapeDtypeStruct((16, ROT), f32),
        ),
        in_specs=[hbm] * 9,
        out_specs=(vmem, vmem),
        scratch_shapes=[
            pltpu.VMEM(cos.shape, bf16),
            pltpu.VMEM(sin.shape, bf16),
            pltpu.VMEM(images.shape, f32),
            pltpu.VMEM(references.shape, bf16),
            pltpu.VMEM(ctf_table.shape, f32),
            pltpu.VMEM(noise_inv.shape, f32),
            pltpu.SMEM((16,), i32),
            pltpu.SMEM((16,), i32),
            pltpu.SMEM((16,), i32),
            pltpu.VMEM((16, CYCLES), f32),
            pltpu.VMEM((16, CYCLES), f32),
            pltpu.VMEM((16, CYCLES), f32),
            pltpu.VMEM((16, 256), f32),
            pltpu.VMEM((2 * CYCLES * LOCAL, 128), f32),
            pltpu.VMEM((2 * CYCLES * LOCAL, 128), f32),
            pltpu.VMEM((NX, 8, 128), f32),
            pltpu.VMEM((NX, 8, 128), f32),
            pltpu.VMEM((2, 128, 128), f32),
            pltpu.VMEM((128, 128), f32),
            pltpu.VMEM((NX, 2, HREF, KT), f32),
            pltpu.VMEM((NZ, 9, 2, 128), f32),
            pltpu.VMEM((16, CYCLES), f32),
            pltpu.VMEM((ROWS, KT), f32),
            pltpu.VMEM((2, ROWS, KT), bf16),
            pltpu.VMEM((2, WIDE, NB * KT), bf16),
            pltpu.VMEM((2, ANG, 128), f32),
            pltpu.VMEM((2, 2, ANG // 2, 128), f32),
            pltpu.VMEM((2, 2 * SHIFTS, NB * KT), bf16),
            pltpu.VMEM((2, 2 * SHIFTS, NB * KT), bf16),
            pltpu.VMEM((2, HROWS, 2 * SHIFTS), f32),
            pltpu.VMEM((ROWS, 128), f32),
            pltpu.VMEM((128, CYCLES), f32),
            pltpu.VMEM((128, 128), f32),
            pltpu.VMEM((NZ, MINE, 128), f32),
            pltpu.VMEM((MINE, 128), f32),
            pltpu.VMEM((NX, MINE, 128), f32),
            dma((9,)),
            dma((NX - 1,)),
            dma((NX - 1,)),
            dma((7,)),
            dma((7,)),
            dma((NZ,)),
            dma((NZ,)),
            dma((NZ,)),
            dma((NZ,)),
            dma((NX - 1,)),
            dma((NX - 1,)),
        ],
        compiler_params=pltpu.CompilerParams(collective_id=0, has_side_effects=True, vmem_limit_bytes=40 << 20),
        name="expectation",
    )(*operands)
    return class_post, rot_post


def solution(mesh):
    cos, sin = phase_tables()
    in_specs = (P("ptl", "cls"), P("cls", None), P(), P(), P("ptl"), P("ptl"), P("ptl"))
    out_specs = (P("ptl", "cls"), P("ptl", None))
    mapped = jax.shard_map(
        body, mesh=mesh, in_specs=(P(), P()) + in_specs, out_specs=out_specs, check_vma=False
    )

    def run(*args):
        return mapped(jnp.asarray(cos), jnp.asarray(sin), *args)

    return run
```

```python
import math

import jax
import jax.numpy as jnp
import numpy as np
from jax import lax
from jax.experimental import pallas as pl
from jax.experimental.pallas import tpu as pltpu
from jax.sharding import PartitionSpec as P

CYCLES = 32
ANG = 144
ROT = 36
SHIFTS = 128
BOX = 128
STEP = ANG // ROT
NX, NZ = 4, 16
LOCAL = 4
MINE = 4
ALL_C = NX * LOCAL
KT = 256
NB = 9
HALF = ROT // 2
HREF = ROT * LOCAL // 2
CHUNKS = HALF // NB
BLOCK = 80
NEAR = 4
MESH = pl.DeviceIdType.MESH
HIGH = lax.Precision.HIGHEST
NT = (((1,), (1,)), ((), ()))


def phase_tables():
    radius = (np.arange(CYCLES, dtype=np.float64) + 1.0) / BOX
    theta = np.arange(ANG, dtype=np.float64) * (2.0 * math.pi / ANG)
    index = np.arange(SHIFTS)
    shift_x = (index % 16 - 8).astype(np.float64)
    shift_y = (index // 16 - SHIFTS // 32).astype(np.float64)
    along = np.cos(theta)[:, None] * shift_x + np.sin(theta)[:, None] * shift_y
    phase = 2.0 * math.pi * radius[:, None, None] * along[None]

    def order(table):
        table = table.reshape(2, NZ, ROT, STEP, SHIFTS).transpose(2, 4, 0, 1, 3)
        return table.reshape(ROT, SHIFTS, 128)[:HALF].astype(jnp.bfloat16)

    return order(np.cos(phase)), order(np.sin(phase))


def iota(shape, axis):
    return lax.broadcasted_iota(jnp.int32, shape, axis)


def send(src, dst, send_sem, recv_sem, device, **other):
    copy = pltpu.make_async_remote_copy(
        src_ref=src,
        dst_ref=dst,
        send_sem=send_sem,
        recv_sem=recv_sem,
        device_id={"cls": device, **other},
        device_id_type=MESH,
    )
    copy.start()
    return copy


def spread_z(buffer, sends, recvs, x, z):
    copies = {}
    for reach in range(NEAR, 0, -1):
        for step in (reach, -reach):
            device = x * NZ + ((z + step) & (NZ - 1))
            slot = buffer.at[z]
            copies[step] = send(slot, slot, sends.at[step % NZ], recvs.at[step % NZ], device)
    return copies


def relay_z(buffer, sends, recvs, x, z, copies):
    for side, last in ((1, NEAR), (-1, NEAR - 1)):
        copies[side * NEAR].wait_recv()
        slot = buffer.at[(z - side * NEAR) & (NZ - 1)]
        for reach in range(last, 0, -1):
            step = side * (NEAR + reach)
            device = x * NZ + ((z + side * reach) & (NZ - 1))
            copies[step] = send(slot, slot, sends.at[step % NZ], recvs.at[step % NZ], device)


def arrive_z(copies):
    for step, copy in copies.items():
        if abs(step) != NEAR:
            copy.wait_recv()


def kernel(
    cos_hbm, sin_hbm, images_hbm, references_hbm, ctf_hbm, noise_hbm, group_hbm, mic_hbm, count_hbm,
    class_post, rot_post,
    cos, sin, images, references, ctf, noise, group, mic, count,
    rows_c, rows_n, rows_s, padded, split_a, split_b, xs, xr, main, tail, rall, gathered, cross,
    ends, matrix, power, zt, mixed, shifted_a, shifted_b, acc_a, score, lines, half, flip, tiles, post, outs,
    local, xsend, xrecv, rsend, rrecv, zsend, zrecv, tsend, trecv, osend, orecv,
):
    me = lax.axis_index("cls")
    x, z = me >> 4, me & (NZ - 1)
    ptl = lax.axis_index("ptl")
    core = ptl & 1
    sibling = ptl + 1 - 2 * core
    along_x = [((x + step) & (NX - 1)) * NZ + z for step in range(1, NX)]

    barrier = pltpu.get_barrier_semaphore()
    near = [x * NZ + ((z + step) & (NZ - 1)) for step in range(-NEAR, NEAR + 1) if step]
    for device in along_x + near:
        pl.semaphore_signal(barrier, inc=1, device_id={"cls": device}, device_id_type=MESH)
    pl.semaphore_signal(barrier, inc=1, device_id={"ptl": sibling}, device_id_type=MESH)
    pairs = [
        (images_hbm, images), (ctf_hbm, ctf), (noise_hbm, noise), (group_hbm, group), (mic_hbm, mic),
        (count_hbm, count), (references_hbm, references), (cos_hbm, cos), (sin_hbm, sin),
    ]
    loads = [pltpu.make_async_copy(a, b, local.at[n]) for n, (a, b) in enumerate(pairs)]
    for load in loads:
        load.start()

    loads[6].wait()
    def divide(m, carry):
        for n in range(8):
            base = pl.multiple_of(8 * ANG * m + ANG * n // 128 * 128, 128)
            block = references[:, pl.ds(base, 256)].astype(jnp.float32)
            if n:
                block = pltpu.roll(block, 256 - 16 * n, 1)
            split_a[pl.ds(8 * m + n, LOCAL, stride=2 * CYCLES), :] = block[:, 0:128]
            split_b[pl.ds(8 * m + n, LOCAL, stride=2 * CYCLES), :] = block[:, 128:256]
        return carry

    lax.fori_loop(0, 2 * CYCLES // 8, divide, 0)
    rho = iota((KT, 1), 0)
    repeat = (iota((KT, 2 * CYCLES), 1) == (rho >> 2)).astype(jnp.float32).astype(jnp.bfloat16)
    angle = iota((1, 256), 1)
    keep = ((rho & 3) == (angle & 3)) & (angle < ANG)
    rho = iota((ROT * LOCAL, 1), 0)
    block_of = jnp.where(rho < LOCAL, 0, ROT - (rho >> 2))
    hit = (angle >> 2) == block_of
    total = jnp.zeros((ROT * LOCAL, KT), jnp.float32)
    for c in range(LOCAL):
        cut = slice(2 * CYCLES * c, 2 * CYCLES * (c + 1))
        one = jnp.concatenate([split_a[cut, :], split_b[cut, :]], axis=1).astype(jnp.bfloat16)
        spread = jnp.dot(repeat, one, preferred_element_type=jnp.float32)
        spread = jnp.where(keep, spread, 0.0).astype(jnp.bfloat16)
        pick = (hit & ((rho & 3) == c)).astype(jnp.float32).astype(jnp.bfloat16)
        total += lax.dot_general(pick, spread, NT, preferred_element_type=jnp.float32)
    rall[x, 0] = total[0:HREF]
    rall[x, 1] = total[HREF:]

    pl.semaphore_wait(barrier, NX + 2 * NEAR)
    left, right = (x + NX - 1) & (NX - 1), (x + 1) & (NX - 1)
    opposite = (x + 2) & (NX - 1)
    part_a, part_b = pl.ds(0, 40), pl.ds(40, HREF - 40)
    slot = rall.at[x, core]
    from_left = send(slot, slot, rsend.at[0], rrecv.at[0], right * NZ + z)
    from_right = send(slot, slot, rsend.at[1], rrecv.at[1], left * NZ + z)

    for load in loads[:6]:
        load.wait()
    for p in range(16):
        rows_c[p : p + 1, :] = ctf[pl.ds(group[p], 1), :]
        rows_n[p : p + 1, :] = noise[pl.ds(mic[p], 1), :]
        rows_s[p : p + 1, :] = jnp.full((1, CYCLES), count[p], jnp.int32).astype(jnp.float32)
    counted = rows_s[...]
    ctf_rows = rows_c[...]
    weight = ctf_rows * rows_n[...] * (counted / (counted + 1.0))
    cross[...] = 0.5 * ctf_rows * weight
    own = (x & 1) * NZ + z
    column = jnp.sum(jnp.where(iota((16, CYCLES), 1) == own, weight, 0.0), axis=1, keepdims=True)
    column = column * jnp.where(x >= 2, -1.0, 1.0)
    padded[...] = jnp.zeros_like(padded)
    tail[...] = jnp.zeros_like(tail)
    score[...] = jnp.zeros_like(score)
    ends[:, :, 2 * HREF :, :] = jnp.zeros((2, 2, 8, 128), jnp.float32)
    padded[:, 0:ANG] = images[...] * column
    full = padded[...]
    row, lane = iota((16, 256), 0) & 3, iota((16, 256), 1) & 3
    rolled = {t: (pltpu.roll(full, t % 256, 1) if t else full) for t in range(-3, 4)}
    for d in range(STEP):
        value = jnp.zeros_like(full)
        for p in range(MINE):
            value = jnp.where((row == p) & (lane == p), rolled[p - d], value)
        for t in range(NX):
            line = jnp.sum(value[4 * t : 4 * t + 4], axis=0, keepdims=True)
            xs[t, d : d + 1, :] = line[:, 0:128]
            xs[t, 4 + d : 5 + d, :] = line[:, 128:256]
    x_copies = []
    for n, device in enumerate(along_x):
        x_copies.append(send(xs.at[(x + n + 1) & (NX - 1)], xr.at[x], xsend.at[n], xrecv.at[n], device))
    xr[x] = xs[x]

    def place(t):
        low, high = rall[t, 0], rall[t, 1]
        plus, minus = low + high, low - high
        for lanes in range(2):
            cut = slice(128 * lanes, 128 * lanes + 128)
            ends[0, lanes, 0:HREF, :] = plus[:, cut]
            ends[0, lanes, HREF : 2 * HREF, :] = plus[:, cut]
            ends[1, lanes, 0:HREF, :] = -minus[:, cut]
            ends[1, lanes, HREF : 2 * HREF, :] = minus[:, cut]
        rows = pl.ds(pl.multiple_of(BLOCK * t, 16), BLOCK)
        for sign in range(2):
            for chunk in range(CHUNKS):
                for q in range(NB):
                    first = LOCAL * (HALF - NB * chunk - q)
                    for lanes in range(2):
                        at = KT * q + 128 * lanes
                        value = ends[sign, lanes, first : first + BLOCK, :]
                        matrix[sign, chunk, rows, at : at + 128] = value.astype(jnp.bfloat16)
        square = jnp.sum((low * low + high * high).reshape(HREF // 8, 8, KT), axis=0)
        power[pl.ds(pl.multiple_of(8 * t, 8), 8), :] = square + pltpu.roll(square, 4, 0)

    for copy in x_copies:
        copy.wait_recv()
    last = jnp.zeros((STEP, 128), jnp.float32)
    for t in range(NX):
        block = xr[t]
        gathered[z, 2 * t] = block[0:2]
        gathered[z, 2 * t + 1] = block[2:4]
        rest = block[4:8]
        last = last + (pltpu.roll(rest, 16 * t, 1) if t else rest)
    moved = pltpu.roll(last, 64, 1)
    gathered[z, 8, 0:1, :] = last[0:1] + moved[1:2]
    gathered[z, 8, 1:2, :] = last[2:3] + moved[3:4]
    z_copies = spread_z(gathered, zsend, zrecv, x, z)

    from_left.wait_recv()
    slot = rall.at[left, core]
    part = rall.at[left, core, part_a]
    onward_a = send(part, part, rsend.at[2], rrecv.at[2], right * NZ + z)
    over_left = send(slot, slot, rsend.at[4], rrecv.at[4], me, ptl=sibling)
    from_right.wait_recv()
    slot = rall.at[right, core]
    part = rall.at[right, core, part_b]
    onward_b = send(part, part, rsend.at[3], rrecv.at[3], left * NZ + z)
    over_right = send(slot, slot, rsend.at[5], rrecv.at[5], me, ptl=sibling)
    relay_z(gathered, zsend, zrecv, x, z, z_copies)
    place(x)
    onward_a.wait_recv()
    onward_b.wait_recv()
    slot = rall.at[opposite, core]
    over_opposite = send(slot, slot, rsend.at[6], rrecv.at[6], me, ptl=sibling)
    over_left.wait_recv()
    place(left)
    over_right.wait_recv()
    place(right)
    over_opposite.wait_recv()
    place(opposite)

    half[...] = jnp.zeros_like(half)
    half[0:MINE, :] = cross[pl.ds(x * MINE, MINE), :]
    lam = iota((1, KT), 1)
    spread = (iota((CYCLES, KT), 0) == ((lam >> 2) & 31)).astype(jnp.float32)
    half_wide = jnp.dot(half[...], spread, precision=HIGH, preferred_element_type=jnp.float32)
    quad = lax.dot_general(power[...], half_wide, NT, precision=HIGH, preferred_element_type=jnp.float32)
    loads[7].wait()
    loads[8].wait()

    arrive_z(z_copies)
    for origin in range(NZ):
        for t in range(NX):
            row = 64 * (t % 2) + 4 * origin
            main[t // 2, row : row + 2, :] = gathered[origin, 2 * t]
            main[t // 2, row + 2 : row + 4, :] = gathered[origin, 2 * t + 1]
        last = gathered[origin, 8]
        moved = pltpu.roll(last, 64, 1)
        row = 4 * origin
        tail[row : row + 1, :] = last[0:1]
        tail[row + 1 : row + 2, :] = moved[0:1]
        tail[row + 2 : row + 3, :] = last[1:2]
        tail[row + 3 : row + 4, :] = moved[1:2]
    rest = tail[...].T
    lane = iota((16, 128), 1)
    for part in range(2):
        zt[part, 0:128] = main[part].T
        low, high = rest[32 * part : 32 * part + 16], rest[32 * part + 16 : 32 * part + 32]
        zt[part, 128:ANG] = jnp.where(lane < 64, low, pltpu.roll(high, 64, 1))
    for part in range(2):
        one, two = zt[part, 0 : ANG // 2, :], zt[part, ANG // 2 : ANG, :]
        mixed[part, 0] = 0.5 * (one + two)
        mixed[part, 1] = 0.5 * (one - two)

    def build(chunk, pair, target):
        for q in range(NB):
            b = chunk * NB + q
            c, s = cos[b].astype(jnp.float32), sin[b].astype(jnp.float32)
            left, right = slice(q * KT, q * KT + 128), slice(q * KT + 128, q * KT + 256)
            for h in range(2):
                line = pl.ds(4 * b + 2 * pair + h, 1)
                rp, rm, ip, im = mixed[0, 0, line], mixed[0, 1, line], mixed[1, 0, line], mixed[1, 1, line]
                rows = slice(128 * h, 128 * h + 128)
                target[0, rows, left] = (c * rp + s * im).astype(jnp.bfloat16)
                target[0, rows, right] = (s * rm - c * ip).astype(jnp.bfloat16)
                target[1, rows, left] = (c * rm + s * ip).astype(jnp.bfloat16)
                target[1, rows, right] = (s * rp - c * im).astype(jnp.bfloat16)

    def multiply(chunk, source, acc):
        for sign in range(2):
            part = lax.dot_general(matrix[sign, chunk], source[sign], NT, preferred_element_type=jnp.float32)
            if chunk:
                acc[sign] += part
            else:
                acc[sign] = part

    def reduce(pair, acc):
        lane = iota((BLOCK, 128), 1)

        def part(t, carry):
            rows = pl.ds(pl.multiple_of(BLOCK * t, 16), BLOCK)
            tops = [jnp.zeros((BLOCK, 128), jnp.float32)] * 2
            totals = [jnp.ones((BLOCK, 128), jnp.float32)] * 2
            for h in range(2):
                even = acc[0, rows, 128 * h : 128 * h + 128]
                odd = acc[1, rows, 128 * h : 128 * h + 128]
                for half, value in enumerate((even + odd, even - odd)):
                    high = jnp.max(value, axis=1, keepdims=True)
                    low = jnp.sum(jnp.exp(value - high), axis=1, keepdims=True)
                    tops[half] = jnp.where(lane == 2 * pair + h, high, tops[half])
                    totals[half] = jnp.where(lane == 2 * pair + h, low, totals[half])
            for half in range(2):
                score[half, rows, :] += tops[half] + jnp.log(totals[half])
            return carry

        lax.fori_loop(0, NX, part, 0)

    def step(pair, carry):
        build(1, pair, shifted_b)
        multiply(0, shifted_a, acc_a)
        build(0, jnp.minimum(pair + 1, 1), shifted_a)
        multiply(1, shifted_b, acc_a)
        reduce(pair, acc_a)
        return carry

    build(0, 0, shifted_a)
    lax.fori_loop(0, 2, step, 0)

    tiles_of = (HREF // 8, 8, 128)
    flip[...] = jnp.zeros_like(flip)
    values = []
    for t in range(NX):
        shift = quad[8 * t : 8 * t + 8]
        pair = [score[half, BLOCK * t : BLOCK * t + HREF, :].reshape(tiles_of) - shift for half in range(2)]
        values.append(pair)
        high = jnp.maximum(jnp.max(pair[0], axis=0), jnp.max(pair[1], axis=0))
        high = jnp.maximum(high, pltpu.roll(high, 4, 0))
        low = jnp.sum(jnp.exp(pair[0] - high), axis=0) + jnp.sum(jnp.exp(pair[1] - high), axis=0)
        low = low + pltpu.roll(low, 4, 0)
        by_class = high + jnp.log(low)
        flip[64 + LOCAL * t : 64 + LOCAL * (t + 1), :] = by_class[0:LOCAL]
    for half in range(2):
        four = [values[t][half] for t in range(NX)]
        high = jnp.maximum(jnp.maximum(four[0], four[1]), jnp.maximum(four[2], four[3]))
        low = jnp.exp(four[0] - high) + jnp.exp(four[1] - high) + jnp.exp(four[2] - high) + jnp.exp(four[3] - high)
        lines[half * HREF : (half + 1) * HREF, :] = (high + jnp.log(low)).reshape(HREF, 128)
    four = [lines[pl.ds(c, ROT, stride=LOCAL), :] for c in range(LOCAL)]
    high = jnp.maximum(jnp.maximum(four[0], four[1]), jnp.maximum(four[2], four[3]))
    low = jnp.exp(four[0] - high) + jnp.exp(four[1] - high) + jnp.exp(four[2] - high) + jnp.exp(four[3] - high)
    flip[0:ROT, :] = high + jnp.log(low)
    tile = flip[...].T[0:MINE, :]

    tiles[z] = tile
    t_copies = []
    for reach in range(NZ // 2, 0, -1):
        for step in (reach, -reach) if reach < NZ // 2 else (reach,):
            device = x * NZ + ((z + step) & (NZ - 1))
            n = step % NZ
            t_copies.append(send(tiles.at[z], tiles.at[z], tsend.at[n], trecv.at[n], device))
    for copy in t_copies:
        copy.wait_recv()
    values = tiles[...]
    high = jnp.max(values, axis=0)
    rot_lse = high + jnp.log(jnp.sum(jnp.exp(values - high[None]), axis=0))
    lane = iota((MINE, 128), 1)
    masked = jnp.where(lane < ROT, rot_lse, -jnp.inf)
    high = jnp.max(masked, axis=1, keepdims=True)
    norm = high + jnp.log(jnp.sum(jnp.exp(masked - high), axis=1, keepdims=True))
    post[...] = jnp.where(lane < ROT, rot_lse, tile) - norm
    outs[x] = post[...]
    o_copies = []
    for n, device in enumerate(along_x):
        o_copies.append(send(post, outs.at[x], osend.at[n], orecv.at[n], device))
    for copy in o_copies:
        copy.wait_recv()
    line = iota((MINE, 128), 0)
    for t in range(NX):
        live = jnp.zeros((MINE, 128), jnp.int32)
        for p in range(MINE):
            live = jnp.where(line == p, count[MINE * t + p], live)
        value = jnp.where(live > 0, outs[t], 0.0)
        rot_post[MINE * t : MINE * t + MINE, :] = value[:, 0:ROT]
        class_post[MINE * t : MINE * t + MINE, :] = pltpu.roll(value, 64 - LOCAL * x, 1)[:, 0:LOCAL]
    sent = x_copies + [from_left, from_right, onward_a, onward_b, over_left, over_right, over_opposite] + list(z_copies.values()) + t_copies + o_copies
    for copy in sent:
        copy.wait_send()


def body(cos, sin, images, references, ctf_table, noise_inv, defocus_group, micrograph, batch_size):
    vmem, hbm = pl.BlockSpec(memory_space=pltpu.VMEM), pl.BlockSpec(memory_space=pltpu.HBM)
    f32, bf16, i32, dma = jnp.float32, jnp.bfloat16, jnp.int32, pltpu.SemaphoreType.DMA
    operands = (cos, sin, images, references, ctf_table, noise_inv, defocus_group, micrograph, batch_size)
    operands = [pltpu.with_memory_space_constraint(a, pltpu.HBM) for a in operands]
    class_post, rot_post = pl.pallas_call(
        kernel,
        out_shape=(
            jax.ShapeDtypeStruct((16, LOCAL), f32),
            jax.ShapeDtypeStruct((16, ROT), f32),
        ),
        in_specs=[hbm] * 9,
        out_specs=(vmem, vmem),
        scratch_shapes=[
            pltpu.VMEM(cos.shape, bf16),
            pltpu.VMEM(sin.shape, bf16),
            pltpu.VMEM(images.shape, f32),
            pltpu.VMEM(references.shape, bf16),
            pltpu.VMEM(ctf_table.shape, f32),
            pltpu.VMEM(noise_inv.shape, f32),
            pltpu.SMEM((16,), i32),
            pltpu.SMEM((16,), i32),
            pltpu.SMEM((16,), i32),
            pltpu.VMEM((16, CYCLES), f32),
            pltpu.VMEM((16, CYCLES), f32),
            pltpu.VMEM((16, CYCLES), f32),
            pltpu.VMEM((16, 256), f32),
            pltpu.VMEM((2 * CYCLES * LOCAL, 128), f32),
            pltpu.VMEM((2 * CYCLES * LOCAL, 128), f32),
            pltpu.VMEM((NX, 8, 128), f32),
            pltpu.VMEM((NX, 8, 128), f32),
            pltpu.VMEM((2, 128, 128), f32),
            pltpu.VMEM((128, 128), f32),
            pltpu.VMEM((NX, 2, HREF, KT), f32),
            pltpu.VMEM((NZ, 9, 2, 128), f32),
            pltpu.VMEM((16, CYCLES), f32),
            pltpu.VMEM((2, 2, 2 * HREF + 8, 128), f32),
            pltpu.VMEM((2, CHUNKS, NX * BLOCK, NB * KT), bf16),
            pltpu.VMEM((NX * 8, KT), f32),
            pltpu.VMEM((2, ANG, 128), f32),
            pltpu.VMEM((2, 2, ANG // 2, 128), f32),
            pltpu.VMEM((2, 2 * SHIFTS, NB * KT), bf16),
            pltpu.VMEM((2, 2 * SHIFTS, NB * KT), bf16),
            pltpu.VMEM((2, NX * BLOCK, 2 * SHIFTS), f32),
            pltpu.VMEM((2, NX * BLOCK, 128), f32),
            pltpu.VMEM((2 * HREF, 128), f32),
            pltpu.VMEM((128, CYCLES), f32),
            pltpu.VMEM((128, 128), f32),
            pltpu.VMEM((NZ, MINE, 128), f32),
            pltpu.VMEM((MINE, 128), f32),
            pltpu.VMEM((NX, MINE, 128), f32),
            dma((9,)),
            dma((NX - 1,)),
            dma((NX - 1,)),
            dma((7,)),
            dma((7,)),
            dma((NZ,)),
            dma((NZ,)),
            dma((NZ,)),
            dma((NZ,)),
            dma((NX - 1,)),
            dma((NX - 1,)),
        ],
        compiler_params=pltpu.CompilerParams(collective_id=0, has_side_effects=True, vmem_limit_bytes=40 << 20),
        name="expectation",
    )(*operands)
    return class_post, rot_post


def solution(mesh):
    cos, sin = phase_tables()
    in_specs = (P("ptl", "cls"), P("cls", None), P(), P(), P("ptl"), P("ptl"), P("ptl"))
    out_specs = (P("ptl", "cls"), P("ptl", None))
    mapped = jax.shard_map(
        body, mesh=mesh, in_specs=(P(), P()) + in_specs, out_specs=out_specs, check_vma=False
    )

    def run(*args):
        return mapped(jnp.asarray(cos), jnp.asarray(sin), *args)

    return run
```

```python
import math

import jax
import jax.numpy as jnp
import numpy as np
from jax import lax
from jax.experimental import pallas as pl
from jax.experimental.pallas import tpu as pltpu
from jax.sharding import PartitionSpec as P

CYCLES = 32
ANG = 144
ROT = 36
SHIFTS = 128
BOX = 128
STEP = ANG // ROT
NX, NZ = 4, 16
LOCAL = 4
MINE = 4
ALL_C = NX * LOCAL
KT = 256
NB = 9
HALF = ROT // 2
HREF = ROT * LOCAL // 2
CHUNKS = HALF // NB
BLOCK = 80
NEAR = 4
MESH = pl.DeviceIdType.MESH
HIGH = lax.Precision.HIGHEST
NT = (((1,), (1,)), ((), ()))


def phase_tables():
    radius = (np.arange(CYCLES, dtype=np.float64) + 1.0) / BOX
    theta = np.arange(ANG, dtype=np.float64) * (2.0 * math.pi / ANG)
    index = np.arange(SHIFTS)
    shift_x = (index % 16 - 8).astype(np.float64)
    shift_y = (index // 16 - SHIFTS // 32).astype(np.float64)
    along = np.cos(theta)[:, None] * shift_x + np.sin(theta)[:, None] * shift_y
    phase = 2.0 * math.pi * radius[:, None, None] * along[None]

    def order(table):
        table = table.reshape(2, NZ, ROT, STEP, SHIFTS).transpose(2, 4, 0, 1, 3)
        return table.reshape(ROT, SHIFTS, 128)[:HALF].astype(jnp.bfloat16)

    return order(np.cos(phase)), order(np.sin(phase))


def iota(shape, axis):
    return lax.broadcasted_iota(jnp.int32, shape, axis)


def send(src, dst, send_sem, recv_sem, device, **other):
    copy = pltpu.make_async_remote_copy(
        src_ref=src,
        dst_ref=dst,
        send_sem=send_sem,
        recv_sem=recv_sem,
        device_id={"cls": device, **other},
        device_id_type=MESH,
    )
    copy.start()
    return copy


def spread_z(buffer, sends, recvs, x, z):
    copies = {}
    for reach in range(NEAR, 0, -1):
        for step in (reach, -reach):
            device = x * NZ + ((z + step) & (NZ - 1))
            slot = buffer.at[z]
            copies[step] = send(slot, slot, sends.at[step % NZ], recvs.at[step % NZ], device)
    return copies


def relay_z(buffer, sends, recvs, x, z, copies):
    for side, last in ((1, NEAR), (-1, NEAR - 1)):
        copies[side * NEAR].wait_recv()
        slot = buffer.at[(z - side * NEAR) & (NZ - 1)]
        for reach in range(last, 0, -1):
            step = side * (NEAR + reach)
            device = x * NZ + ((z + side * reach) & (NZ - 1))
            copies[step] = send(slot, slot, sends.at[step % NZ], recvs.at[step % NZ], device)


def arrive_z(copies):
    for step, copy in copies.items():
        if abs(step) != NEAR:
            copy.wait_recv()


def kernel(
    cos_hbm, sin_hbm, images_hbm, references_hbm, ctf_hbm, noise_hbm, group_hbm, mic_hbm, count_hbm,
    class_post, rot_post,
    cos, sin, images, references, ctf, noise, group, mic, count,
    rows_c, rows_n, rows_s, padded, split_a, split_b, xs, xr, main, tail, rall, gathered, cross,
    ends, matrix, power, zt, mixed, shifted_a, shifted_b, acc_a, score, lines, half, flip, tiles, post, outs,
    local, xsend, xrecv, rsend, rrecv, zsend, zrecv, tsend, trecv, osend, orecv,
):
    me = lax.axis_index("cls")
    x, z = me >> 4, me & (NZ - 1)
    ptl = lax.axis_index("ptl")
    core = ptl & 1
    sibling = ptl + 1 - 2 * core
    along_x = [((x + step) & (NX - 1)) * NZ + z for step in range(1, NX)]

    barrier = pltpu.get_barrier_semaphore()
    near = [x * NZ + ((z + step) & (NZ - 1)) for step in range(-NEAR, NEAR + 1) if step]
    for device in along_x + near:
        pl.semaphore_signal(barrier, inc=1, device_id={"cls": device}, device_id_type=MESH)
    pl.semaphore_signal(barrier, inc=1, device_id={"ptl": sibling}, device_id_type=MESH)
    pairs = [
        (images_hbm, images), (ctf_hbm, ctf), (noise_hbm, noise), (group_hbm, group), (mic_hbm, mic),
        (count_hbm, count), (references_hbm, references), (cos_hbm, cos), (sin_hbm, sin),
    ]
    loads = [pltpu.make_async_copy(a, b, local.at[n]) for n, (a, b) in enumerate(pairs)]
    for load in loads:
        load.start()

    for load in loads[:6]:
        load.wait()
    for p in range(16):
        rows_c[p : p + 1, :] = ctf[pl.ds(group[p], 1), :]
        rows_n[p : p + 1, :] = noise[pl.ds(mic[p], 1), :]
        rows_s[p : p + 1, :] = jnp.full((1, CYCLES), count[p], jnp.int32).astype(jnp.float32)
    counted = rows_s[...]
    ctf_rows = rows_c[...]
    weight = ctf_rows * rows_n[...] * (counted / (counted + 1.0))
    cross[...] = 0.5 * ctf_rows * weight
    own = (x & 1) * NZ + z
    column = jnp.sum(jnp.where(iota((16, CYCLES), 1) == own, weight, 0.0), axis=1, keepdims=True)
    column = column * jnp.where(x >= 2, -1.0, 1.0)
    padded[...] = jnp.zeros_like(padded)
    tail[...] = jnp.zeros_like(tail)
    score[...] = jnp.zeros_like(score)
    ends[:, :, 2 * HREF :, :] = jnp.zeros((2, 2, 8, 128), jnp.float32)
    padded[:, 0:ANG] = images[...] * column
    full = padded[...]
    row, lane = iota((16, 256), 0) & 3, iota((16, 256), 1) & 3
    rolled = {t: (pltpu.roll(full, t % 256, 1) if t else full) for t in range(-3, 4)}
    for d in range(STEP):
        value = jnp.zeros_like(full)
        for p in range(MINE):
            value = jnp.where((row == p) & (lane == p), rolled[p - d], value)
        for t in range(NX):
            line = jnp.sum(value[4 * t : 4 * t + 4], axis=0, keepdims=True)
            xs[t, d : d + 1, :] = line[:, 0:128]
            xs[t, 4 + d : 5 + d, :] = line[:, 128:256]

    pl.semaphore_wait(barrier, NX + 2 * NEAR)
    x_copies = []
    for n, device in enumerate(along_x):
        x_copies.append(send(xs.at[(x + n + 1) & (NX - 1)], xr.at[x], xsend.at[n], xrecv.at[n], device))
    xr[x] = xs[x]

    loads[6].wait()
    def divide(m, carry):
        for n in range(8):
            base = pl.multiple_of(8 * ANG * m + ANG * n // 128 * 128, 128)
            block = references[:, pl.ds(base, 256)].astype(jnp.float32)
            if n:
                block = pltpu.roll(block, 256 - 16 * n, 1)
            split_a[pl.ds(8 * m + n, LOCAL, stride=2 * CYCLES), :] = block[:, 0:128]
            split_b[pl.ds(8 * m + n, LOCAL, stride=2 * CYCLES), :] = block[:, 128:256]
        return carry

    lax.fori_loop(0, 2 * CYCLES // 8, divide, 0)
    rho = iota((KT, 1), 0)
    repeat = (iota((KT, 2 * CYCLES), 1) == (rho >> 2)).astype(jnp.float32).astype(jnp.bfloat16)
    angle = iota((1, 256), 1)
    keep = ((rho & 3) == (angle & 3)) & (angle < ANG)
    rho = iota((ROT * LOCAL, 1), 0)
    block_of = jnp.where(rho < LOCAL, 0, ROT - (rho >> 2))
    hit = (angle >> 2) == block_of
    total = jnp.zeros((ROT * LOCAL, KT), jnp.float32)
    for c in range(LOCAL):
        cut = slice(2 * CYCLES * c, 2 * CYCLES * (c + 1))
        one = jnp.concatenate([split_a[cut, :], split_b[cut, :]], axis=1).astype(jnp.bfloat16)
        spread = jnp.dot(repeat, one, preferred_element_type=jnp.float32)
        spread = jnp.where(keep, spread, 0.0).astype(jnp.bfloat16)
        pick = (hit & ((rho & 3) == c)).astype(jnp.float32).astype(jnp.bfloat16)
        total += lax.dot_general(pick, spread, NT, preferred_element_type=jnp.float32)
    rall[x, 0] = total[0:HREF]
    rall[x, 1] = total[HREF:]

    left, right = (x + NX - 1) & (NX - 1), (x + 1) & (NX - 1)
    opposite = (x + 2) & (NX - 1)
    part_a, part_b = pl.ds(0, 40), pl.ds(40, HREF - 40)
    slot = rall.at[x, core]
    from_left = send(slot, slot, rsend.at[0], rrecv.at[0], right * NZ + z)
    from_right = send(slot, slot, rsend.at[1], rrecv.at[1], left * NZ + z)

    def place(t):
        low, high = rall[t, 0], rall[t, 1]
        plus, minus = low + high, low - high
        for lanes in range(2):
            cut = slice(128 * lanes, 128 * lanes + 128)
            ends[0, lanes, 0:HREF, :] = plus[:, cut]
            ends[0, lanes, HREF : 2 * HREF, :] = plus[:, cut]
            ends[1, lanes, 0:HREF, :] = -minus[:, cut]
            ends[1, lanes, HREF : 2 * HREF, :] = minus[:, cut]
        rows = pl.ds(pl.multiple_of(BLOCK * t, 16), BLOCK)
        for sign in range(2):
            for chunk in range(CHUNKS):
                for q in range(NB):
                    first = LOCAL * (HALF - NB * chunk - q)
                    for lanes in range(2):
                        at = KT * q + 128 * lanes
                        value = ends[sign, lanes, first : first + BLOCK, :]
                        matrix[sign, chunk, rows, at : at + 128] = value.astype(jnp.bfloat16)
        square = jnp.sum((low * low + high * high).reshape(HREF // 8, 8, KT), axis=0)
        power[pl.ds(pl.multiple_of(8 * t, 8), 8), :] = square + pltpu.roll(square, 4, 0)

    for copy in x_copies:
        copy.wait_recv()
    last = jnp.zeros((STEP, 128), jnp.float32)
    for t in range(NX):
        block = xr[t]
        gathered[z, 2 * t] = block[0:2]
        gathered[z, 2 * t + 1] = block[2:4]
        rest = block[4:8]
        last = last + (pltpu.roll(rest, 16 * t, 1) if t else rest)
    moved = pltpu.roll(last, 64, 1)
    gathered[z, 8, 0:1, :] = last[0:1] + moved[1:2]
    gathered[z, 8, 1:2, :] = last[2:3] + moved[3:4]
    z_copies = spread_z(gathered, zsend, zrecv, x, z)

    from_left.wait_recv()
    slot = rall.at[left, core]
    part = rall.at[left, core, part_a]
    onward_a = send(part, part, rsend.at[2], rrecv.at[2], right * NZ + z)
    over_left = send(slot, slot, rsend.at[4], rrecv.at[4], me, ptl=sibling)
    from_right.wait_recv()
    slot = rall.at[right, core]
    part = rall.at[right, core, part_b]
    onward_b = send(part, part, rsend.at[3], rrecv.at[3], left * NZ + z)
    over_right = send(slot, slot, rsend.at[5], rrecv.at[5], me, ptl=sibling)
    relay_z(gathered, zsend, zrecv, x, z, z_copies)
    place(x)
    onward_a.wait_recv()
    onward_b.wait_recv()
    slot = rall.at[opposite, core]
    over_opposite = send(slot, slot, rsend.at[6], rrecv.at[6], me, ptl=sibling)
    over_left.wait_recv()
    place(left)
    over_right.wait_recv()
    place(right)
    over_opposite.wait_recv()
    place(opposite)

    half[...] = jnp.zeros_like(half)
    half[0:MINE, :] = cross[pl.ds(x * MINE, MINE), :]
    lam = iota((1, KT), 1)
    spread = (iota((CYCLES, KT), 0) == ((lam >> 2) & 31)).astype(jnp.float32)
    half_wide = jnp.dot(half[...], spread, precision=HIGH, preferred_element_type=jnp.float32)
    quad = lax.dot_general(power[...], half_wide, NT, precision=HIGH, preferred_element_type=jnp.float32)
    loads[7].wait()
    loads[8].wait()

    arrive_z(z_copies)
    for origin in range(NZ):
        for t in range(NX):
            row = 64 * (t % 2) + 4 * origin
            main[t // 2, row : row + 2, :] = gathered[origin, 2 * t]
            main[t // 2, row + 2 : row + 4, :] = gathered[origin, 2 * t + 1]
        last = gathered[origin, 8]
        moved = pltpu.roll(last, 64, 1)
        row = 4 * origin
        tail[row : row + 1, :] = last[0:1]
        tail[row + 1 : row + 2, :] = moved[0:1]
        tail[row + 2 : row + 3, :] = last[1:2]
        tail[row + 3 : row + 4, :] = moved[1:2]
    rest = tail[...].T
    lane = iota((16, 128), 1)
    for part in range(2):
        zt[part, 0:128] = main[part].T
        low, high = rest[32 * part : 32 * part + 16], rest[32 * part + 16 : 32 * part + 32]
        zt[part, 128:ANG] = jnp.where(lane < 64, low, pltpu.roll(high, 64, 1))
    for part in range(2):
        one, two = zt[part, 0 : ANG // 2, :], zt[part, ANG // 2 : ANG, :]
        mixed[part, 0] = 0.5 * (one + two)
        mixed[part, 1] = 0.5 * (one - two)

    def build(chunk, pair, target):
        for q in range(NB):
            b = chunk * NB + q
            c, s = cos[b].astype(jnp.float32), sin[b].astype(jnp.float32)
            left, right = slice(q * KT, q * KT + 128), slice(q * KT + 128, q * KT + 256)
            for h in range(2):
                line = pl.ds(4 * b + 2 * pair + h, 1)
                rp, rm, ip, im = mixed[0, 0, line], mixed[0, 1, line], mixed[1, 0, line], mixed[1, 1, line]
                rows = slice(128 * h, 128 * h + 128)
                target[0, rows, left] = (c * rp + s * im).astype(jnp.bfloat16)
                target[0, rows, right] = (s * rm - c * ip).astype(jnp.bfloat16)
                target[1, rows, left] = (c * rm + s * ip).astype(jnp.bfloat16)
                target[1, rows, right] = (s * rp - c * im).astype(jnp.bfloat16)

    def multiply(chunk, source, acc):
        for sign in range(2):
            part = lax.dot_general(matrix[sign, chunk], source[sign], NT, preferred_element_type=jnp.float32)
            if chunk:
                acc[sign] += part
            else:
                acc[sign] = part

    def reduce(pair, acc):
        lane = iota((BLOCK, 128), 1)

        def part(t, carry):
            rows = pl.ds(pl.multiple_of(BLOCK * t, 16), BLOCK)
            tops = [jnp.zeros((BLOCK, 128), jnp.float32)] * 2
            totals = [jnp.ones((BLOCK, 128), jnp.float32)] * 2
            for h in range(2):
                even = acc[0, rows, 128 * h : 128 * h + 128]
                odd = acc[1, rows, 128 * h : 128 * h + 128]
                for half, value in enumerate((even + odd, even - odd)):
                    high = jnp.max(value, axis=1, keepdims=True)
                    low = jnp.sum(jnp.exp(value - high), axis=1, keepdims=True)
                    tops[half] = jnp.where(lane == 2 * pair + h, high, tops[half])
                    totals[half] = jnp.where(lane == 2 * pair + h, low, totals[half])
            for half in range(2):
                score[half, rows, :] += tops[half] + jnp.log(totals[half])
            return carry

        lax.fori_loop(0, NX, part, 0)

    def step(pair, carry):
        build(1, pair, shifted_b)
        multiply(0, shifted_a, acc_a)
        build(0, jnp.minimum(pair + 1, 1), shifted_a)
        multiply(1, shifted_b, acc_a)
        reduce(pair, acc_a)
        return carry

    build(0, 0, shifted_a)
    lax.fori_loop(0, 2, step, 0)

    tiles_of = (HREF // 8, 8, 128)
    flip[...] = jnp.zeros_like(flip)
    values = []
    for t in range(NX):
        shift = quad[8 * t : 8 * t + 8]
        pair = [score[half, BLOCK * t : BLOCK * t + HREF, :].reshape(tiles_of) - shift for half in range(2)]
        values.append(pair)
        high = jnp.maximum(jnp.max(pair[0], axis=0), jnp.max(pair[1], axis=0))
        high = jnp.maximum(high, pltpu.roll(high, 4, 0))
        low = jnp.sum(jnp.exp(pair[0] - high), axis=0) + jnp.sum(jnp.exp(pair[1] - high), axis=0)
        low = low + pltpu.roll(low, 4, 0)
        by_class = high + jnp.log(low)
        flip[64 + LOCAL * t : 64 + LOCAL * (t + 1), :] = by_class[0:LOCAL]
    for half in range(2):
        four = [values[t][half] for t in range(NX)]
        high = jnp.maximum(jnp.maximum(four[0], four[1]), jnp.maximum(four[2], four[3]))
        low = jnp.exp(four[0] - high) + jnp.exp(four[1] - high) + jnp.exp(four[2] - high) + jnp.exp(four[3] - high)
        lines[half * HREF : (half + 1) * HREF, :] = (high + jnp.log(low)).reshape(HREF, 128)
    four = [lines[pl.ds(c, ROT, stride=LOCAL), :] for c in range(LOCAL)]
    high = jnp.maximum(jnp.maximum(four[0], four[1]), jnp.maximum(four[2], four[3]))
    low = jnp.exp(four[0] - high) + jnp.exp(four[1] - high) + jnp.exp(four[2] - high) + jnp.exp(four[3] - high)
    flip[0:ROT, :] = high + jnp.log(low)
    tile = flip[...].T[0:MINE, :]

    tiles[z] = tile
    t_copies = []
    for reach in range(NZ // 2, 0, -1):
        for step in (reach, -reach) if reach < NZ // 2 else (reach,):
            device = x * NZ + ((z + step) & (NZ - 1))
            n = step % NZ
            t_copies.append(send(tiles.at[z], tiles.at[z], tsend.at[n], trecv.at[n], device))
    for copy in t_copies:
        copy.wait_recv()
    values = tiles[...]
    high = jnp.max(values, axis=0)
    rot_lse = high + jnp.log(jnp.sum(jnp.exp(values - high[None]), axis=0))
    lane = iota((MINE, 128), 1)
    masked = jnp.where(lane < ROT, rot_lse, -jnp.inf)
    high = jnp.max(masked, axis=1, keepdims=True)
    norm = high + jnp.log(jnp.sum(jnp.exp(masked - high), axis=1, keepdims=True))
    post[...] = jnp.where(lane < ROT, rot_lse, tile) - norm
    outs[x] = post[...]
    o_copies = []
    for n, device in enumerate(along_x):
        o_copies.append(send(post, outs.at[x], osend.at[n], orecv.at[n], device))
    for copy in o_copies:
        copy.wait_recv()
    line = iota((MINE, 128), 0)
    for t in range(NX):
        live = jnp.zeros((MINE, 128), jnp.int32)
        for p in range(MINE):
            live = jnp.where(line == p, count[MINE * t + p], live)
        value = jnp.where(live > 0, outs[t], 0.0)
        rot_post[MINE * t : MINE * t + MINE, :] = value[:, 0:ROT]
        class_post[MINE * t : MINE * t + MINE, :] = pltpu.roll(value, 64 - LOCAL * x, 1)[:, 0:LOCAL]
    sent = x_copies + [from_left, from_right, onward_a, onward_b, over_left, over_right, over_opposite] + list(z_copies.values()) + t_copies + o_copies
    for copy in sent:
        copy.wait_send()


def body(cos, sin, images, references, ctf_table, noise_inv, defocus_group, micrograph, batch_size):
    vmem, hbm = pl.BlockSpec(memory_space=pltpu.VMEM), pl.BlockSpec(memory_space=pltpu.HBM)
    f32, bf16, i32, dma = jnp.float32, jnp.bfloat16, jnp.int32, pltpu.SemaphoreType.DMA
    operands = (cos, sin, images, references, ctf_table, noise_inv, defocus_group, micrograph, batch_size)
    operands = [pltpu.with_memory_space_constraint(a, pltpu.HBM) for a in operands]
    class_post, rot_post = pl.pallas_call(
        kernel,
        out_shape=(
            jax.ShapeDtypeStruct((16, LOCAL), f32),
            jax.ShapeDtypeStruct((16, ROT), f32),
        ),
        in_specs=[hbm] * 9,
        out_specs=(vmem, vmem),
        scratch_shapes=[
            pltpu.VMEM(cos.shape, bf16),
            pltpu.VMEM(sin.shape, bf16),
            pltpu.VMEM(images.shape, f32),
            pltpu.VMEM(references.shape, bf16),
            pltpu.VMEM(ctf_table.shape, f32),
            pltpu.VMEM(noise_inv.shape, f32),
            pltpu.SMEM((16,), i32),
            pltpu.SMEM((16,), i32),
            pltpu.SMEM((16,), i32),
            pltpu.VMEM((16, CYCLES), f32),
            pltpu.VMEM((16, CYCLES), f32),
            pltpu.VMEM((16, CYCLES), f32),
            pltpu.VMEM((16, 256), f32),
            pltpu.VMEM((2 * CYCLES * LOCAL, 128), f32),
            pltpu.VMEM((2 * CYCLES * LOCAL, 128), f32),
            pltpu.VMEM((NX, 8, 128), f32),
            pltpu.VMEM((NX, 8, 128), f32),
            pltpu.VMEM((2, 128, 128), f32),
            pltpu.VMEM((128, 128), f32),
            pltpu.VMEM((NX, 2, HREF, KT), f32),
            pltpu.VMEM((NZ, 9, 2, 128), f32),
            pltpu.VMEM((16, CYCLES), f32),
            pltpu.VMEM((2, 2, 2 * HREF + 8, 128), f32),
            pltpu.VMEM((2, CHUNKS, NX * BLOCK, NB * KT), bf16),
            pltpu.VMEM((NX * 8, KT), f32),
            pltpu.VMEM((2, ANG, 128), f32),
            pltpu.VMEM((2, 2, ANG // 2, 128), f32),
            pltpu.VMEM((2, 2 * SHIFTS, NB * KT), bf16),
            pltpu.VMEM((2, 2 * SHIFTS, NB * KT), bf16),
            pltpu.VMEM((2, NX * BLOCK, 2 * SHIFTS), f32),
            pltpu.VMEM((2, NX * BLOCK, 128), f32),
            pltpu.VMEM((2 * HREF, 128), f32),
            pltpu.VMEM((128, CYCLES), f32),
            pltpu.VMEM((128, 128), f32),
            pltpu.VMEM((NZ, MINE, 128), f32),
            pltpu.VMEM((MINE, 128), f32),
            pltpu.VMEM((NX, MINE, 128), f32),
            dma((9,)),
            dma((NX - 1,)),
            dma((NX - 1,)),
            dma((7,)),
            dma((7,)),
            dma((NZ,)),
            dma((NZ,)),
            dma((NZ,)),
            dma((NZ,)),
            dma((NX - 1,)),
            dma((NX - 1,)),
        ],
        compiler_params=pltpu.CompilerParams(collective_id=0, has_side_effects=True, vmem_limit_bytes=40 << 20),
        name="expectation",
    )(*operands)
    return class_post, rot_post


def solution(mesh):
    cos, sin = phase_tables()
    in_specs = (P("ptl", "cls"), P("cls", None), P(), P(), P("ptl"), P("ptl"), P("ptl"))
    out_specs = (P("ptl", "cls"), P("ptl", None))
    mapped = jax.shard_map(
        body, mesh=mesh, in_specs=(P(), P()) + in_specs, out_specs=out_specs, check_vma=False
    )

    def run(*args):
        return mapped(jnp.asarray(cos), jnp.asarray(sin), *args)

    return run
```

```python
import math

import jax
import jax.numpy as jnp
import numpy as np
from jax import lax
from jax.experimental import pallas as pl
from jax.experimental.pallas import tpu as pltpu
from jax.sharding import PartitionSpec as P

CYCLES = 32
ANG = 144
ROT = 36
SHIFTS = 128
BOX = 128
STEP = ANG // ROT
NX, NZ = 4, 16
LOCAL = 4
MINE = 4
ALL_C = NX * LOCAL
KT = 256
HALF = ROT // 2
HREF = ROT * LOCAL // 2
BLOCK = 80
NEAR = 4
MESH = pl.DeviceIdType.MESH
HIGH = lax.Precision.HIGHEST
NT = (((1,), (1,)), ((), ()))


def phase_tables():
    radius = (np.arange(CYCLES, dtype=np.float64) + 1.0) / BOX
    theta = np.arange(ANG, dtype=np.float64) * (2.0 * math.pi / ANG)
    index = np.arange(SHIFTS)
    shift_x = (index % 16 - 8).astype(np.float64)
    shift_y = (index // 16 - SHIFTS // 32).astype(np.float64)
    along = np.cos(theta)[:, None] * shift_x + np.sin(theta)[:, None] * shift_y
    phase = 2.0 * math.pi * radius[:, None, None] * along[None]

    def order(table):
        table = table.reshape(2, NZ, ROT, STEP, SHIFTS).transpose(2, 4, 1, 0, 3)
        return table.reshape(ROT, SHIFTS, 128)[:HALF].astype(jnp.bfloat16)

    return order(np.cos(phase)), order(np.sin(phase))


def iota(shape, axis):
    return lax.broadcasted_iota(jnp.int32, shape, axis)


def send(src, dst, send_sem, recv_sem, device, **other):
    copy = pltpu.make_async_remote_copy(
        src_ref=src,
        dst_ref=dst,
        send_sem=send_sem,
        recv_sem=recv_sem,
        device_id={"cls": device, **other},
        device_id_type=MESH,
    )
    copy.start()
    return copy


def spread_z(buffer, sends, recvs, x, z):
    copies = {}
    for reach in range(NEAR, 0, -1):
        for step in (reach, -reach):
            device = x * NZ + ((z + step) & (NZ - 1))
            slot = buffer.at[z]
            copies[step] = send(slot, slot, sends.at[step % NZ], recvs.at[step % NZ], device)
    return copies


def relay_z(buffer, sends, recvs, x, z, copies):
    for side, last in ((1, NEAR), (-1, NEAR - 1)):
        copies[side * NEAR].wait_recv()
        slot = buffer.at[(z - side * NEAR) & (NZ - 1)]
        for reach in range(last, 0, -1):
            step = side * (NEAR + reach)
            device = x * NZ + ((z + side * reach) & (NZ - 1))
            copies[step] = send(slot, slot, sends.at[step % NZ], recvs.at[step % NZ], device)


def arrive_z(copies, nearer):
    for step, copy in copies.items():
        if abs(step) != NEAR and (abs(step) < NEAR) == nearer:
            copy.wait_recv()


def kernel(
    cos_hbm, sin_hbm, images_hbm, references_hbm, ctf_hbm, noise_hbm, group_hbm, mic_hbm, count_hbm,
    class_post, rot_post,
    cos, sin, images, references, ctf, noise, group, mic, count,
    rows_c, rows_n, rows_s, padded, split_a, split_b, xs, xr, main, tail, ahead, rall, gathered, cross,
    ends, matrix, power, zt, mixed, shifted_a, shifted_b, acc_a, acc_b, table_c, table_s, score, lines, half, flip, tiles, post, outs,
    local, xsend, xrecv, rsend, rrecv, zsend, zrecv, tsend, trecv, osend, orecv,
):
    me = lax.axis_index("cls")
    x, z = me >> 4, me & (NZ - 1)
    ptl = lax.axis_index("ptl")
    core = ptl & 1
    sibling = ptl + 1 - 2 * core
    along_x = [((x + step) & (NX - 1)) * NZ + z for step in range(1, NX)]

    barrier = pltpu.get_barrier_semaphore()
    near = [x * NZ + ((z + step) & (NZ - 1)) for step in range(-NEAR, NEAR + 1) if step]
    for device in along_x + near:
        pl.semaphore_signal(barrier, inc=1, device_id={"cls": device}, device_id_type=MESH)
    pl.semaphore_signal(barrier, inc=1, device_id={"ptl": sibling}, device_id_type=MESH)
    pairs = [
        (images_hbm, images), (ctf_hbm, ctf), (noise_hbm, noise), (group_hbm, group), (mic_hbm, mic),
        (count_hbm, count), (references_hbm, references), (cos_hbm, cos), (sin_hbm, sin),
    ]
    loads = [pltpu.make_async_copy(a, b, local.at[n]) for n, (a, b) in enumerate(pairs)]
    for load in loads:
        load.start()

    for load in loads[:6]:
        load.wait()
    for p in range(16):
        rows_c[p : p + 1, :] = ctf[pl.ds(group[p], 1), :]
        rows_n[p : p + 1, :] = noise[pl.ds(mic[p], 1), :]
        rows_s[p : p + 1, :] = jnp.full((1, CYCLES), count[p], jnp.int32).astype(jnp.float32)
    counted = rows_s[...]
    ctf_rows = rows_c[...]
    weight = ctf_rows * rows_n[...] * (counted / (counted + 1.0))
    cross[...] = 0.5 * ctf_rows * weight
    own = (x & 1) * NZ + z
    column = jnp.sum(jnp.where(iota((16, CYCLES), 1) == own, weight, 0.0), axis=1, keepdims=True)
    column = column * jnp.where(x >= 2, -1.0, 1.0)
    padded[...] = jnp.zeros_like(padded)
    tail[...] = jnp.zeros_like(tail)
    score[...] = jnp.zeros_like(score)
    ends[:, :, 2 * HREF :, :] = jnp.zeros((2, 2, 8, 128), jnp.float32)
    padded[:, 0:ANG] = images[...] * column
    full = padded[...]
    row, lane = iota((16, 256), 0) & 3, iota((16, 256), 1) & 3
    rolled = {t: (pltpu.roll(full, t % 256, 1) if t else full) for t in range(-3, 4)}
    for d in range(STEP):
        value = jnp.zeros_like(full)
        for p in range(MINE):
            value = jnp.where((row == p) & (lane == p), rolled[p - d], value)
        for t in range(NX):
            line = jnp.sum(value[4 * t : 4 * t + 4], axis=0, keepdims=True)
            xs[t, d : d + 1, :] = line[:, 0:128]
            xs[t, 4 + d : 5 + d, :] = line[:, 128:256]

    pl.semaphore_wait(barrier, NX + 2 * NEAR)
    x_copies = []
    for n, device in enumerate(along_x):
        x_copies.append(send(xs.at[(x + n + 1) & (NX - 1)], xr.at[x], xsend.at[n], xrecv.at[n], device))
    xr[x] = xs[x]

    loads[6].wait()
    def divide(m, carry):
        for n in range(8):
            base = pl.multiple_of(8 * ANG * m + ANG * n // 128 * 128, 128)
            block = references[:, pl.ds(base, 256)].astype(jnp.float32)
            if n:
                block = pltpu.roll(block, 256 - 16 * n, 1)
            split_a[pl.ds(8 * m + n, LOCAL, stride=2 * CYCLES), :] = block[:, 0:128]
            split_b[pl.ds(8 * m + n, LOCAL, stride=2 * CYCLES), :] = block[:, 128:256]
        return carry

    lax.fori_loop(0, 2 * CYCLES // 8, divide, 0)
    rho = iota((KT, 1), 0)
    source = (z - 4 + ((rho >> 7) << 3) + ((rho >> 3) & 7)) & (NZ - 1)
    kappa = (((rho >> 6) & 1) << 5) + (((rho >> 2) & 1) << 4) + source
    repeat = (iota((KT, 2 * CYCLES), 1) == kappa).astype(jnp.float32).astype(jnp.bfloat16)
    angle = iota((1, 256), 1)
    keep = ((rho & 3) == (angle & 3)) & (angle < ANG)
    rho = iota((ROT * LOCAL, 1), 0)
    block_of = jnp.where(rho < LOCAL, 0, ROT - (rho >> 2))
    hit = (angle >> 2) == block_of
    total = jnp.zeros((ROT * LOCAL, KT), jnp.float32)
    for c in range(LOCAL):
        cut = slice(2 * CYCLES * c, 2 * CYCLES * (c + 1))
        one = jnp.concatenate([split_a[cut, :], split_b[cut, :]], axis=1).astype(jnp.bfloat16)
        spread = jnp.dot(repeat, one, preferred_element_type=jnp.float32)
        spread = jnp.where(keep, spread, 0.0).astype(jnp.bfloat16)
        pick = (hit & ((rho & 3) == c)).astype(jnp.float32).astype(jnp.bfloat16)
        total += lax.dot_general(pick, spread, NT, preferred_element_type=jnp.float32)
    rall[x, 0] = total[0:HREF]
    rall[x, 1] = total[HREF:]

    left, right = (x + NX - 1) & (NX - 1), (x + 1) & (NX - 1)
    opposite = (x + 2) & (NX - 1)
    part_a, part_b = pl.ds(0, 40), pl.ds(40, HREF - 40)
    slot = rall.at[x, core]
    from_left = send(slot, slot, rsend.at[0], rrecv.at[0], right * NZ + z)
    from_right = send(slot, slot, rsend.at[1], rrecv.at[1], left * NZ + z)

    def place(t):
        low, high = rall[t, 0], rall[t, 1]
        plus, minus = low + high, low - high
        for lanes in range(2):
            cut = slice(128 * lanes, 128 * lanes + 128)
            ends[0, lanes, 0:HREF, :] = plus[:, cut]
            ends[0, lanes, HREF : 2 * HREF, :] = plus[:, cut]
            ends[1, lanes, 0:HREF, :] = -minus[:, cut]
            ends[1, lanes, HREF : 2 * HREF, :] = minus[:, cut]
        rows = pl.ds(pl.multiple_of(BLOCK * t, 16), BLOCK)
        for sign in range(2):
            for b in range(HALF):
                first = LOCAL * (HALF - b)
                for lanes in range(2):
                    value = ends[sign, lanes, first : first + BLOCK, :]
                    matrix[sign, lanes, rows, 128 * b : 128 * b + 128] = value.astype(jnp.bfloat16)
        square = jnp.sum((low * low + high * high).reshape(HREF // 8, 8, KT), axis=0)
        power[pl.ds(pl.multiple_of(8 * t, 8), 8), :] = square + pltpu.roll(square, 4, 0)

    for copy in x_copies:
        copy.wait_recv()
    for part in range(2):
        last = jnp.zeros((1, 128), jnp.float32)
        for low in range(2):
            t = 2 * part + low
            block = xr[t]
            gathered[z, 2 * t] = block[0:2]
            gathered[z, 2 * t + 1] = block[2:4]
            for d in range(STEP):
                at = 16 * (STEP * low + d)
                rest = block[4 + d : 5 + d]
                last = last + (pltpu.roll(rest, at, 1) if at else rest)
        gathered[z, 8, part : part + 1, :] = last
    z_copies = spread_z(gathered, zsend, zrecv, x, z)

    loads[7].wait()
    loads[8].wait()
    first_lanes = iota((128, 128), 1) < 64
    turn = ((20 - z) * 8) & 127

    def arrange(b, carry):
        for table, rolled_table, sign in ((cos, table_c, -1.0), (sin, table_s, 1.0)):
            value = pltpu.roll(table[b].astype(jnp.float32), turn, 1)
            moved = pltpu.roll(value, 64, 1)
            rolled_table[0, b] = jnp.where(first_lanes, value, sign * moved)
            rolled_table[1, b] = jnp.where(first_lanes, moved, sign * value)
        return carry

    lax.fori_loop(0, HALF, arrange, 0)

    from_left.wait_recv()
    slot = rall.at[left, core]
    part = rall.at[left, core, part_a]
    onward_a = send(part, part, rsend.at[2], rrecv.at[2], right * NZ + z)
    over_left = send(slot, slot, rsend.at[4], rrecv.at[4], me, ptl=sibling)
    from_right.wait_recv()
    slot = rall.at[right, core]
    part = rall.at[right, core, part_b]
    onward_b = send(part, part, rsend.at[3], rrecv.at[3], left * NZ + z)
    over_right = send(slot, slot, rsend.at[5], rrecv.at[5], me, ptl=sibling)
    relay_z(gathered, zsend, zrecv, x, z, z_copies)
    place(x)
    onward_a.wait_recv()
    onward_b.wait_recv()
    slot = rall.at[opposite, core]
    over_opposite = send(slot, slot, rsend.at[6], rrecv.at[6], me, ptl=sibling)
    over_left.wait_recv()
    place(left)
    over_right.wait_recv()
    place(right)
    over_opposite.wait_recv()
    place(opposite)

    half[...] = jnp.zeros_like(half)
    half[0:MINE, :] = cross[pl.ds(x * MINE, MINE), :]
    lam = iota((1, KT), 1)
    cycle = (((lam >> 2) & 1) << 4) + ((z - 4 + ((lam >> 7) << 3) + ((lam >> 3) & 7)) & (NZ - 1))
    spread = (iota((CYCLES, KT), 0) == cycle).astype(jnp.float32)
    half_wide = jnp.dot(half[...], spread, precision=HIGH, preferred_element_type=jnp.float32)
    quad = lax.dot_general(power[...], half_wide, NT, precision=HIGH, preferred_element_type=jnp.float32)
    def unpack(far):
        for zr in range(8):
            origin = (z - 4 + 8 * far + zr) & (NZ - 1)
            for t in range(NX):
                row = 64 * (t // 2) + 8 * zr + 4 * (t % 2)
                main[row : row + 2, :] = gathered[origin, 2 * t]
                main[row + 2 : row + 4, :] = gathered[origin, 2 * t + 1]
            last = gathered[origin, 8]
            ahead[zr : zr + 1, :] = last[0:1]
            ahead[8 + zr : 9 + zr, :] = last[1:2]
        last = ahead[...]
        for n in range(8):
            moved = pltpu.roll(last, 128 - 16 * n, 1) if n else last
            tail[pl.ds(n, 8, stride=8), :] = moved[0:8]
            tail[pl.ds(64 + n, 8, stride=8), :] = moved[8:16]
        zt[0:128] = main[...].T
        zt[128:ANG] = tail[...].T[0:16]
        one, two = zt[0 : ANG // 2, :], zt[ANG // 2 : ANG, :]
        plus, minus = 0.5 * (one + two), 0.5 * (one - two)
        mixed[0] = plus
        mixed[1] = minus
        mixed[2] = pltpu.roll(plus, 64, 1)
        mixed[3] = pltpu.roll(minus, 64, 1)

    def build(far, pair, target):
        for b in range(HALF):
            c, s = table_c[far, b], table_s[far, b]
            lanes = slice(128 * b, 128 * b + 128)
            for h in range(2):
                line = slice(4 * b + 2 * pair + h, 4 * b + 2 * pair + h + 1)
                rows = slice(128 * h, 128 * h + 128)
                target[0, rows, lanes] = (c * mixed[0, line] + s * mixed[3, line]).astype(jnp.bfloat16)
                target[1, rows, lanes] = (c * mixed[1, line] + s * mixed[2, line]).astype(jnp.bfloat16)

    def multiply(far, source, acc):
        for sign in range(2):
            part = lax.dot_general(matrix[sign, far], source[sign], NT, preferred_element_type=jnp.float32)
            if far:
                acc[sign] += part
            else:
                acc[sign] = part

    def reduce(pair, acc):
        lane = iota((BLOCK, 128), 1)

        def part(t, carry):
            rows = pl.ds(pl.multiple_of(BLOCK * t, 16), BLOCK)
            tops = [jnp.zeros((BLOCK, 128), jnp.float32)] * 2
            totals = [jnp.ones((BLOCK, 128), jnp.float32)] * 2
            for h in range(2):
                even = acc[0, rows, 128 * h : 128 * h + 128]
                odd = acc[1, rows, 128 * h : 128 * h + 128]
                for half, value in enumerate((even + odd, even - odd)):
                    high = jnp.max(value, axis=1, keepdims=True)
                    low = jnp.sum(jnp.exp(value - high), axis=1, keepdims=True)
                    tops[half] = jnp.where(lane == 2 * pair + h, high, tops[half])
                    totals[half] = jnp.where(lane == 2 * pair + h, low, totals[half])
            for half in range(2):
                score[half, rows, :] += tops[half] + jnp.log(totals[half])
            return carry

        lax.fori_loop(0, NX, part, 0)

    for far in range(2):
        arrive_z(z_copies, far == 0)
        unpack(far)
        build(far, 0, shifted_a)
        build(far, 1, shifted_b)
        multiply(far, shifted_a, acc_a)
        multiply(far, shifted_b, acc_b)
    reduce(0, acc_a)
    reduce(1, acc_b)

    tiles_of = (HREF // 8, 8, 128)
    flip[...] = jnp.zeros_like(flip)
    values = []
    for t in range(NX):
        shift = quad[8 * t : 8 * t + 8]
        pair = [score[half, BLOCK * t : BLOCK * t + HREF, :].reshape(tiles_of) - shift for half in range(2)]
        values.append(pair)
        high = jnp.maximum(jnp.max(pair[0], axis=0), jnp.max(pair[1], axis=0))
        high = jnp.maximum(high, pltpu.roll(high, 4, 0))
        low = jnp.sum(jnp.exp(pair[0] - high), axis=0) + jnp.sum(jnp.exp(pair[1] - high), axis=0)
        low = low + pltpu.roll(low, 4, 0)
        by_class = high + jnp.log(low)
        flip[64 + LOCAL * t : 64 + LOCAL * (t + 1), :] = by_class[0:LOCAL]
    for half in range(2):
        four = [values[t][half] for t in range(NX)]
        high = jnp.maximum(jnp.maximum(four[0], four[1]), jnp.maximum(four[2], four[3]))
        low = jnp.exp(four[0] - high) + jnp.exp(four[1] - high) + jnp.exp(four[2] - high) + jnp.exp(four[3] - high)
        lines[half * HREF : (half + 1) * HREF, :] = (high + jnp.log(low)).reshape(HREF, 128)
    four = [lines[pl.ds(c, ROT, stride=LOCAL), :] for c in range(LOCAL)]
    high = jnp.maximum(jnp.maximum(four[0], four[1]), jnp.maximum(four[2], four[3]))
    low = jnp.exp(four[0] - high) + jnp.exp(four[1] - high) + jnp.exp(four[2] - high) + jnp.exp(four[3] - high)
    flip[0:ROT, :] = high + jnp.log(low)
    tile = flip[...].T[0:MINE, :]

    tiles[z] = tile
    t_copies = []
    for reach in range(NZ // 2, 0, -1):
        for step in (reach, -reach) if reach < NZ // 2 else (reach,):
            device = x * NZ + ((z + step) & (NZ - 1))
            n = step % NZ
            t_copies.append(send(tiles.at[z], tiles.at[z], tsend.at[n], trecv.at[n], device))
    for copy in t_copies:
        copy.wait_recv()
    values = tiles[...]
    high = jnp.max(values, axis=0)
    rot_lse = high + jnp.log(jnp.sum(jnp.exp(values - high[None]), axis=0))
    lane = iota((MINE, 128), 1)
    masked = jnp.where(lane < ROT, rot_lse, -jnp.inf)
    high = jnp.max(masked, axis=1, keepdims=True)
    norm = high + jnp.log(jnp.sum(jnp.exp(masked - high), axis=1, keepdims=True))
    post[...] = jnp.where(lane < ROT, rot_lse, tile) - norm
    outs[x] = post[...]
    o_copies = []
    for n, device in enumerate(along_x):
        o_copies.append(send(post, outs.at[x], osend.at[n], orecv.at[n], device))
    for copy in o_copies:
        copy.wait_recv()
    line = iota((MINE, 128), 0)
    for t in range(NX):
        live = jnp.zeros((MINE, 128), jnp.int32)
        for p in range(MINE):
            live = jnp.where(line == p, count[MINE * t + p], live)
        value = jnp.where(live > 0, outs[t], 0.0)
        rot_post[MINE * t : MINE * t + MINE, :] = value[:, 0:ROT]
        class_post[MINE * t : MINE * t + MINE, :] = pltpu.roll(value, 64 - LOCAL * x, 1)[:, 0:LOCAL]
    sent = x_copies + [from_left, from_right, onward_a, onward_b, over_left, over_right, over_opposite] + list(z_copies.values()) + t_copies + o_copies
    for copy in sent:
        copy.wait_send()


def body(cos, sin, images, references, ctf_table, noise_inv, defocus_group, micrograph, batch_size):
    vmem, hbm = pl.BlockSpec(memory_space=pltpu.VMEM), pl.BlockSpec(memory_space=pltpu.HBM)
    f32, bf16, i32, dma = jnp.float32, jnp.bfloat16, jnp.int32, pltpu.SemaphoreType.DMA
    operands = (cos, sin, images, references, ctf_table, noise_inv, defocus_group, micrograph, batch_size)
    operands = [pltpu.with_memory_space_constraint(a, pltpu.HBM) for a in operands]
    class_post, rot_post = pl.pallas_call(
        kernel,
        out_shape=(
            jax.ShapeDtypeStruct((16, LOCAL), f32),
            jax.ShapeDtypeStruct((16, ROT), f32),
        ),
        in_specs=[hbm] * 9,
        out_specs=(vmem, vmem),
        scratch_shapes=[
            pltpu.VMEM(cos.shape, bf16),
            pltpu.VMEM(sin.shape, bf16),
            pltpu.VMEM(images.shape, f32),
            pltpu.VMEM(references.shape, bf16),
            pltpu.VMEM(ctf_table.shape, f32),
            pltpu.VMEM(noise_inv.shape, f32),
            pltpu.SMEM((16,), i32),
            pltpu.SMEM((16,), i32),
            pltpu.SMEM((16,), i32),
            pltpu.VMEM((16, CYCLES), f32),
            pltpu.VMEM((16, CYCLES), f32),
            pltpu.VMEM((16, CYCLES), f32),
            pltpu.VMEM((16, 256), f32),
            pltpu.VMEM((2 * CYCLES * LOCAL, 128), f32),
            pltpu.VMEM((2 * CYCLES * LOCAL, 128), f32),
            pltpu.VMEM((NX, 8, 128), f32),
            pltpu.VMEM((NX, 8, 128), f32),
            pltpu.VMEM((128, 128), f32),
            pltpu.VMEM((128, 128), f32),
            pltpu.VMEM((16, 128), f32),
            pltpu.VMEM((NX, 2, HREF, KT), f32),
            pltpu.VMEM((NZ, 9, 2, 128), f32),
            pltpu.VMEM((16, CYCLES), f32),
            pltpu.VMEM((2, 2, 2 * HREF + 8, 128), f32),
            pltpu.VMEM((2, 2, NX * BLOCK, HALF * 128), bf16),
            pltpu.VMEM((NX * 8, KT), f32),
            pltpu.VMEM((ANG, 128), f32),
            pltpu.VMEM((4, ANG // 2, 128), f32),
            pltpu.VMEM((2, 2 * SHIFTS, HALF * 128), bf16),
            pltpu.VMEM((2, 2 * SHIFTS, HALF * 128), bf16),
            pltpu.VMEM((2, NX * BLOCK, 2 * SHIFTS), f32),
            pltpu.VMEM((2, NX * BLOCK, 2 * SHIFTS), f32),
            pltpu.VMEM((2, HALF, SHIFTS, 128), f32),
            pltpu.VMEM((2, HALF, SHIFTS, 128), f32),
            pltpu.VMEM((2, NX * BLOCK, 128), f32),
            pltpu.VMEM((2 * HREF, 128), f32),
            pltpu.VMEM((128, CYCLES), f32),
            pltpu.VMEM((128, 128), f32),
            pltpu.VMEM((NZ, MINE, 128), f32),
            pltpu.VMEM((MINE, 128), f32),
            pltpu.VMEM((NX, MINE, 128), f32),
            dma((9,)),
            dma((NX - 1,)),
            dma((NX - 1,)),
            dma((7,)),
            dma((7,)),
            dma((NZ,)),
            dma((NZ,)),
            dma((NZ,)),
            dma((NZ,)),
            dma((NX - 1,)),
            dma((NX - 1,)),
        ],
        compiler_params=pltpu.CompilerParams(collective_id=0, has_side_effects=True, vmem_limit_bytes=40 << 20),
        name="expectation",
    )(*operands)
    return class_post, rot_post


def solution(mesh):
    cos, sin = phase_tables()
    in_specs = (P("ptl", "cls"), P("cls", None), P(), P(), P("ptl"), P("ptl"), P("ptl"))
    out_specs = (P("ptl", "cls"), P("ptl", None))
    mapped = jax.shard_map(
        body, mesh=mesh, in_specs=(P(), P()) + in_specs, out_specs=out_specs, check_vma=False
    )

    def run(*args):
        return mapped(jnp.asarray(cos), jnp.asarray(sin), *args)

    return run
```

```python
import math

import jax
import jax.numpy as jnp
import numpy as np
from jax import lax
from jax.experimental import pallas as pl
from jax.experimental.pallas import tpu as pltpu
from jax.sharding import PartitionSpec as P

CYCLES = 32
ANG = 144
ROT = 36
SHIFTS = 128
BOX = 128
STEP = ANG // ROT
NX, NZ = 4, 16
LOCAL = 4
MINE = 4
ALL_C = NX * LOCAL
KT = 256
HALF = ROT // 2
HREF = ROT * LOCAL // 2
BLOCK = 80
NEAR = 4
MESH = pl.DeviceIdType.MESH
HIGH = lax.Precision.HIGHEST
NT = (((1,), (1,)), ((), ()))


def phase_tables():
    radius = (np.arange(CYCLES, dtype=np.float64) + 1.0) / BOX
    theta = np.arange(ANG, dtype=np.float64) * (2.0 * math.pi / ANG)
    index = np.arange(SHIFTS)
    shift_x = (index % 16 - 8).astype(np.float64)
    shift_y = (index // 16 - SHIFTS // 32).astype(np.float64)
    along = np.cos(theta)[:, None] * shift_x + np.sin(theta)[:, None] * shift_y
    phase = 2.0 * math.pi * radius[:, None, None] * along[None]

    def order(table):
        table = table.reshape(2, NZ, ROT, STEP, SHIFTS).transpose(2, 4, 1, 0, 3)
        return table.reshape(ROT, SHIFTS, 128)[:HALF].astype(jnp.bfloat16)

    return order(np.cos(phase)), order(np.sin(phase))


def iota(shape, axis):
    return lax.broadcasted_iota(jnp.int32, shape, axis)


def send(src, dst, send_sem, recv_sem, device, **other):
    copy = pltpu.make_async_remote_copy(
        src_ref=src,
        dst_ref=dst,
        send_sem=send_sem,
        recv_sem=recv_sem,
        device_id={"cls": device, **other},
        device_id_type=MESH,
    )
    copy.start()
    return copy


def spread_z(buffer, sends, recvs, x, z):
    copies = {}
    for reach in range(NEAR, 0, -1):
        for step in (reach, -reach):
            device = x * NZ + ((z + step) & (NZ - 1))
            slot = buffer.at[z]
            copies[step] = send(slot, slot, sends.at[step % NZ], recvs.at[step % NZ], device)
    return copies


def relay_z(buffer, sends, recvs, x, z, copies):
    for side, last in ((1, NEAR), (-1, NEAR - 1)):
        copies[side * NEAR].wait_recv()
        slot = buffer.at[(z - side * NEAR) & (NZ - 1)]
        for reach in range(last, 0, -1):
            step = side * (NEAR + reach)
            device = x * NZ + ((z + side * reach) & (NZ - 1))
            copies[step] = send(slot, slot, sends.at[step % NZ], recvs.at[step % NZ], device)


def arrive_z(copies, nearer):
    for step, copy in copies.items():
        if abs(step) != NEAR and (abs(step) < NEAR) == nearer:
            copy.wait_recv()


def kernel(
    cos_hbm, sin_hbm, images_hbm, references_hbm, ctf_hbm, noise_hbm, group_hbm, mic_hbm, count_hbm,
    class_post, rot_post,
    cos, sin, images, references, ctf, noise, group, mic, count,
    rows_c, rows_n, rows_s, padded, split_a, split_b, xs, xr, main, tail, ahead, rall, gathered, cross,
    ends, matrix, power, zt, mixed, shifted_a, shifted_b, acc_a, acc_b, table_c, table_s, score, lines, half, flip, tiles, post, outs,
    local, xsend, xrecv, rsend, rrecv, zsend, zrecv, tsend, trecv, osend, orecv,
):
    me = lax.axis_index("cls")
    x, z = me >> 4, me & (NZ - 1)
    ptl = lax.axis_index("ptl")
    core = ptl & 1
    sibling = ptl + 1 - 2 * core
    along_x = [((x + step) & (NX - 1)) * NZ + z for step in range(1, NX)]

    barrier = pltpu.get_barrier_semaphore()
    near = [x * NZ + ((z + step) & (NZ - 1)) for step in range(-NEAR, NEAR + 1) if step]
    for device in along_x + near:
        pl.semaphore_signal(barrier, inc=1, device_id={"cls": device}, device_id_type=MESH)
    pl.semaphore_signal(barrier, inc=1, device_id={"ptl": sibling}, device_id_type=MESH)
    pairs = [
        (images_hbm, images), (ctf_hbm, ctf), (noise_hbm, noise), (group_hbm, group), (mic_hbm, mic),
        (count_hbm, count), (references_hbm, references), (cos_hbm, cos), (sin_hbm, sin),
    ]
    loads = [pltpu.make_async_copy(a, b, local.at[n]) for n, (a, b) in enumerate(pairs)]
    for load in loads:
        load.start()

    for load in loads[:6]:
        load.wait()
    for p in range(16):
        rows_c[p : p + 1, :] = ctf[pl.ds(group[p], 1), :]
        rows_n[p : p + 1, :] = noise[pl.ds(mic[p], 1), :]
        rows_s[p : p + 1, :] = jnp.full((1, CYCLES), count[p], jnp.int32).astype(jnp.float32)
    counted = rows_s[...]
    ctf_rows = rows_c[...]
    weight = ctf_rows * rows_n[...] * (counted / (counted + 1.0))
    cross[...] = 0.5 * ctf_rows * weight
    own = (x & 1) * NZ + z
    column = jnp.sum(jnp.where(iota((16, CYCLES), 1) == own, weight, 0.0), axis=1, keepdims=True)
    column = column * jnp.where(x >= 2, -1.0, 1.0)
    padded[...] = jnp.zeros_like(padded)
    tail[...] = jnp.zeros_like(tail)
    score[...] = jnp.zeros_like(score)
    ends[:, :, 2 * HREF :, :] = jnp.zeros((2, 2, 8, 128), jnp.float32)
    padded[:, 0:ANG] = images[...] * column
    full = padded[...]
    row, lane = iota((16, 256), 0) & 3, iota((16, 256), 1) & 3
    rolled = {t: (pltpu.roll(full, t % 256, 1) if t else full) for t in range(-3, 4)}
    for d in range(STEP):
        value = jnp.zeros_like(full)
        for p in range(MINE):
            value = jnp.where((row == p) & (lane == p), rolled[p - d], value)
        for t in range(NX):
            line = jnp.sum(value[4 * t : 4 * t + 4], axis=0, keepdims=True)
            xs[t, d : d + 1, :] = line[:, 0:128]
            xs[t, 4 + d : 5 + d, :] = line[:, 128:256]

    pl.semaphore_wait(barrier, NX + 2 * NEAR)
    x_copies = []
    for n, device in enumerate(along_x):
        x_copies.append(send(xs.at[(x + n + 1) & (NX - 1)], xr.at[x], xsend.at[n], xrecv.at[n], device))
    xr[x] = xs[x]

    loads[6].wait()
    def divide(m, carry):
        for n in range(8):
            base = pl.multiple_of(8 * ANG * m + ANG * n // 128 * 128, 128)
            block = references[:, pl.ds(base, 256)].astype(jnp.float32)
            if n:
                block = pltpu.roll(block, 256 - 16 * n, 1)
            split_a[pl.ds(8 * m + n, LOCAL, stride=2 * CYCLES), :] = block[:, 0:128]
            split_b[pl.ds(8 * m + n, LOCAL, stride=2 * CYCLES), :] = block[:, 128:256]
        return carry

    lax.fori_loop(0, 2 * CYCLES // 8, divide, 0)
    rho = iota((KT, 1), 0)
    source = (z - 4 + ((rho >> 7) << 3) + ((rho >> 3) & 7)) & (NZ - 1)
    kappa = (((rho >> 6) & 1) << 5) + (((rho >> 2) & 1) << 4) + source
    repeat = (iota((KT, 2 * CYCLES), 1) == kappa).astype(jnp.float32).astype(jnp.bfloat16)
    angle = iota((1, 256), 1)
    keep = ((rho & 3) == (angle & 3)) & (angle < ANG)
    rho = iota((ROT * LOCAL, 1), 0)
    block_of = jnp.where(rho < LOCAL, 0, ROT - (rho >> 2))
    hit = (angle >> 2) == block_of
    total = jnp.zeros((ROT * LOCAL, KT), jnp.float32)
    for c in range(LOCAL):
        cut = slice(2 * CYCLES * c, 2 * CYCLES * (c + 1))
        one = jnp.concatenate([split_a[cut, :], split_b[cut, :]], axis=1).astype(jnp.bfloat16)
        spread = jnp.dot(repeat, one, preferred_element_type=jnp.float32)
        spread = jnp.where(keep, spread, 0.0).astype(jnp.bfloat16)
        pick = (hit & ((rho & 3) == c)).astype(jnp.float32).astype(jnp.bfloat16)
        total += lax.dot_general(pick, spread, NT, preferred_element_type=jnp.float32)
    rall[x, 0] = total[0:HREF]
    rall[x, 1] = total[HREF:]

    left, right = (x + NX - 1) & (NX - 1), (x + 1) & (NX - 1)
    opposite = (x + 2) & (NX - 1)
    part_a, part_b = pl.ds(0, 40), pl.ds(40, HREF - 40)
    slot = rall.at[x, core]
    from_left = send(slot, slot, rsend.at[0], rrecv.at[0], right * NZ + z)
    from_right = send(slot, slot, rsend.at[1], rrecv.at[1], left * NZ + z)

    def place(t):
        low, high = rall[t, 0], rall[t, 1]
        plus, minus = low + high, low - high
        for lanes in range(2):
            cut = slice(128 * lanes, 128 * lanes + 128)
            ends[0, lanes, 0:HREF, :] = plus[:, cut]
            ends[0, lanes, HREF : 2 * HREF, :] = plus[:, cut]
            ends[1, lanes, 0:HREF, :] = -minus[:, cut]
            ends[1, lanes, HREF : 2 * HREF, :] = minus[:, cut]
        rows = pl.ds(pl.multiple_of(BLOCK * t, 16), BLOCK)
        for sign in range(2):
            for b in range(HALF):
                first = LOCAL * (HALF - b)
                for lanes in range(2):
                    value = ends[sign, lanes, first : first + BLOCK, :]
                    matrix[sign, lanes, rows, 128 * b : 128 * b + 128] = value.astype(jnp.bfloat16)
        square = jnp.sum((low * low + high * high).reshape(HREF // 8, 8, KT), axis=0)
        power[pl.ds(pl.multiple_of(8 * t, 8), 8), :] = square + pltpu.roll(square, 4, 0)

    for copy in x_copies:
        copy.wait_recv()
    for part in range(2):
        last = jnp.zeros((1, 128), jnp.float32)
        for low in range(2):
            t = 2 * part + low
            block = xr[t]
            gathered[z, 2 * t] = block[0:2]
            gathered[z, 2 * t + 1] = block[2:4]
            for d in range(STEP):
                at = 16 * (STEP * low + d)
                rest = block[4 + d : 5 + d]
                last = last + (pltpu.roll(rest, at, 1) if at else rest)
        gathered[z, 8, part : part + 1, :] = last
    z_copies = spread_z(gathered, zsend, zrecv, x, z)

    loads[7].wait()
    loads[8].wait()
    first_lanes = iota((128, 128), 1) < 64
    turn = ((20 - z) * 8) & 127

    def arrange(b, carry):
        for table, rolled_table, sign in ((cos, table_c, -1.0), (sin, table_s, 1.0)):
            value = pltpu.roll(table[b].astype(jnp.float32), turn, 1)
            moved = pltpu.roll(value, 64, 1)
            rolled_table[0, b] = jnp.where(first_lanes, value, sign * moved)
            rolled_table[1, b] = jnp.where(first_lanes, moved, sign * value)
        return carry

    lax.fori_loop(0, HALF, arrange, 0)

    from_left.wait_recv()
    slot = rall.at[left, core]
    part = rall.at[left, core, part_a]
    onward_a = send(part, part, rsend.at[2], rrecv.at[2], right * NZ + z)
    over_left = send(slot, slot, rsend.at[4], rrecv.at[4], me, ptl=sibling)
    from_right.wait_recv()
    slot = rall.at[right, core]
    part = rall.at[right, core, part_b]
    onward_b = send(part, part, rsend.at[3], rrecv.at[3], left * NZ + z)
    over_right = send(slot, slot, rsend.at[5], rrecv.at[5], me, ptl=sibling)
    place(x)
    onward_a.wait_recv()
    onward_b.wait_recv()
    slot = rall.at[opposite, core]
    over_opposite = send(slot, slot, rsend.at[6], rrecv.at[6], me, ptl=sibling)
    relay_z(gathered, zsend, zrecv, x, z, z_copies)
    over_left.wait_recv()
    place(left)
    over_right.wait_recv()
    place(right)
    over_opposite.wait_recv()
    place(opposite)

    def quadratic():
        half[...] = jnp.zeros_like(half)
        half[0:MINE, :] = cross[pl.ds(x * MINE, MINE), :]
        lam = iota((1, KT), 1)
        cycle = (((lam >> 2) & 1) << 4) + ((z - 4 + ((lam >> 7) << 3) + ((lam >> 3) & 7)) & (NZ - 1))
        spread = (iota((CYCLES, KT), 0) == cycle).astype(jnp.float32)
        half_wide = jnp.dot(half[...], spread, precision=HIGH, preferred_element_type=jnp.float32)
        return lax.dot_general(power[...], half_wide, NT, precision=HIGH, preferred_element_type=jnp.float32)

    def unpack(far):
        for zr in range(8):
            origin = (z - 4 + 8 * far + zr) & (NZ - 1)
            for t in range(NX):
                row = 64 * (t // 2) + 8 * zr + 4 * (t % 2)
                main[row : row + 2, :] = gathered[origin, 2 * t]
                main[row + 2 : row + 4, :] = gathered[origin, 2 * t + 1]
            last = gathered[origin, 8]
            ahead[zr : zr + 1, :] = last[0:1]
            ahead[8 + zr : 9 + zr, :] = last[1:2]
        last = ahead[...]
        for n in range(8):
            moved = pltpu.roll(last, 128 - 16 * n, 1) if n else last
            tail[pl.ds(n, 8, stride=8), :] = moved[0:8]
            tail[pl.ds(64 + n, 8, stride=8), :] = moved[8:16]
        zt[0:128] = main[...].T
        zt[128:ANG] = tail[...].T[0:16]
        one, two = zt[0 : ANG // 2, :], zt[ANG // 2 : ANG, :]
        plus, minus = 0.5 * (one + two), 0.5 * (one - two)
        mixed[0] = plus
        mixed[1] = minus
        mixed[2] = pltpu.roll(plus, 64, 1)
        mixed[3] = pltpu.roll(minus, 64, 1)

    def build(far, pair, target):
        for b in range(HALF):
            c, s = table_c[far, b], table_s[far, b]
            lanes = slice(128 * b, 128 * b + 128)
            for h in range(2):
                line = slice(4 * b + 2 * pair + h, 4 * b + 2 * pair + h + 1)
                rows = slice(128 * h, 128 * h + 128)
                target[0, rows, lanes] = (c * mixed[0, line] + s * mixed[3, line]).astype(jnp.bfloat16)
                target[1, rows, lanes] = (c * mixed[1, line] + s * mixed[2, line]).astype(jnp.bfloat16)

    def multiply(far, source, acc):
        for sign in range(2):
            part = lax.dot_general(matrix[sign, far], source[sign], NT, preferred_element_type=jnp.float32)
            if far:
                acc[sign] += part
            else:
                acc[sign] = part

    def reduce(pair, acc):
        lane = iota((BLOCK, 128), 1)

        def part(t, carry):
            rows = pl.ds(pl.multiple_of(BLOCK * t, 16), BLOCK)
            tops = [jnp.zeros((BLOCK, 128), jnp.float32)] * 2
            totals = [jnp.ones((BLOCK, 128), jnp.float32)] * 2
            for h in range(2):
                even = acc[0, rows, 128 * h : 128 * h + 128]
                odd = acc[1, rows, 128 * h : 128 * h + 128]
                for half, value in enumerate((even + odd, even - odd)):
                    high = jnp.max(value, axis=1, keepdims=True)
                    low = jnp.sum(jnp.exp(value - high), axis=1, keepdims=True)
                    tops[half] = jnp.where(lane == 2 * pair + h, high, tops[half])
                    totals[half] = jnp.where(lane == 2 * pair + h, low, totals[half])
            for half in range(2):
                score[half, rows, :] += tops[half] + jnp.log(totals[half])
            return carry

        lax.fori_loop(0, NX, part, 0)

    for far in range(2):
        arrive_z(z_copies, far == 0)
        unpack(far)
        build(far, 0, shifted_a)
        build(far, 1, shifted_b)
        multiply(far, shifted_a, acc_a)
        multiply(far, shifted_b, acc_b)
        if far == 0:
            quad = quadratic()
    reduce(0, acc_a)
    reduce(1, acc_b)

    tiles_of = (HREF // 8, 8, 128)
    flip[...] = jnp.zeros_like(flip)
    values = []
    for t in range(NX):
        shift = quad[8 * t : 8 * t + 8]
        pair = [score[half, BLOCK * t : BLOCK * t + HREF, :].reshape(tiles_of) - shift for half in range(2)]
        values.append(pair)
        high = jnp.maximum(jnp.max(pair[0], axis=0), jnp.max(pair[1], axis=0))
        high = jnp.maximum(high, pltpu.roll(high, 4, 0))
        low = jnp.sum(jnp.exp(pair[0] - high), axis=0) + jnp.sum(jnp.exp(pair[1] - high), axis=0)
        low = low + pltpu.roll(low, 4, 0)
        by_class = high + jnp.log(low)
        flip[64 + LOCAL * t : 64 + LOCAL * (t + 1), :] = by_class[0:LOCAL]
    for half in range(2):
        four = [values[t][half] for t in range(NX)]
        high = jnp.maximum(jnp.maximum(four[0], four[1]), jnp.maximum(four[2], four[3]))
        low = jnp.exp(four[0] - high) + jnp.exp(four[1] - high) + jnp.exp(four[2] - high) + jnp.exp(four[3] - high)
        lines[half * HREF : (half + 1) * HREF, :] = (high + jnp.log(low)).reshape(HREF, 128)
    four = [lines[pl.ds(c, ROT, stride=LOCAL), :] for c in range(LOCAL)]
    high = jnp.maximum(jnp.maximum(four[0], four[1]), jnp.maximum(four[2], four[3]))
    low = jnp.exp(four[0] - high) + jnp.exp(four[1] - high) + jnp.exp(four[2] - high) + jnp.exp(four[3] - high)
    flip[0:ROT, :] = high + jnp.log(low)
    tile = flip[...].T[0:MINE, :]

    tiles[z] = tile
    t_copies = []
    for reach in range(NZ // 2, 0, -1):
        for step in (reach, -reach) if reach < NZ // 2 else (reach,):
            device = x * NZ + ((z + step) & (NZ - 1))
            n = step % NZ
            t_copies.append(send(tiles.at[z], tiles.at[z], tsend.at[n], trecv.at[n], device))
    for copy in t_copies:
        copy.wait_recv()
    values = tiles[...]
    high = jnp.max(values, axis=0)
    rot_lse = high + jnp.log(jnp.sum(jnp.exp(values - high[None]), axis=0))
    lane = iota((MINE, 128), 1)
    masked = jnp.where(lane < ROT, rot_lse, -jnp.inf)
    high = jnp.max(masked, axis=1, keepdims=True)
    norm = high + jnp.log(jnp.sum(jnp.exp(masked - high), axis=1, keepdims=True))
    post[...] = jnp.where(lane < ROT, rot_lse, tile) - norm
    outs[x] = post[...]
    o_copies = []
    for n, device in enumerate(along_x):
        o_copies.append(send(post, outs.at[x], osend.at[n], orecv.at[n], device))
    for copy in o_copies:
        copy.wait_recv()
    line = iota((MINE, 128), 0)
    for t in range(NX):
        live = jnp.zeros((MINE, 128), jnp.int32)
        for p in range(MINE):
            live = jnp.where(line == p, count[MINE * t + p], live)
        value = jnp.where(live > 0, outs[t], 0.0)
        rot_post[MINE * t : MINE * t + MINE, :] = value[:, 0:ROT]
        class_post[MINE * t : MINE * t + MINE, :] = pltpu.roll(value, 64 - LOCAL * x, 1)[:, 0:LOCAL]
    sent = x_copies + [from_left, from_right, onward_a, onward_b, over_left, over_right, over_opposite] + list(z_copies.values()) + t_copies + o_copies
    for copy in sent:
        copy.wait_send()


def body(cos, sin, images, references, ctf_table, noise_inv, defocus_group, micrograph, batch_size):
    vmem, hbm = pl.BlockSpec(memory_space=pltpu.VMEM), pl.BlockSpec(memory_space=pltpu.HBM)
    f32, bf16, i32, dma = jnp.float32, jnp.bfloat16, jnp.int32, pltpu.SemaphoreType.DMA
    operands = (cos, sin, images, references, ctf_table, noise_inv, defocus_group, micrograph, batch_size)
    operands = [pltpu.with_memory_space_constraint(a, pltpu.HBM) for a in operands]
    class_post, rot_post = pl.pallas_call(
        kernel,
        out_shape=(
            jax.ShapeDtypeStruct((16, LOCAL), f32),
            jax.ShapeDtypeStruct((16, ROT), f32),
        ),
        in_specs=[hbm] * 9,
        out_specs=(vmem, vmem),
        scratch_shapes=[
            pltpu.VMEM(cos.shape, bf16),
            pltpu.VMEM(sin.shape, bf16),
            pltpu.VMEM(images.shape, f32),
            pltpu.VMEM(references.shape, bf16),
            pltpu.VMEM(ctf_table.shape, f32),
            pltpu.VMEM(noise_inv.shape, f32),
            pltpu.SMEM((16,), i32),
            pltpu.SMEM((16,), i32),
            pltpu.SMEM((16,), i32),
            pltpu.VMEM((16, CYCLES), f32),
            pltpu.VMEM((16, CYCLES), f32),
            pltpu.VMEM((16, CYCLES), f32),
            pltpu.VMEM((16, 256), f32),
            pltpu.VMEM((2 * CYCLES * LOCAL, 128), f32),
            pltpu.VMEM((2 * CYCLES * LOCAL, 128), f32),
            pltpu.VMEM((NX, 8, 128), f32),
            pltpu.VMEM((NX, 8, 128), f32),
            pltpu.VMEM((128, 128), f32),
            pltpu.VMEM((128, 128), f32),
            pltpu.VMEM((16, 128), f32),
            pltpu.VMEM((NX, 2, HREF, KT), f32),
            pltpu.VMEM((NZ, 9, 2, 128), f32),
            pltpu.VMEM((16, CYCLES), f32),
            pltpu.VMEM((2, 2, 2 * HREF + 8, 128), f32),
            pltpu.VMEM((2, 2, NX * BLOCK, HALF * 128), bf16),
            pltpu.VMEM((NX * 8, KT), f32),
            pltpu.VMEM((ANG, 128), f32),
            pltpu.VMEM((4, ANG // 2, 128), f32),
            pltpu.VMEM((2, 2 * SHIFTS, HALF * 128), bf16),
            pltpu.VMEM((2, 2 * SHIFTS, HALF * 128), bf16),
            pltpu.VMEM((2, NX * BLOCK, 2 * SHIFTS), f32),
            pltpu.VMEM((2, NX * BLOCK, 2 * SHIFTS), f32),
            pltpu.VMEM((2, HALF, SHIFTS, 128), f32),
            pltpu.VMEM((2, HALF, SHIFTS, 128), f32),
            pltpu.VMEM((2, NX * BLOCK, 128), f32),
            pltpu.VMEM((2 * HREF, 128), f32),
            pltpu.VMEM((128, CYCLES), f32),
            pltpu.VMEM((128, 128), f32),
            pltpu.VMEM((NZ, MINE, 128), f32),
            pltpu.VMEM((MINE, 128), f32),
            pltpu.VMEM((NX, MINE, 128), f32),
            dma((9,)),
            dma((NX - 1,)),
            dma((NX - 1,)),
            dma((7,)),
            dma((7,)),
            dma((NZ,)),
            dma((NZ,)),
            dma((NZ,)),
            dma((NZ,)),
            dma((NX - 1,)),
            dma((NX - 1,)),
        ],
        compiler_params=pltpu.CompilerParams(collective_id=0, has_side_effects=True, vmem_limit_bytes=40 << 20),
        name="expectation",
    )(*operands)
    return class_post, rot_post


def solution(mesh):
    cos, sin = phase_tables()
    in_specs = (P("ptl", "cls"), P("cls", None), P(), P(), P("ptl"), P("ptl"), P("ptl"))
    out_specs = (P("ptl", "cls"), P("ptl", None))
    mapped = jax.shard_map(
        body, mesh=mesh, in_specs=(P(), P()) + in_specs, out_specs=out_specs, check_vma=False
    )

    def run(*args):
        return mapped(jnp.asarray(cos), jnp.asarray(sin), *args)

    return run
```

```python
import math

import jax
import jax.numpy as jnp
import numpy as np
from jax import lax
from jax.experimental import pallas as pl
from jax.experimental.pallas import tpu as pltpu
from jax.sharding import PartitionSpec as P

CYCLES = 32
ANG = 144
ROT = 36
SHIFTS = 128
BOX = 128
STEP = ANG // ROT
NX, NZ = 4, 16
LOCAL = 4
MINE = 4
ALL_C = NX * LOCAL
KT = 256
HALF = ROT // 2
HREF = ROT * LOCAL // 2
BLOCK = 80
NEAR = 4
MESH = pl.DeviceIdType.MESH
HIGH = lax.Precision.HIGHEST
NT = (((1,), (1,)), ((), ()))


def phase_tables():
    radius = (np.arange(CYCLES, dtype=np.float64) + 1.0) / BOX
    theta = np.arange(ANG, dtype=np.float64) * (2.0 * math.pi / ANG)
    index = np.arange(SHIFTS)
    shift_x = (index % 16 - 8).astype(np.float64)
    shift_y = (index // 16 - SHIFTS // 32).astype(np.float64)
    along = np.cos(theta)[:, None] * shift_x + np.sin(theta)[:, None] * shift_y
    phase = 2.0 * math.pi * radius[:, None, None] * along[None]

    def order(table):
        table = table.reshape(2, NZ, ROT, STEP, SHIFTS).transpose(2, 4, 1, 0, 3)
        return table.reshape(ROT, SHIFTS, 128)[:HALF].astype(jnp.bfloat16)

    return order(np.cos(phase)), order(np.sin(phase))


def iota(shape, axis):
    return lax.broadcasted_iota(jnp.int32, shape, axis)


def send(src, dst, send_sem, recv_sem, device, **other):
    copy = pltpu.make_async_remote_copy(
        src_ref=src,
        dst_ref=dst,
        send_sem=send_sem,
        recv_sem=recv_sem,
        device_id={"cls": device, **other},
        device_id_type=MESH,
    )
    copy.start()
    return copy


def spread_z(buffer, sends, recvs, x, z):
    copies = {}
    for reach in range(NEAR, 0, -1):
        for step in (reach, -reach):
            device = x * NZ + ((z + step) & (NZ - 1))
            slot = buffer.at[z]
            copies[step] = send(slot, slot, sends.at[step % NZ], recvs.at[step % NZ], device)
    return copies


def relay_z(buffer, sends, recvs, x, z, copies):
    for side, last in ((1, NEAR), (-1, NEAR - 1)):
        copies[side * NEAR].wait_recv()
        slot = buffer.at[(z - side * NEAR) & (NZ - 1)]
        for reach in range(last, 0, -1):
            step = side * (NEAR + reach)
            device = x * NZ + ((z + side * reach) & (NZ - 1))
            copies[step] = send(slot, slot, sends.at[step % NZ], recvs.at[step % NZ], device)


def arrive_z(copies, nearer):
    for step, copy in copies.items():
        if abs(step) != NEAR and (abs(step) < NEAR) == nearer:
            copy.wait_recv()


def kernel(
    cos_hbm, sin_hbm, images_hbm, references_hbm, ctf_hbm, noise_hbm, group_hbm, mic_hbm, count_hbm,
    class_post, rot_post,
    cos, sin, images, references, ctf, noise, group, mic, count,
    rows_c, rows_n, rows_s, padded, split_a, split_b, xs, xr, main, tail, ahead, rall, gathered, cross,
    ends, matrix, power, zt, mixed, shifted_a, shifted_b, acc_a, acc_b, table_c, table_s, score, lines, half, flip, tiles, post, outs,
    local, xsend, xrecv, rsend, rrecv, zsend, zrecv, tsend, trecv, osend, orecv,
):
    me = lax.axis_index("cls")
    x, z = me >> 4, me & (NZ - 1)
    ptl = lax.axis_index("ptl")
    core = ptl & 1
    sibling = ptl + 1 - 2 * core
    along_x = [((x + step) & (NX - 1)) * NZ + z for step in range(1, NX)]

    barrier = pltpu.get_barrier_semaphore()
    near = [x * NZ + ((z + step) & (NZ - 1)) for step in range(-NEAR, NEAR + 1) if step]
    for device in along_x + near:
        pl.semaphore_signal(barrier, inc=1, device_id={"cls": device}, device_id_type=MESH)
    pl.semaphore_signal(barrier, inc=1, device_id={"ptl": sibling}, device_id_type=MESH)
    pairs = [
        (images_hbm, images), (ctf_hbm, ctf), (noise_hbm, noise), (group_hbm, group), (mic_hbm, mic),
        (count_hbm, count), (references_hbm, references), (cos_hbm, cos), (sin_hbm, sin),
    ]
    loads = [pltpu.make_async_copy(a, b, local.at[n]) for n, (a, b) in enumerate(pairs)]
    for load in loads:
        load.start()

    for load in loads[:6]:
        load.wait()
    for p in range(16):
        rows_c[p : p + 1, :] = ctf[pl.ds(group[p], 1), :]
        rows_n[p : p + 1, :] = noise[pl.ds(mic[p], 1), :]
        rows_s[p : p + 1, :] = jnp.full((1, CYCLES), count[p], jnp.int32).astype(jnp.float32)
    counted = rows_s[...]
    ctf_rows = rows_c[...]
    weight = ctf_rows * rows_n[...] * (counted / (counted + 1.0))
    cross[...] = 0.5 * ctf_rows * weight
    own = (x & 1) * NZ + z
    column = jnp.sum(jnp.where(iota((16, CYCLES), 1) == own, weight, 0.0), axis=1, keepdims=True)
    column = column * jnp.where(x >= 2, -1.0, 1.0)
    padded[...] = jnp.zeros_like(padded)
    tail[...] = jnp.zeros_like(tail)
    score[...] = jnp.zeros_like(score)
    ends[:, :, 2 * HREF :, :] = jnp.zeros((2, 2, 8, 128), jnp.float32)
    padded[:, 0:ANG] = images[...] * column
    full = padded[...]
    row, lane = iota((16, 256), 0) & 3, iota((16, 256), 1) & 3
    rolled = {t: (pltpu.roll(full, t % 256, 1) if t else full) for t in range(-3, 4)}
    for d in range(STEP):
        value = jnp.zeros_like(full)
        for p in range(MINE):
            value = jnp.where((row == p) & (lane == p), rolled[p - d], value)
        for t in range(NX):
            line = jnp.sum(value[4 * t : 4 * t + 4], axis=0, keepdims=True)
            xs[t, d : d + 1, :] = line[:, 0:128]
            xs[t, 4 + d : 5 + d, :] = line[:, 128:256]

    pl.semaphore_wait(barrier, NX + 2 * NEAR)
    x_copies = []
    for n, device in enumerate(along_x):
        x_copies.append(send(xs.at[(x + n + 1) & (NX - 1)], xr.at[x], xsend.at[n], xrecv.at[n], device))
    xr[x] = xs[x]

    loads[6].wait()
    def divide(m, carry):
        for n in range(8):
            base = pl.multiple_of(8 * ANG * m + ANG * n // 128 * 128, 128)
            block = references[:, pl.ds(base, 256)].astype(jnp.float32)
            if n:
                block = pltpu.roll(block, 256 - 16 * n, 1)
            split_a[pl.ds(8 * m + n, LOCAL, stride=2 * CYCLES), :] = block[:, 0:128]
            split_b[pl.ds(8 * m + n, LOCAL, stride=2 * CYCLES), :] = block[:, 128:256]
        return carry

    lax.fori_loop(0, 2 * CYCLES // 8, divide, 0)
    rho = iota((KT, 1), 0)
    source = (z - 4 + ((rho >> 7) << 3) + ((rho >> 3) & 7)) & (NZ - 1)
    kappa = (((rho >> 6) & 1) << 5) + (((rho >> 2) & 1) << 4) + source
    repeat = (iota((KT, 2 * CYCLES), 1) == kappa).astype(jnp.float32).astype(jnp.bfloat16)
    angle = iota((1, 256), 1)
    keep = ((rho & 3) == (angle & 3)) & (angle < ANG)
    rho = iota((ROT * LOCAL, 1), 0)
    block_of = jnp.where(rho < LOCAL, 0, ROT - (rho >> 2))
    hit = (angle >> 2) == block_of
    total = jnp.zeros((ROT * LOCAL, KT), jnp.float32)
    for c in range(LOCAL):
        cut = slice(2 * CYCLES * c, 2 * CYCLES * (c + 1))
        one = jnp.concatenate([split_a[cut, :], split_b[cut, :]], axis=1).astype(jnp.bfloat16)
        spread = jnp.dot(repeat, one, preferred_element_type=jnp.float32)
        spread = jnp.where(keep, spread, 0.0).astype(jnp.bfloat16)
        pick = (hit & ((rho & 3) == c)).astype(jnp.float32).astype(jnp.bfloat16)
        total += lax.dot_general(pick, spread, NT, preferred_element_type=jnp.float32)
    rall[x, 0] = total[0:HREF]
    rall[x, 1] = total[HREF:]

    left, right = (x + NX - 1) & (NX - 1), (x + 1) & (NX - 1)
    opposite = (x + 2) & (NX - 1)
    part_a, part_b = pl.ds(0, 40), pl.ds(40, HREF - 40)
    slot = rall.at[x, core]
    from_left = send(slot, slot, rsend.at[0], rrecv.at[0], right * NZ + z)
    from_right = send(slot, slot, rsend.at[1], rrecv.at[1], left * NZ + z)

    def place(t):
        low, high = rall[t, 0], rall[t, 1]
        plus, minus = low + high, low - high
        for lanes in range(2):
            cut = slice(128 * lanes, 128 * lanes + 128)
            ends[0, lanes, 0:HREF, :] = plus[:, cut]
            ends[0, lanes, HREF : 2 * HREF, :] = plus[:, cut]
            ends[1, lanes, 0:HREF, :] = -minus[:, cut]
            ends[1, lanes, HREF : 2 * HREF, :] = minus[:, cut]
        rows = pl.ds(pl.multiple_of(BLOCK * t, 16), BLOCK)
        for sign in range(2):
            for b in range(HALF):
                first = LOCAL * (HALF - b)
                for lanes in range(2):
                    value = ends[sign, lanes, first : first + BLOCK, :]
                    matrix[sign, lanes, rows, 128 * b : 128 * b + 128] = value.astype(jnp.bfloat16)
        square = jnp.sum((low * low + high * high).reshape(HREF // 8, 8, KT), axis=0)
        power[pl.ds(pl.multiple_of(8 * t, 8), 8), :] = square + pltpu.roll(square, 4, 0)

    for copy in x_copies:
        copy.wait_recv()
    for part in range(2):
        last = jnp.zeros((1, 128), jnp.float32)
        for low in range(2):
            t = 2 * part + low
            block = xr[t]
            gathered[z, 2 * t] = block[0:2]
            gathered[z, 2 * t + 1] = block[2:4]
            for d in range(STEP):
                at = 16 * (STEP * low + d)
                rest = block[4 + d : 5 + d]
                last = last + (pltpu.roll(rest, at, 1) if at else rest)
        gathered[z, 8, part : part + 1, :] = last
    z_copies = spread_z(gathered, zsend, zrecv, x, z)

    loads[7].wait()
    loads[8].wait()
    first_lanes = iota((128, 128), 1) < 64
    turn = ((20 - z) * 8) & 127

    def arrange(b, carry):
        for table, rolled_table, sign in ((cos, table_c, -1.0), (sin, table_s, 1.0)):
            value = pltpu.roll(table[b].astype(jnp.float32), turn, 1)
            moved = pltpu.roll(value, 64, 1)
            rolled_table[0, b] = jnp.where(first_lanes, value, sign * moved)
            rolled_table[1, b] = jnp.where(first_lanes, moved, sign * value)
        return carry

    lax.fori_loop(0, HALF, arrange, 0)

    relay_z(gathered, zsend, zrecv, x, z, z_copies)
    from_left.wait_recv()
    slot = rall.at[left, core]
    part = rall.at[left, core, part_a]
    onward_a = send(part, part, rsend.at[2], rrecv.at[2], right * NZ + z)
    over_left = send(slot, slot, rsend.at[4], rrecv.at[4], me, ptl=sibling)
    from_right.wait_recv()
    slot = rall.at[right, core]
    part = rall.at[right, core, part_b]
    onward_b = send(part, part, rsend.at[3], rrecv.at[3], left * NZ + z)
    over_right = send(slot, slot, rsend.at[5], rrecv.at[5], me, ptl=sibling)
    place(x)
    onward_a.wait_recv()
    onward_b.wait_recv()
    slot = rall.at[opposite, core]
    over_opposite = send(slot, slot, rsend.at[6], rrecv.at[6], me, ptl=sibling)
    over_left.wait_recv()
    place(left)
    over_right.wait_recv()
    place(right)
    over_opposite.wait_recv()
    place(opposite)

    def quadratic():
        half[...] = jnp.zeros_like(half)
        half[0:MINE, :] = cross[pl.ds(x * MINE, MINE), :]
        lam = iota((1, KT), 1)
        cycle = (((lam >> 2) & 1) << 4) + ((z - 4 + ((lam >> 7) << 3) + ((lam >> 3) & 7)) & (NZ - 1))
        spread = (iota((CYCLES, KT), 0) == cycle).astype(jnp.float32)
        half_wide = jnp.dot(half[...], spread, precision=HIGH, preferred_element_type=jnp.float32)
        return lax.dot_general(power[...], half_wide, NT, precision=HIGH, preferred_element_type=jnp.float32)

    def unpack(far):
        for zr in range(8):
            origin = (z - 4 + 8 * far + zr) & (NZ - 1)
            for t in range(NX):
                row = 64 * (t // 2) + 8 * zr + 4 * (t % 2)
                main[row : row + 2, :] = gathered[origin, 2 * t]
                main[row + 2 : row + 4, :] = gathered[origin, 2 * t + 1]
            last = gathered[origin, 8]
            ahead[zr : zr + 1, :] = last[0:1]
            ahead[8 + zr : 9 + zr, :] = last[1:2]
        last = ahead[...]
        for n in range(8):
            moved = pltpu.roll(last, 128 - 16 * n, 1) if n else last
            tail[pl.ds(n, 8, stride=8), :] = moved[0:8]
            tail[pl.ds(64 + n, 8, stride=8), :] = moved[8:16]
        zt[0:128] = main[...].T
        zt[128:ANG] = tail[...].T[0:16]
        one, two = zt[0 : ANG // 2, :], zt[ANG // 2 : ANG, :]
        plus, minus = 0.5 * (one + two), 0.5 * (one - two)
        mixed[0] = plus
        mixed[1] = minus
        mixed[2] = pltpu.roll(plus, 64, 1)
        mixed[3] = pltpu.roll(minus, 64, 1)

    def build(far, pair, target):
        for b in range(HALF):
            c, s = table_c[far, b], table_s[far, b]
            lanes = slice(128 * b, 128 * b + 128)
            for h in range(2):
                line = slice(4 * b + 2 * pair + h, 4 * b + 2 * pair + h + 1)
                rows = slice(128 * h, 128 * h + 128)
                target[0, rows, lanes] = (c * mixed[0, line] + s * mixed[3, line]).astype(jnp.bfloat16)
                target[1, rows, lanes] = (c * mixed[1, line] + s * mixed[2, line]).astype(jnp.bfloat16)

    def multiply(far, source, acc):
        for sign in range(2):
            part = lax.dot_general(matrix[sign, far], source[sign], NT, preferred_element_type=jnp.float32)
            if far:
                acc[sign] += part
            else:
                acc[sign] = part

    def reduce(pair, acc):
        lane = iota((BLOCK, 128), 1)

        def part(t, carry):
            rows = pl.ds(pl.multiple_of(BLOCK * t, 16), BLOCK)
            tops = [jnp.zeros((BLOCK, 128), jnp.float32)] * 2
            totals = [jnp.ones((BLOCK, 128), jnp.float32)] * 2
            for h in range(2):
                even = acc[0, rows, 128 * h : 128 * h + 128]
                odd = acc[1, rows, 128 * h : 128 * h + 128]
                for half, value in enumerate((even + odd, even - odd)):
                    high = jnp.max(value, axis=1, keepdims=True)
                    low = jnp.sum(jnp.exp(value - high), axis=1, keepdims=True)
                    tops[half] = jnp.where(lane == 2 * pair + h, high, tops[half])
                    totals[half] = jnp.where(lane == 2 * pair + h, low, totals[half])
            for half in range(2):
                score[half, rows, :] += tops[half] + jnp.log(totals[half])
            return carry

        lax.fori_loop(0, NX, part, 0)

    for far in range(2):
        arrive_z(z_copies, far == 0)
        unpack(far)
        build(far, 0, shifted_a)
        build(far, 1, shifted_b)
        multiply(far, shifted_a, acc_a)
        multiply(far, shifted_b, acc_b)
        if far == 0:
            quad = quadratic()
    reduce(0, acc_a)
    reduce(1, acc_b)

    tiles_of = (HREF // 8, 8, 128)
    flip[...] = jnp.zeros_like(flip)
    values = []
    for t in range(NX):
        shift = quad[8 * t : 8 * t + 8]
        pair = [score[half, BLOCK * t : BLOCK * t + HREF, :].reshape(tiles_of) - shift for half in range(2)]
        values.append(pair)
        high = jnp.maximum(jnp.max(pair[0], axis=0), jnp.max(pair[1], axis=0))
        high = jnp.maximum(high, pltpu.roll(high, 4, 0))
        low = jnp.sum(jnp.exp(pair[0] - high), axis=0) + jnp.sum(jnp.exp(pair[1] - high), axis=0)
        low = low + pltpu.roll(low, 4, 0)
        by_class = high + jnp.log(low)
        flip[64 + LOCAL * t : 64 + LOCAL * (t + 1), :] = by_class[0:LOCAL]
    for half in range(2):
        four = [values[t][half] for t in range(NX)]
        high = jnp.maximum(jnp.maximum(four[0], four[1]), jnp.maximum(four[2], four[3]))
        low = jnp.exp(four[0] - high) + jnp.exp(four[1] - high) + jnp.exp(four[2] - high) + jnp.exp(four[3] - high)
        lines[half * HREF : (half + 1) * HREF, :] = (high + jnp.log(low)).reshape(HREF, 128)
    four = [lines[pl.ds(c, ROT, stride=LOCAL), :] for c in range(LOCAL)]
    high = jnp.maximum(jnp.maximum(four[0], four[1]), jnp.maximum(four[2], four[3]))
    low = jnp.exp(four[0] - high) + jnp.exp(four[1] - high) + jnp.exp(four[2] - high) + jnp.exp(four[3] - high)
    flip[0:ROT, :] = high + jnp.log(low)
    tile = flip[...].T[0:MINE, :]

    tiles[z] = tile
    t_copies = []
    for reach in range(NZ // 2, 0, -1):
        for step in (reach, -reach) if reach < NZ // 2 else (reach,):
            device = x * NZ + ((z + step) & (NZ - 1))
            n = step % NZ
            t_copies.append(send(tiles.at[z], tiles.at[z], tsend.at[n], trecv.at[n], device))
    for copy in t_copies:
        copy.wait_recv()
    values = tiles[...]
    high = jnp.max(values, axis=0)
    rot_lse = high + jnp.log(jnp.sum(jnp.exp(values - high[None]), axis=0))
    lane = iota((MINE, 128), 1)
    masked = jnp.where(lane < ROT, rot_lse, -jnp.inf)
    high = jnp.max(masked, axis=1, keepdims=True)
    norm = high + jnp.log(jnp.sum(jnp.exp(masked - high), axis=1, keepdims=True))
    post[...] = jnp.where(lane < ROT, rot_lse, tile) - norm
    outs[x] = post[...]
    o_copies = []
    for n, device in enumerate(along_x):
        o_copies.append(send(post, outs.at[x], osend.at[n], orecv.at[n], device))
    for copy in o_copies:
        copy.wait_recv()
    line = iota((MINE, 128), 0)
    for t in range(NX):
        live = jnp.zeros((MINE, 128), jnp.int32)
        for p in range(MINE):
            live = jnp.where(line == p, count[MINE * t + p], live)
        value = jnp.where(live > 0, outs[t], 0.0)
        rot_post[MINE * t : MINE * t + MINE, :] = value[:, 0:ROT]
        class_post[MINE * t : MINE * t + MINE, :] = pltpu.roll(value, 64 - LOCAL * x, 1)[:, 0:LOCAL]
    sent = x_copies + [from_left, from_right, onward_a, onward_b, over_left, over_right, over_opposite] + list(z_copies.values()) + t_copies + o_copies
    for copy in sent:
        copy.wait_send()


def body(cos, sin, images, references, ctf_table, noise_inv, defocus_group, micrograph, batch_size):
    vmem, hbm = pl.BlockSpec(memory_space=pltpu.VMEM), pl.BlockSpec(memory_space=pltpu.HBM)
    f32, bf16, i32, dma = jnp.float32, jnp.bfloat16, jnp.int32, pltpu.SemaphoreType.DMA
    operands = (cos, sin, images, references, ctf_table, noise_inv, defocus_group, micrograph, batch_size)
    operands = [pltpu.with_memory_space_constraint(a, pltpu.HBM) for a in operands]
    class_post, rot_post = pl.pallas_call(
        kernel,
        out_shape=(
            jax.ShapeDtypeStruct((16, LOCAL), f32),
            jax.ShapeDtypeStruct((16, ROT), f32),
        ),
        in_specs=[hbm] * 9,
        out_specs=(vmem, vmem),
        scratch_shapes=[
            pltpu.VMEM(cos.shape, bf16),
            pltpu.VMEM(sin.shape, bf16),
            pltpu.VMEM(images.shape, f32),
            pltpu.VMEM(references.shape, bf16),
            pltpu.VMEM(ctf_table.shape, f32),
            pltpu.VMEM(noise_inv.shape, f32),
            pltpu.SMEM((16,), i32),
            pltpu.SMEM((16,), i32),
            pltpu.SMEM((16,), i32),
            pltpu.VMEM((16, CYCLES), f32),
            pltpu.VMEM((16, CYCLES), f32),
            pltpu.VMEM((16, CYCLES), f32),
            pltpu.VMEM((16, 256), f32),
            pltpu.VMEM((2 * CYCLES * LOCAL, 128), f32),
            pltpu.VMEM((2 * CYCLES * LOCAL, 128), f32),
            pltpu.VMEM((NX, 8, 128), f32),
            pltpu.VMEM((NX, 8, 128), f32),
            pltpu.VMEM((128, 128), f32),
            pltpu.VMEM((128, 128), f32),
            pltpu.VMEM((16, 128), f32),
            pltpu.VMEM((NX, 2, HREF, KT), f32),
            pltpu.VMEM((NZ, 9, 2, 128), f32),
            pltpu.VMEM((16, CYCLES), f32),
            pltpu.VMEM((2, 2, 2 * HREF + 8, 128), f32),
            pltpu.VMEM((2, 2, NX * BLOCK, HALF * 128), bf16),
            pltpu.VMEM((NX * 8, KT), f32),
            pltpu.VMEM((ANG, 128), f32),
            pltpu.VMEM((4, ANG // 2, 128), f32),
            pltpu.VMEM((2, 2 * SHIFTS, HALF * 128), bf16),
            pltpu.VMEM((2, 2 * SHIFTS, HALF * 128), bf16),
            pltpu.VMEM((2, NX * BLOCK, 2 * SHIFTS), f32),
            pltpu.VMEM((2, NX * BLOCK, 2 * SHIFTS), f32),
            pltpu.VMEM((2, HALF, SHIFTS, 128), f32),
            pltpu.VMEM((2, HALF, SHIFTS, 128), f32),
            pltpu.VMEM((2, NX * BLOCK, 128), f32),
            pltpu.VMEM((2 * HREF, 128), f32),
            pltpu.VMEM((128, CYCLES), f32),
            pltpu.VMEM((128, 128), f32),
            pltpu.VMEM((NZ, MINE, 128), f32),
            pltpu.VMEM((MINE, 128), f32),
            pltpu.VMEM((NX, MINE, 128), f32),
            dma((9,)),
            dma((NX - 1,)),
            dma((NX - 1,)),
            dma((7,)),
            dma((7,)),
            dma((NZ,)),
            dma((NZ,)),
            dma((NZ,)),
            dma((NZ,)),
            dma((NX - 1,)),
            dma((NX - 1,)),
        ],
        compiler_params=pltpu.CompilerParams(collective_id=0, has_side_effects=True, vmem_limit_bytes=40 << 20),
        name="expectation",
    )(*operands)
    return class_post, rot_post


def solution(mesh):
    cos, sin = phase_tables()
    in_specs = (P("ptl", "cls"), P("cls", None), P(), P(), P("ptl"), P("ptl"), P("ptl"))
    out_specs = (P("ptl", "cls"), P("ptl", None))
    mapped = jax.shard_map(
        body, mesh=mesh, in_specs=(P(), P()) + in_specs, out_specs=out_specs, check_vma=False
    )

    def run(*args):
        return mapped(jnp.asarray(cos), jnp.asarray(sin), *args)

    return run
```
